32 devices in a mesh: dp: 8 (over z, core), tensor: 4 (over y, x).
Axes of the slice: x: 2, y: 2, z: 4, core: 2. Of those that a mesh axis runs over, the one named last changes fastest.
Arguments:
- tokens: bfloat16 [1024, 16, 2048], P('tensor', 'dp'), may hold values from -6 to 6
- cotangent: bfloat16 [1024, 16, 2048], P('tensor', 'dp'), may hold values from -8 to 8
- doc_lengths: int32 [16, 8], P('dp'), may hold values from 1 to 1017, as said below
- rel_bucket: int32 [2047], replicated, may hold values from 0 to 31
- gain_attn: bfloat16 [2048], P('dp'), may hold values from 0.5 to 1.5
- w_query: bfloat16 [2048, 2048], P('dp', 'tensor'), may hold values from -0.03125 to 0.03125
- w_key: bfloat16 [2048, 2048], P('dp', 'tensor'), may hold values from -0.125 to 0.125
- w_value: bfloat16 [2048, 2048], P('dp', 'tensor'), may hold values from -0.125 to 0.125
- w_out: bfloat16 [2048, 2048], P('tensor', 'dp'), may hold values from -0.5 to 0.5
- rel_table: bfloat16 [32, 32], P('dp', 'tensor'), may hold values from -4 to 4
- gain_ff: bfloat16 [2048], P('dp'), may hold values from 0.5 to 1.5
- w_gate: bfloat16 [2048, 5120], P('dp', 'tensor'), may hold values from -0.125 to 0.125
- w_up: bfloat16 [2048, 5120], P('dp', 'tensor'), may hold values from -0.125 to 0.125
- w_down: bfloat16 [5120, 2048], P('tensor', 'dp'), may hold values from -0.078125 to 0.078125
Outputs:
- output: bfloat16 [1024, 16, 2048], P('tensor', 'dp')
- grad_tokens: bfloat16 [1024, 16, 2048], P('tensor', 'dp')
- grad_gain_attn: float32 [2048], P('dp')
- grad_w_query: float32 [2048, 2048], P('dp', 'tensor')
- grad_w_key: float32 [2048, 2048], P('dp', 'tensor')
- grad_w_value: float32 [2048, 2048], P('dp', 'tensor')
- grad_w_out: float32 [2048, 2048], P('tensor', 'dp')
- grad_rel_table: float32 [32, 32], P('dp', 'tensor')
- grad_gain_ff: float32 [2048], P('dp')
- grad_w_gate: float32 [2048, 5120], P('dp', 'tensor')
- grad_w_up: float32 [2048, 5120], P('dp', 'tensor')
- grad_w_down: float32 [5120, 2048], P('tensor', 'dp')
The draws below stay inside these ranges and needn't reach their ends.
Inputs may be any that keep to these rules, and one draw needn't show every extreme that they name: `doc_lengths`: each row gives 7 document lengths, each 1 or more, then a tail padding length of 1 to 128; each row sums to 1024. In one sequence of every 2 consecutive ones the first document holds 1017 slots.
All inputs are finite; a program needn't handle non-finite values.
Results may differ from the reference program's by a relative error of at most 0.024.
Values may be sent and summed in bfloat16 or wider, within the bound.
No kernel may reach another device: no remote copies, remote signals or barrier semaphores. Data moves between devices by JAX's collectives and lax.ppermute only.
A program may use at most 448 MiB of HBM per device.

```python
import jax
import jax.numpy as jnp
from jax import lax

D = 2048
HEADS = 32
HEAD_DIM = 64
FF = 5120
BUCKETS = 32
L = 1024
NDOC = 8
GSEQ = 2
SEQS = 16


def draw_doc_lengths(key, part):
    key_pad, key_root, key_pick = jax.random.split(key, 3)
    padding = jax.random.randint(key_pad, (SEQS,), 1, L // 8 + 1)
    roots = jax.random.randint(key_root, (SEQS, NDOC - 1), 1, 9)
    weights = roots * roots * roots
    chosen = jax.random.randint(key_pick, (SEQS // GSEQ,), 0, GSEQ)
    sequence = jnp.arange(SEQS, dtype=jnp.int32)
    is_long = sequence % GSEQ == jnp.repeat(chosen, GSEQ)
    leading = jnp.arange(NDOC - 1, dtype=jnp.int32) == 0
    padding = jnp.where(is_long, 1, padding)
    weights = jnp.where(is_long[:, None], jnp.where(leading[None, :], 1, 0), weights)
    usable = L - padding
    spare = usable - (NDOC - 1)
    weight_total = jnp.sum(weights, axis=1)
    shares = weights * spare[:, None] // weight_total[:, None]
    remain = spare - jnp.sum(shares, axis=1)
    documents = 1 + shares + jnp.where(leading[None, :], remain[:, None], 0)
    return jnp.concatenate([documents, padding[:, None]], axis=1).astype(jnp.int32)


def plant(array, rng, low, top_value):
    dims = array.shape
    index_at = [jax.random.randint(jax.random.fold_in(rng, axis), (), 0, dims[axis]) for axis in range(len(dims))]
    array = array.at[tuple(index_at)].set(low)
    longest = dims.index(max(dims))
    index_at[longest] = (index_at[longest] + 1) % dims[longest]
    return array.at[tuple(index_at)].set(top_value)


def spiked(array, own_key, source, target, shards_of, factor):
    def block_of(position):
        return (jnp.arange(array.shape[position]) // (array.shape[position] // shards_of)).reshape((-1,) + (1,) * (array.ndim - 1 - position))

    first = jax.random.permutation(own_key, shards_of)[block_of(target)]
    far = (block_of(target) + shards_of // 2) % shards_of
    return jnp.where((block_of(source) == first) | (block_of(source) == far), factor * array, array)


def block_levels(key, shape, shards, least, largest):
    def one(position, shards_of):
        draws = jax.random.uniform(jax.random.fold_in(jax.random.fold_in(key, 6), position), (shards_of,), jnp.float32, least / len(shards), largest / len(shards))
        return jnp.repeat(jnp.exp(draws), shape[position] // shards_of).reshape((-1,) + (1,) * (len(shape) - position - 1))

    level = one(*shards[0])
    for cut in shards[1:]:
        level = level * one(*cut)
    return level


def bell_draw(rng, shape, spread, most, pieces=(), kind=jnp.bfloat16):
    values = spread * jax.random.normal(rng, shape, jnp.float32)
    if pieces:
        values = values * block_levels(rng, shape, pieces, -0.22, 0.18)
    return jnp.clip(values, -most, most).astype(kind)


def heavy_noise(own_key, shape, deviation, most, cuts, heavy, held_as=jnp.bfloat16):
    drawn = deviation * jax.random.normal(own_key, shape, jnp.float32)
    if cuts:
        drawn = drawn * block_levels(own_key, shape, cuts, -0.22, 0.18)
    return jnp.clip(spiked(drawn, jax.random.fold_in(own_key, 3), *heavy), -most, most).astype(held_as)


def setup_inputs(seed: int = 0) -> dict:
    key_list = jax.random.split(jax.random.key(seed), 15)
    tokens = bell_draw(key_list[0], (L, SEQS, D), 1.0, 6.0, ((0, 4), (1, 8)))
    cotangent = heavy_noise(key_list[1], (L, SEQS, D), 1.0, 8.0, ((0, 4), (1, 8)), (1, 2, 8, 2.0))
    doc_lengths = draw_doc_lengths(jax.random.fold_in(key_list[14], 71), 0)
    rel_bucket = plant(jax.random.randint(key_list[3], (2 * L - 1,), 0, BUCKETS), jax.random.fold_in(key_list[3], 1), 0, BUCKETS - 1).astype(jnp.int32)
    gain_attn = jnp.clip(1.0 + 0.1 * jax.random.normal(key_list[4], (D,), jnp.float32), 0.5, 1.5).astype(jnp.bfloat16)
    w_query = bell_draw(key_list[5], (D, HEADS * HEAD_DIM), (16 * D) ** -0.5, 0.03125, ((0, 8), (1, 4)))
    w_key = bell_draw(key_list[6], (D, HEADS * HEAD_DIM), D ** -0.5, 0.125, ((0, 8), (1, 4)))
    w_value = bell_draw(key_list[7], (D, HEADS * HEAD_DIM), D ** -0.5, 0.125, ((0, 8), (1, 4)))
    w_out = bell_draw(key_list[8], (HEADS * HEAD_DIM, D), (HEADS * HEAD_DIM // 16) ** -0.5, 0.5, ((0, 4), (1, 8)))
    rel_table = bell_draw(key_list[9], (BUCKETS, HEADS), 1.0, 4.0, ((0, 8), (1, 4)))
    gain_ff = jnp.clip(1.0 + 0.1 * jax.random.normal(key_list[10], (D,), jnp.float32), 0.5, 1.5).astype(jnp.bfloat16)
    w_gate = bell_draw(key_list[11], (D, FF), D ** -0.5, 0.125, ((0, 8), (1, 4)))
    w_up = bell_draw(key_list[12], (D, FF), D ** -0.5, 0.125, ((0, 8), (1, 4)))
    w_down = bell_draw(key_list[13], (FF, D), FF ** -0.5, 0.078125, ((0, 4), (1, 8)))
    return {"tokens": tokens, "cotangent": cotangent, "doc_lengths": doc_lengths, "rel_bucket": rel_bucket, "gain_attn": gain_attn, "w_query": w_query, "w_key": w_key, "w_value": w_value, "w_out": w_out, "rel_table": rel_table, "gain_ff": gain_ff, "w_gate": w_gate, "w_up": w_up, "w_down": w_down}


EPSILON = 1e-06
NEGATIVE = -1e+30
HIGH = lax.Precision.HIGHEST

@jax.custom_vjp
def low(v):
    return lax.optimization_barrier(v.astype(jnp.bfloat16)).astype(jnp.float32)

@jax.custom_vjp
def low_back(v):
    return v

def low_keep(v):
    return (low(v), None)

def low_pass(kept, grad):
    return (grad,)

def back_keep(v):
    return (v, None)

def back_low(kept, grad):
    return (low(grad),)
low.defvjp(low_keep, low_pass)
low_back.defvjp(back_keep, back_low)

def segment_ids(lengths, length):
    ends = jnp.cumsum(lengths, axis=1)
    slots = jnp.arange(length, dtype=jnp.int32)
    passed = lax.optimization_barrier(jnp.sum((slots[None, :, None] >= ends[:, None, :]).astype(jnp.int32), axis=2))
    number = lengths.shape[1]
    return jnp.where(passed == number - 1, 0, passed + 1).astype(jnp.int32)

def norm_rows(rows, gain):
    return rows * lax.rsqrt(lax.optimization_barrier(jnp.mean(rows * rows, axis=-1, keepdims=True)) + EPSILON) * gain

def product(left, right):
    return jnp.dot(left, right, precision=HIGH)

def layer(params, rows, segments, bucket_onehot):
    w_query, w_key, w_value, w_out, w_gate, w_up, w_down, gain_attn, gain_ff, rel_table = params
    length = rows.shape[0]
    normed = low(norm_rows(rows, gain_attn))
    queries = low(low_back(product(normed, w_query))).reshape(length, HEADS, HEAD_DIM)
    keys = low(low_back(product(normed, w_key))).reshape(length, HEADS, HEAD_DIM)
    values = low(low_back(product(normed, w_value))).reshape(length, HEADS, HEAD_DIM)
    bias_offset = product(bucket_onehot, rel_table)
    positions = jnp.arange(length, dtype=jnp.int32)
    offsets = positions[None, :] - positions[:, None] + length - 1
    bias = jnp.transpose(bias_offset[offsets], (2, 0, 1))
    scores = jnp.einsum('qhd,khd->hqk', queries, keys, precision=HIGH) + bias
    scores = low_back(scores)
    same = segments[:, None] == segments[None, :]
    scores = jnp.where(same[None], scores, NEGATIVE)
    peak = lax.optimization_barrier(jnp.max(scores, axis=2, keepdims=True))
    weights = jnp.exp(scores - peak)
    shares = low(weights / lax.optimization_barrier(jnp.sum(weights, axis=2, keepdims=True)))
    mixed = jnp.einsum('hqk,khd->qhd', shares, values, precision=HIGH).reshape(length, HEADS * HEAD_DIM)
    mixed = low(low_back(mixed))
    middle = rows + low_back(product(mixed, w_out))
    normed_ff = low(norm_rows(middle, gain_ff))
    gate = low_back(product(normed_ff, w_gate))
    upward = low_back(product(normed_ff, w_up))
    hidden = low(jax.nn.gelu(gate, approximate=True) * upward)
    return middle + low_back(product(hidden, w_down))

def reference(tokens, cotangent, doc_lengths, rel_bucket, gain_attn, w_query, w_key, w_value, w_out, rel_table, gain_ff, w_gate, w_up, w_down):
    length = tokens.shape[0]
    segments = segment_ids(doc_lengths, length)
    bucket_onehot = (rel_bucket[:, None] == jnp.arange(BUCKETS, dtype=jnp.int32)[None, :]).astype(jnp.float32)
    params = tuple((weight.astype(jnp.float32) for weight in (w_query, w_key, w_value, w_out, w_gate, w_up, w_down, gain_attn, gain_ff, rel_table)))
    rows = jnp.moveaxis(tokens.astype(jnp.float32), 1, 0)
    layer_saved = jax.checkpoint(layer)

    def forward(params, rows):

        def advance(carry, item):
            return (carry, layer_saved(params, item[0], item[1], bucket_onehot))
        return lax.scan(advance, jnp.zeros((), jnp.float32), (rows, segments))[1]
    outputs, pullback = jax.vjp(forward, params, rows)
    grads, grad_rows = pullback(jnp.moveaxis(cotangent.astype(jnp.float32), 1, 0))
    output = jnp.moveaxis(outputs, 0, 1).astype(jnp.bfloat16)
    grad_tokens = jnp.moveaxis(grad_rows, 0, 1).astype(jnp.bfloat16)
    return (output, grad_tokens, grads[7], grads[0], grads[1], grads[2], grads[3], grads[9], grads[8], grads[4], grads[5], grads[6])
```

```python
import functools
import jax
import jax.numpy as jnp
from jax import lax
from jax.experimental import pallas as pl
from jax.experimental.pallas import tpu as pltpu
from jax.sharding import PartitionSpec as P

HD=64
B=256
BIG=1e30
F32=jnp.float32; BF=jnp.bfloat16

def nt(a,b): return lax.dot_general(a,b,(((1,),(1,)),((),())),preferred_element_type=F32)
def nn(a,b): return lax.dot_general(a,b,(((1,),(0,)),((),())),preferred_element_type=F32)

def strips_kernel(w_ref, out_ref):
    nrb=w_ref.shape[1]
    def body(i,_):
        w=w_ref[0,pl.ds(i,1),:]
        t=pltpu.roll(jnp.broadcast_to(w,(B,2*B)),0,1,stride=1,stride_axis=0)
        out_ref[0,pl.ds(pl.multiple_of(i*B,B),B),:]=t[:,:B]
        return 0
    lax.fori_loop(0,nrb,body,0)

def strips_call(w,n):
    heads=w.shape[0]
    return pl.pallas_call(strips_kernel,grid=(heads,),
        in_specs=[pl.BlockSpec((1,2*n-1,2*B),lambda h:(h,0,0))],
        out_specs=pl.BlockSpec((1,(2*n-1)*B,B),lambda h:(h,0,0)),
        out_shape=jax.ShapeDtypeStruct((heads,(2*n-1)*B,B),F32),
        compiler_params=pltpu.CompilerParams(vmem_limit_bytes=32<<20),name="bias_strips")(w)

def fwd_kernel(n,act_ref,blk_ref,qkv_ref,fq_ref,fk_ref,bias_ref,o_ref,lse_ref,qx,kx,vx,s_scr,m_scr,o_scr):
    lane=lax.broadcasted_iota(jnp.int32,(1,128),1)
    q=qkv_ref[:,0:128]; k=qkv_ref[:,128:256]; v=qkv_ref[:,256:384]
    vt=v.T
    for h in range(2):
        own=(lane<HD) if h==0 else (lane>=HD)
        qx[h]=jnp.where(own,q,fq_ref[...])
        kx[h]=jnp.where(own,k,fk_ref[...])
        vx[h]=jnp.concatenate([vt[h*HD:(h+1)*HD],jnp.ones((16,vt.shape[1]),BF)],axis=0)
    def row(qi,_):
        qs=pl.ds(pl.multiple_of(qi*B,B),B)
        m_scr[...]=jnp.full_like(m_scr,-3e38)
        o_scr[...]=jnp.zeros_like(o_scr)
        def p1(kb,_):
            @pl.when(act_ref[qi*n+kb]!=0)
            def _():
                ks=pl.ds(pl.multiple_of(kb*B,B),B)
                bs=pl.ds(pl.multiple_of((blk_ref[kb]-blk_ref[qi]+n-1)*B,B),B)
                for h in range(2):
                    s=nt(kx[h,ks,:],qx[h,qs,:])+bias_ref[h,bs,:]
                    s_scr[h,ks,:]=s
                    m_scr[h]=jnp.maximum(m_scr[h],jnp.max(s.reshape(B//8,8,B),axis=0))
            return 0
        lax.fori_loop(0,n,p1,0)
        ms=[jnp.max(m_scr[h],axis=0,keepdims=True) for h in range(2)]
        def p2(kb,_):
            @pl.when(act_ref[qi*n+kb]!=0)
            def _():
                ks=pl.ds(pl.multiple_of(kb*B,B),B)
                for h in range(2):
                    p=jnp.exp(s_scr[h,ks,:]-ms[h]).astype(BF)
                    o_scr[h]+=nn(vx[h,:,ks],p)
            return 0
        lax.fori_loop(0,n,p2,0)
        outs=[]
        for h in range(2):
            tot=o_scr[h,HD:HD+1,:]
            outs.append(o_scr[h,0:HD,:]/tot)
            lse_ref[0,pl.ds(h,1),qs]=ms[h]+jnp.log(tot)
        o_ref[qs,:]=jnp.concatenate(outs,axis=0).T.astype(BF)
        return 0
    lax.fori_loop(0,n,row,0)

def attend_fwd(qkv,fq,fk,bias,act,blk):
    L,w3=qkv.shape; n=L//B; np_=w3//384
    H2=2
    return pl.pallas_call(functools.partial(fwd_kernel,n),
        grid_spec=pltpu.PrefetchScalarGridSpec(num_scalar_prefetch=2,grid=(np_,),
          in_specs=[pl.BlockSpec((L,384),lambda p,*_:(0,p)),
                    pl.BlockSpec((L,128),lambda p,*_:(0,0)),
                    pl.BlockSpec((L,128),lambda p,*_:(0,0)),
                    pl.BlockSpec((2,(2*n-1)*B,B),lambda p,*_:(p,0,0))],
          out_specs=[pl.BlockSpec((L,128),lambda p,*_:(0,p)),
                     pl.BlockSpec((1,2,L),lambda p,*_:(p,0,0))],
          scratch_shapes=[pltpu.VMEM((2,L,128),BF),pltpu.VMEM((2,L,128),BF),pltpu.VMEM((2,HD+16,L),BF),
                          pltpu.VMEM((2,L,B),F32),pltpu.VMEM((2,8,B),F32),pltpu.VMEM((2,HD+16,B),F32)]),
        out_shape=[jax.ShapeDtypeStruct((L,np_*128),BF),jax.ShapeDtypeStruct((np_,2,L),F32)],
        compiler_params=pltpu.CompilerParams(vmem_limit_bytes=40<<20),
        cost_estimate=pl.CostEstimate(flops=int(np_*2*L*L*128*2*2),bytes_accessed=int(L*w3*2+np_*2*(2*n-1)*B*B*4),transcendentals=np_*2*L*L),
        name="attend_forward")(act,blk,qkv,fq,fk,bias)

def bwd_kernel(n,act_ref,blk_ref,qkv_ref,fq_ref,fk_ref,bias_ref,lse_ref,o_ref,do_ref,g_ref,fold_ref,qx,kx,v0,kt,delta,dk,dv,dqt,diag):
    lane=lax.broadcasted_iota(jnp.int32,(1,128),1)
    q=qkv_ref[:,0:128]; k=qkv_ref[:,128:256]; v=qkv_ref[:,256:384]
    for h in range(2):
        own=(lane<HD) if h==0 else (lane>=HD)
        qx[h]=jnp.where(own,q,fq_ref[...])
        kx[h]=jnp.where(own,k,fk_ref[...])
        v0[h]=jnp.where(own,v,jnp.zeros_like(v))
    kt[...]=k.T
    prod=(o_ref[...].astype(F32)*do_ref[...].astype(F32)).T
    for h in range(2):
        delta[h:h+1,:]=jnp.sum(prod[h*HD:(h+1)*HD],axis=0,keepdims=True)
    dk[...]=jnp.zeros_like(dk); dv[...]=jnp.zeros_like(dv); diag[...]=jnp.zeros_like(diag)
    def row(qi,_):
        qs=pl.ds(pl.multiple_of(qi*B,B),B)
        dqt[...]=jnp.zeros_like(dqt)
        lses=[lse_ref[0,pl.ds(h,1),qs] for h in range(2)]
        dels=[delta[pl.ds(h,1),qs] for h in range(2)]
        def inner(kb,_):
            @pl.when(act_ref[qi*n+kb]!=0)
            def _():
                ks=pl.ds(pl.multiple_of(kb*B,B),B)
                bs=pl.ds(pl.multiple_of((blk_ref[kb]-blk_ref[qi]+n-1)*B,B),B)
                dob=do_ref[qs,:]; qb=qkv_ref[qs,0:128]
                for h in range(2):
                    s=nt(kx[h,ks,:],qx[h,qs,:])+bias_ref[h,bs,:]
                    dp=nt(v0[h,ks,:],dob)
                    p=jnp.exp(s-lses[h])
                    ds=p*(dp-dels[h])
                    pb=p.astype(BF); dsb=ds.astype(BF)
                    diag[h,bs,:]+=ds
                    dv[h,ks,:]+=nn(pb,dob)
                    dk[h,ks,:]+=nn(dsb,qb)
                    dqt[h]+=nn(kt[h*HD:(h+1)*HD,ks],dsb)
            return 0
        lax.fori_loop(0,n,inner,0)
        g_ref[qs,0:128]=jnp.concatenate([dqt[0],dqt[1]],axis=0).T.astype(BF)
        return 0
    lax.fori_loop(0,n,row,0)
    first=lane<HD
    g_ref[:,128:256]=jnp.where(first,dk[0],dk[1]).astype(BF)
    g_ref[:,256:384]=jnp.where(first,dv[0],dv[1]).astype(BF)
    for h in range(2):
        def fold(i,_):
            a=diag[h,pl.ds(pl.multiple_of(i*B,B),B),:]
            zero=jnp.zeros((8,B),F32)
            acc=jnp.zeros((8,2*B),F32)
            for g in range(B//8):
                part=jnp.concatenate([a[8*g:8*g+8],zero],axis=1)
                acc=acc+(pltpu.roll(part,2*B-8*g,1) if g else part)
            tot=acc[0:1]
            for r in range(1,8):
                tot=tot+pltpu.roll(acc[r:r+1],2*B-r,1)
            fold_ref[0,h,pl.ds(i,1),:]=tot
            return 0
        lax.fori_loop(0,2*n-1,fold,0)

def attend_bwd(qkv,fq,fk,bias,lse,o,do,act,blk):
    L,w3=qkv.shape; n=L//B; np_=w3//384
    return pl.pallas_call(functools.partial(bwd_kernel,n),
        grid_spec=pltpu.PrefetchScalarGridSpec(num_scalar_prefetch=2,grid=(np_,),
          in_specs=[pl.BlockSpec((L,384),lambda p,*_:(0,p)),
                    pl.BlockSpec((L,128),lambda p,*_:(0,0)),
                    pl.BlockSpec((L,128),lambda p,*_:(0,0)),
                    pl.BlockSpec((2,(2*n-1)*B,B),lambda p,*_:(p,0,0)),
                    pl.BlockSpec((1,2,L),lambda p,*_:(p,0,0)),
                    pl.BlockSpec((L,128),lambda p,*_:(0,p)),
                    pl.BlockSpec((L,128),lambda p,*_:(0,p))],
          out_specs=[pl.BlockSpec((L,384),lambda p,*_:(0,p)),
                     pl.BlockSpec((1,2,2*n-1,2*B),lambda p,*_:(p,0,0,0))],
          scratch_shapes=[pltpu.VMEM((2,L,128),BF),pltpu.VMEM((2,L,128),BF),pltpu.VMEM((2,L,128),BF),
                          pltpu.VMEM((128,L),BF),pltpu.VMEM((2,L),F32),
                          pltpu.VMEM((2,L,128),F32),pltpu.VMEM((2,L,128),F32),pltpu.VMEM((2,HD,B),F32),
                          pltpu.VMEM((2,(2*n-1)*B,B),F32)]),
        out_shape=[jax.ShapeDtypeStruct((L,w3),BF),jax.ShapeDtypeStruct((np_,2,2*n-1,2*B),F32)],
        compiler_params=pltpu.CompilerParams(vmem_limit_bytes=48<<20),
        cost_estimate=pl.CostEstimate(flops=int(np_*2*L*L*128*2*5),bytes_accessed=int(L*w3*4+np_*2*(2*n-1)*B*B*4),transcendentals=np_*2*L*L),
        name="attend_backward")(act,blk,qkv,fq,fk,bias,lse,o,do)

EPSILON = 1e-06
MICRO = 2


def norm_scale(rows):
    return lax.rsqrt(jnp.mean(rows * rows, axis=-1, keepdims=True) + EPSILON)


def norm_back(rows, scale, gain, grad_normed):
    scaled = gain * grad_normed
    inner = jnp.mean(scaled * rows, axis=-1, keepdims=True)
    grad_rows = scale * scaled - rows * scale * scale * scale * inner
    return grad_rows, jnp.sum(grad_normed * rows * scale, axis=0)


def tn(left, right):
    return lax.dot_general(left, right, (((0,), (0,)), ((), ())), preferred_element_type=F32)


def hop(part, bit, count):
    return lax.ppermute(part, "tensor", [(i, i ^ bit) for i in range(count)])


def gather_rows(part, count):
    if count != 4:
        return lax.all_gather(part, "tensor", axis=0, tiled=True)
    half = part.shape[0] // 2
    from_x = hop(part, 1, count)
    from_y = hop(part, 2, count)
    diag_low = hop(from_y[:half], 1, count)
    diag_high = hop(from_x[half:], 2, count)
    return jnp.concatenate([part, from_x, from_y, diag_low, diag_high], axis=0)


def reduce_rows(partial, count):
    if count != 4:
        return lax.psum_scatter(partial, "tensor", scatter_dimension=0, tiled=True).astype(F32)
    size = partial.shape[0] // 4
    half = size // 2
    own, to_x, to_y, to_d = (partial[i * size : (i + 1) * size] for i in range(4))
    x_first = hop(jnp.concatenate([to_x[:half], to_d[:half]], axis=0), 1, count)
    y_first = hop(jnp.concatenate([to_y[half:], to_d[half:]], axis=0), 2, count)
    x_second = hop((to_x[half:].astype(F32) + y_first[half:].astype(F32)).astype(BF), 1, count)
    y_second = hop((to_y[:half].astype(F32) + x_first[half:].astype(F32)).astype(BF), 2, count)
    low = own[:half].astype(F32) + x_first[:half].astype(F32) + y_second.astype(F32)
    high = own[half:].astype(F32) + y_first[:half].astype(F32) + x_second.astype(F32)
    return jnp.concatenate([low, high], axis=0)


def gelu_parts(gate):
    c = 0.7978845608028654
    square = gate * gate
    th = jnp.tanh(c * gate * (1.0 + 0.044715 * square))
    value = 0.5 * gate * (1.0 + th)
    slope = 0.5 * (1.0 + th) + 0.5 * gate * (1.0 - th * th) * c * (1.0 + 3 * 0.044715 * square)
    return value, slope


def local(
    count_dp,
    count,
    tokens,
    cotangent,
    doc_lengths,
    rel_bucket,
    gain_attn,
    w_query,
    w_key,
    w_value,
    w_out,
    rel_table,
    gain_ff,
    w_gate,
    w_up,
    w_down,
):
    slots = tokens.shape[0]
    length = slots * count
    blocks = length // B
    rows_w, width = w_query.shape
    width_ff = w_gate.shape[1]
    pairs = width // 128
    heads = width // HD
    buckets_local = rel_table.shape[0]
    buckets = buckets_local * count_dp
    docs = doc_lengths.shape[1]

    def spread(part):
        return lax.all_gather(part, "dp", axis=0, tiled=True)

    local_qkv = jnp.stack(
        [w.reshape(rows_w, pairs, 128) for w in (w_query, w_key, w_value)], axis=2
    ).reshape(rows_w, 3 * width)
    small = spread(jnp.concatenate([gain_attn, gain_ff, rel_table.reshape(-1)])[None])
    full_qkv = spread(local_qkv)
    full_out = spread(w_out.T)
    full_ff = spread(jnp.concatenate([w_gate, w_up], axis=1))
    full_down = spread(w_down.T)
    gain_one = small[:, :rows_w].reshape(1, -1).astype(F32)
    gain_two = small[:, rows_w : 2 * rows_w].reshape(1, -1).astype(F32)
    table = small[:, 2 * rows_w :].reshape(buckets, heads)

    reverse = jnp.concatenate([jnp.full((1,), -1, jnp.int32), rel_bucket[::-1]])
    onehot = reverse[None, :] == jnp.arange(buckets, dtype=jnp.int32)[:, None]
    offsets = lax.dot_general(
        table, onehot.astype(BF), (((0,), (0,)), ((), ())), preferred_element_type=F32
    ).reshape(heads, 2 * blocks, B)
    tiles = 2 * blocks - 1
    ahead = offsets[:, ::-1]
    bias = strips_call(jnp.concatenate([ahead[:, :tiles], ahead[:, 1:]], axis=2), blocks)

    order = jnp.arange(blocks, dtype=jnp.int32)
    if count == 4:
        order = order ^ lax.axis_index("tensor").astype(jnp.int32)
    positions = (order[:, None] * B + jnp.arange(B, dtype=jnp.int32)[None]).reshape(-1)
    ends = jnp.cumsum(doc_lengths, axis=1)
    lane = jnp.arange(128, dtype=jnp.int32) % HD

    xs, scales, wholes, cots, attends = [], [], [], [], []
    for m in range(MICRO):
        rows = tokens[:, m].astype(F32)
        scale = norm_scale(rows)
        xs.append(rows)
        scales.append(scale)
        wholes.append(gather_rows((rows * scale * gain_one).astype(BF), count))
    for m in range(MICRO):
        cots.append(gather_rows(cotangent[:, m], count))

    saved = []
    for m in range(MICRO):
        number = jnp.sum((positions[:, None] >= ends[m][None, :]).astype(jnp.int32), axis=1)
        by_block = number.reshape(blocks, B)
        least, most = by_block.min(axis=1), by_block.max(axis=1)
        active = (least[:, None] <= most[None, :]) & (least[None, :] <= most[:, None])
        active = active.astype(jnp.int32).reshape(-1)
        same = number[:, None] == lane[None, :]
        feat_q = same.astype(BF)
        feat_k = jnp.where(same | (lane >= docs)[None, :], 0.0, -BIG).astype(BF)
        qkv = nn(wholes[m], full_qkv).astype(BF)
        mixed, logsum = attend_fwd(qkv, feat_q, feat_k, bias, active, order)
        middle = xs[m] + reduce_rows(nt(mixed, full_out).astype(BF), count)
        scale_two = norm_scale(middle)
        whole_two = gather_rows((middle * scale_two * gain_two).astype(BF), count)
        saved.append((qkv, feat_q, feat_k, active, mixed, logsum, middle, scale_two, whole_two))

    ff_saved, outputs, mid_saved = [], [], []
    for m in range(MICRO):
        middle, scale_two, whole_two = saved[m][6:]
        gate_up = nn(whole_two, full_ff).astype(BF)
        gate = gate_up[:, :width_ff].astype(F32)
        up = gate_up[:, width_ff:].astype(F32)
        value, slope = gelu_parts(gate)
        hidden = (value * up).astype(BF)
        grad_hidden = nn(cots[m], full_down)
        grad_ff = jnp.concatenate([grad_hidden * up * slope, grad_hidden * value], axis=1).astype(BF)
        grad_normed = reduce_rows(nt(grad_ff, full_ff).astype(BF), count)
        grad_norm, grad_gain_two = norm_back(middle, scale_two, gain_two, grad_normed)
        grad_middle = cotangent[:, m].astype(F32) + grad_norm
        whole_mid = gather_rows(grad_middle.astype(BF), count)
        mid_saved.append((grad_middle, whole_mid, grad_gain_two))
        ff_saved.append((hidden, grad_ff))
    for m in range(MICRO):
        ff_rows = reduce_rows(nt(ff_saved[m][0], full_down).astype(BF), count)
        outputs.append((saved[m][6] + ff_rows).astype(BF))

    def over_both(lefts, rights):
        total = tn(lefts[0], rights[0])
        for left, right in zip(lefts[1:], rights[1:]):
            total = total + tn(left, right)
        return lax.psum_scatter(total.astype(BF), "dp", scatter_dimension=0, tiled=True).astype(F32)

    grad_ff_weight = over_both([s[8] for s in saved], [f[1] for f in ff_saved])
    grad_down = over_both(cots, [f[0] for f in ff_saved])

    projects, folds, grad_inputs, gains_one = [], [], [], []
    for m in range(MICRO):
        qkv, feat_q, feat_k, active, mixed, logsum = saved[m][:6]
        grad_middle, whole_mid, _ = mid_saved[m]
        grad_mixed = nn(whole_mid, full_out).astype(BF)
        project, fold = attend_bwd(
            qkv, feat_q, feat_k, bias, logsum, mixed, grad_mixed, active, order
        )
        projects.append(project)
        folds.append(fold)
        grad_normed = reduce_rows(nt(project, full_qkv).astype(BF), count)
        grad_norm, grad_gain_one = norm_back(xs[m], scales[m], gain_one, grad_normed)
        grad_inputs.append((grad_middle + grad_norm).astype(BF))
        gains_one.append(grad_gain_one)
    grad_out = over_both([s[1] for s in mid_saved], [s[4] for s in saved])
    grad_qkv = over_both(wholes, projects)

    fold = sum(folds).reshape(heads, tiles, 2 * B)
    zero = jnp.zeros((heads, 1, B), F32)
    by_offset = (
        jnp.concatenate([fold[:, :, :B], zero], axis=1)
        + jnp.concatenate([zero, fold[:, :, B:]], axis=1)
    )[:, ::-1].reshape(heads, 2 * length)
    grad_table = lax.dot_general(
        onehot.astype(F32), by_offset, (((1,), (1,)), ((), ())), precision=lax.Precision.HIGHEST
    )
    gain_grads = jnp.concatenate(
        [
            sum(gains_one).reshape(count_dp, rows_w),
            sum(s[2] for s in mid_saved).reshape(count_dp, rows_w),
            grad_table.reshape(count_dp, buckets_local * heads),
        ],
        axis=1,
    )
    gain_grads = lax.psum_scatter(gain_grads, "dp", scatter_dimension=0, tiled=True)[0]
    both_gains = lax.psum(gain_grads[: 2 * rows_w], "tensor")
    grad_qkv = grad_qkv.reshape(rows_w, pairs, 3, 128)
    return (
        jnp.stack(outputs, axis=1),
        jnp.stack(grad_inputs, axis=1),
        both_gains[:rows_w],
        grad_qkv[:, :, 0].reshape(rows_w, width),
        grad_qkv[:, :, 1].reshape(rows_w, width),
        grad_qkv[:, :, 2].reshape(rows_w, width),
        grad_out.T,
        gain_grads[2 * rows_w :].reshape(buckets_local, heads),
        both_gains[rows_w:],
        grad_ff_weight[:, :width_ff],
        grad_ff_weight[:, width_ff:],
        grad_down.T,
    )


def solution(mesh):
    row, col = P("dp", "tensor"), P("tensor", "dp")
    acts = P("tensor", "dp", None)
    in_specs = (
        acts, acts, P("dp", None), P(), P("dp"), row, row, row, col, row, P("dp"), row, row, col
    )
    out_specs = (acts, acts, P("dp"), row, row, row, col, row, P("dp"), row, row, col)
    body = functools.partial(local, mesh.shape["dp"], mesh.shape["tensor"])
    return jax.shard_map(body, mesh=mesh, in_specs=in_specs, out_specs=out_specs, check_vma=False)
```

```python
import functools
import jax
import jax.numpy as jnp
from jax import lax
from jax.experimental import pallas as pl
from jax.experimental.pallas import tpu as pltpu
from jax.sharding import PartitionSpec as P

HD=64
B=256
BIG=1e30
F32=jnp.float32; BF=jnp.bfloat16

def nt(a,b): return lax.dot_general(a,b,(((1,),(1,)),((),())),preferred_element_type=F32)
def nn(a,b): return lax.dot_general(a,b,(((1,),(0,)),((),())),preferred_element_type=F32)


EPSILON = 1e-06
MICRO = 2
HBM = pl.BlockSpec(memory_space=pltpu.HBM)
MIB = 1 << 20
CHEAP = pl.CostEstimate(flops=1, bytes_accessed=1, transcendentals=0)


def tn(left, right):
    return lax.dot_general(left, right, (((0,), (0,)), ((), ())), preferred_element_type=F32)


def pick(size, *tiles, start=0):
    return next(tile for tile in (*tiles, 128, size) if size % tile == 0 and start % tile == 0)


def strips_kernel(w_ref, out_ref):
    def body(i, _):
        wide = jnp.broadcast_to(w_ref[0, pl.ds(i, 1), :], (B, 2 * B))
        rolled = pltpu.roll(wide, 0, 1, stride=1, stride_axis=0)
        out_ref[0, pl.ds(pl.multiple_of(i * B, B), B), :] = rolled[:, :B]
        return 0

    lax.fori_loop(0, w_ref.shape[1], body, 0)


def bias_strips(w):
    heads, tiles, _ = w.shape
    return pl.pallas_call(
        strips_kernel,
        grid=(heads,),
        in_specs=[pl.BlockSpec((1, tiles, 2 * B), lambda h: (h, 0, 0))],
        out_specs=pl.BlockSpec((1, tiles * B, B), lambda h: (h, 0, 0)),
        out_shape=jax.ShapeDtypeStruct((heads, tiles * B, B), F32),
        compiler_params=pltpu.CompilerParams(vmem_limit_bytes=60 * MIB),
        cost_estimate=CHEAP,
        name="bias_strips",
    )(w)


def attend_forward_kernel(n, extra, *refs):
    act_ref, blk_ref, qkv_ref, fq_ref, fk_ref, bias_ref = refs[:6]
    o_ref, lse_ref, qx, kx, vx, s_scr, m_scr, o_scr = refs[6 + extra :]
    lane = lax.broadcasted_iota(jnp.int32, (1, 128), 1)
    q, k, v = qkv_ref[:, 0:128], qkv_ref[:, 128:256], qkv_ref[:, 256:384]
    vt = v.T
    for h in range(2):
        own = (lane < HD) if h == 0 else (lane >= HD)
        qx[h] = jnp.where(own, q, fq_ref[...])
        kx[h] = jnp.where(own, k, fk_ref[...])
        vx[h] = jnp.concatenate([vt[h * HD : (h + 1) * HD], jnp.ones((16, vt.shape[1]), BF)], axis=0)

    def row(qi, _):
        qs = pl.ds(pl.multiple_of(qi * B, B), B)
        m_scr[...] = jnp.full_like(m_scr, -3e38)
        o_scr[...] = jnp.zeros_like(o_scr)

        def score(kb, _):
            @pl.when(act_ref[qi * n + kb] != 0)
            def _():
                ks = pl.ds(pl.multiple_of(kb * B, B), B)
                bs = pl.ds(pl.multiple_of((blk_ref[kb] - blk_ref[qi] + n - 1) * B, B), B)
                for h in range(2):
                    s = nt(kx[h, ks, :], qx[h, qs, :]) + bias_ref[h, bs, :]
                    s_scr[h, ks, :] = s
                    m_scr[h] = jnp.maximum(m_scr[h], jnp.max(s.reshape(B // 8, 8, B), axis=0))

            return 0

        lax.fori_loop(0, n, score, 0)
        peaks = [jnp.max(m_scr[h], axis=0, keepdims=True) for h in range(2)]

        def share(kb, _):
            @pl.when(act_ref[qi * n + kb] != 0)
            def _():
                ks = pl.ds(pl.multiple_of(kb * B, B), B)
                for h in range(2):
                    p = jnp.exp(s_scr[h, ks, :] - peaks[h]).astype(BF)
                    o_scr[h] += nn(vx[h, :, ks], p)

            return 0

        lax.fori_loop(0, n, share, 0)
        outs = []
        for h in range(2):
            total = o_scr[h, HD : HD + 1, :]
            outs.append(o_scr[h, 0:HD, :] / total)
            lse_ref[0, pl.ds(h, 1), qs] = peaks[h] + jnp.log(total)
        o_ref[qs, :] = jnp.concatenate(outs, axis=0).T.astype(BF)
        return 0

    lax.fori_loop(0, n, row, 0)


def attend_forward(qkv, feat_q, feat_k, bias, active, order, first, into=(), deps=()):
    length, width3 = qkv.shape
    n, number, pairs = length // B, width3 // 384, bias.shape[0] // 2
    rows = (2 * n - 1) * B
    extra = len(into) + len(deps)
    whole = pl.BlockSpec((length, 128), lambda p, *_: (0, 0))
    return pl.pallas_call(
        functools.partial(attend_forward_kernel, n, extra),
        grid_spec=pltpu.PrefetchScalarGridSpec(
            num_scalar_prefetch=2,
            grid=(number,),
            in_specs=[
                pl.BlockSpec((length, 384), lambda p, *_: (0, p)),
                whole,
                whole,
                pl.BlockSpec((2, rows, B), lambda p, *_: (p + first, 0, 0)),
            ]
            + [HBM] * extra,
            out_specs=[
                pl.BlockSpec((length, 128), lambda p, *_: (0, p + first)),
                pl.BlockSpec((1, 2, length), lambda p, *_: (p + first, 0, 0)),
            ],
            scratch_shapes=[
                pltpu.VMEM((2, length, 128), BF),
                pltpu.VMEM((2, length, 128), BF),
                pltpu.VMEM((2, HD + 16, length), BF),
                pltpu.VMEM((2, length, B), F32),
                pltpu.VMEM((2, 8, B), F32),
                pltpu.VMEM((2, HD + 16, B), F32),
            ],
        ),
        out_shape=[
            jax.ShapeDtypeStruct((length, pairs * 128), BF),
            jax.ShapeDtypeStruct((pairs, 2, length), F32),
        ],
        input_output_aliases={6 + i: i for i in range(len(into))},
        compiler_params=pltpu.CompilerParams(vmem_limit_bytes=60 * MIB),
        cost_estimate=CHEAP,
        name="attend_forward",
    )(active, order, qkv, feat_q, feat_k, bias, *into, *deps)


def attend_backward_kernel(n, extra, *refs):
    act_ref, blk_ref, qkv_ref, fq_ref, fk_ref, bias_ref, lse_ref, o_ref, do_ref, sc_ref = refs[:10]
    g_ref, fold_ref, qx, kx, v0, kt, delta, dk, dv, dqt, diag = refs[10 + extra :]
    lane = lax.broadcasted_iota(jnp.int32, (1, 128), 1)
    q, k, v = qkv_ref[:, 0:128], qkv_ref[:, 128:256], qkv_ref[:, 256:384]
    for h in range(2):
        own = (lane < HD) if h == 0 else (lane >= HD)
        qx[h] = jnp.where(own, q, fq_ref[...])
        kx[h] = jnp.where(own, k, fk_ref[...])
        v0[h] = jnp.where(own, v, jnp.zeros_like(v))
    kt[...] = k.T
    prod = (o_ref[...].astype(F32) * do_ref[...].astype(F32)).T
    for h in range(2):
        delta[h : h + 1, :] = jnp.sum(prod[h * HD : (h + 1) * HD], axis=0, keepdims=True)
    dk[...] = jnp.zeros_like(dk)
    dv[...] = jnp.zeros_like(dv)
    diag[...] = jnp.zeros_like(diag)

    def row(qi, _):
        qs = pl.ds(pl.multiple_of(qi * B, B), B)
        dqt[...] = jnp.zeros_like(dqt)
        lses = [lse_ref[0, pl.ds(h, 1), qs] for h in range(2)]
        dels = [delta[pl.ds(h, 1), qs] for h in range(2)]

        def inner(kb, _):
            @pl.when(act_ref[qi * n + kb] != 0)
            def _():
                ks = pl.ds(pl.multiple_of(kb * B, B), B)
                bs = pl.ds(pl.multiple_of((blk_ref[kb] - blk_ref[qi] + n - 1) * B, B), B)
                dob = do_ref[qs, :]
                qb = qkv_ref[qs, 0:128]
                for h in range(2):
                    s = nt(kx[h, ks, :], qx[h, qs, :]) + bias_ref[h, bs, :]
                    dp = nt(v0[h, ks, :], dob)
                    p = jnp.exp(s - lses[h])
                    ds = p * (dp - dels[h])
                    pb, dsb = p.astype(BF), ds.astype(BF)
                    diag[h, bs, :] += ds
                    dv[h, ks, :] += nn(pb, dob)
                    dk[h, ks, :] += nn(dsb, qb)
                    dqt[h] += nn(kt[h * HD : (h + 1) * HD, ks], dsb)

            return 0

        lax.fori_loop(0, n, inner, 0)
        g_ref[qs, 0:128] = (jnp.concatenate([dqt[0], dqt[1]], axis=0).T * sc_ref[qs, :]).astype(BF)
        return 0

    lax.fori_loop(0, n, row, 0)
    left = lane < HD
    g_ref[:, 128:256] = (jnp.where(left, dk[0], dk[1]) * sc_ref[...]).astype(BF)
    g_ref[:, 256:384] = (jnp.where(left, dv[0], dv[1]) * sc_ref[...]).astype(BF)
    for h in range(2):

        def fold(i, _):
            a = diag[h, pl.ds(pl.multiple_of(i * B, B), B), :]
            zero = jnp.zeros((8, B), F32)
            acc = jnp.zeros((8, 2 * B), F32)
            for g in range(B // 8):
                part = jnp.concatenate([a[8 * g : 8 * g + 8], zero], axis=1)
                acc = acc + (pltpu.roll(part, 2 * B - 8 * g, 1) if g else part)
            total = acc[0:1]
            for r in range(1, 8):
                total = total + pltpu.roll(acc[r : r + 1], 2 * B - r, 1)
            fold_ref[0, h, pl.ds(i, 1), :] = total
            return 0

        lax.fori_loop(0, 2 * n - 1, fold, 0)


def attend_backward(
    qkv, feat_q, feat_k, bias, lse, mixed, grad, scale, active, order, first, into=(), deps=()
):
    length, width3 = qkv.shape
    n, number, pairs = length // B, width3 // 384, bias.shape[0] // 2
    tiles = 2 * n - 1
    rows = tiles * B
    extra = len(into) + len(deps)
    whole = pl.BlockSpec((length, 128), lambda p, *_: (0, 0))
    one = pl.BlockSpec((length, 128), lambda p, *_: (0, p + first))
    three = pl.BlockSpec((length, 384), lambda p, *_: (0, p))
    return pl.pallas_call(
        functools.partial(attend_backward_kernel, n, extra),
        grid_spec=pltpu.PrefetchScalarGridSpec(
            num_scalar_prefetch=2,
            grid=(number,),
            in_specs=[
                three,
                whole,
                whole,
                pl.BlockSpec((2, rows, B), lambda p, *_: (p + first, 0, 0)),
                pl.BlockSpec((1, 2, length), lambda p, *_: (p + first, 0, 0)),
                one,
                one,
                whole,
            ]
            + [HBM] * extra,
            out_specs=[three, pl.BlockSpec((1, 2, tiles, 2 * B), lambda p, *_: (p + first, 0, 0, 0))],
            scratch_shapes=[
                pltpu.VMEM((2, length, 128), BF),
                pltpu.VMEM((2, length, 128), BF),
                pltpu.VMEM((2, length, 128), BF),
                pltpu.VMEM((128, length), BF),
                pltpu.VMEM((2, length), F32),
                pltpu.VMEM((2, length, 128), F32),
                pltpu.VMEM((2, length, 128), F32),
                pltpu.VMEM((2, HD, B), F32),
                pltpu.VMEM((2, rows, B), F32),
            ],
        ),
        out_shape=[
            jax.ShapeDtypeStruct((length, width3), BF),
            jax.ShapeDtypeStruct((pairs, 2, tiles, 2 * B), F32),
        ],
        input_output_aliases={10: 1} if into else {},
        compiler_params=pltpu.CompilerParams(vmem_limit_bytes=60 * MIB),
        cost_estimate=CHEAP,
        name="attend_backward",
    )(active, order, qkv, feat_q, feat_k, bias, lse, mixed, grad, scale, *into, *deps)


def load(pieces, rows, sems):
    copies, start = [], 0
    for i, piece in enumerate(pieces):
        size = piece.shape[0]
        copies.append(pltpu.make_async_copy(piece, rows.at[pl.ds(start, size)], sems.at[i]))
        start += size

    @pl.when(pl.program_id(0) == 0)
    def _():
        for copy in copies:
            copy.start()
        for copy in copies:
            copy.wait()


def product_kernel(mode, count, extra, carried, *refs):
    pieces, w_ref = refs[:count], refs[count]
    refs = refs[count + 1 :]
    if mode == "take":
        sc_ref, refs = refs[0], refs[1:]
    refs = refs[extra:]
    o_ref, refs = refs[0], refs[1:]
    if mode == "make":
        sc_ref, refs = refs[0], refs[1:]
    rows, sems = refs[carried:]
    load(pieces, rows, sems)
    if mode == "make":

        @pl.when(pl.program_id(0) == 0)
        def _():
            step = pick(rows.shape[0], 256)

            def body(i, _):
                part = pl.ds(pl.multiple_of(i * step, step), step)
                x = rows[part, :].astype(F32)
                scale = norm_scale(x)
                sc_ref[part, :] = jnp.broadcast_to(scale, (step, 128))
                return 0

            lax.fori_loop(0, rows.shape[0] // step, body, 0)

    value = nn(rows[...], w_ref[...])
    if mode != "plain":
        value = value * sc_ref[:, 0:1]
    o_ref[...] = value.astype(BF)


def product(pieces, w, start, width, mode="plain", scale=(), deps=(), carry=()):
    length, depth = sum(p.shape[0] for p in pieces), w.shape[0]
    tile = pick(width, 512, 256, start=start)
    by_row = pl.BlockSpec((length, 128), lambda j: (0, 0))
    make = mode == "make"
    return pl.pallas_call(
        functools.partial(product_kernel, mode, len(pieces), len(deps) + len(carry), len(carry)),
        grid=(width // tile,),
        in_specs=[HBM] * len(pieces)
        + [pl.BlockSpec((depth, tile), lambda j: (0, start // tile + j))]
        + [by_row] * len(scale)
        + [HBM] * (len(deps) + len(carry)),
        out_specs=[pl.BlockSpec((length, tile), lambda j: (0, j))] + [by_row] * make + [HBM] * len(carry),
        out_shape=[jax.ShapeDtypeStruct((length, width), BF)]
        + [jax.ShapeDtypeStruct((length, 128), F32)] * make
        + [jax.ShapeDtypeStruct(c.shape, c.dtype) for c in carry],
        input_output_aliases={
            len(pieces) + 1 + len(scale) + len(deps) + i: 1 + make + i for i in range(len(carry))
        },
        scratch_shapes=[pltpu.VMEM((length, depth), BF), pltpu.SemaphoreType.DMA((len(pieces),))],
        compiler_params=pltpu.CompilerParams(vmem_limit_bytes=60 * MIB),
        cost_estimate=CHEAP,
        name="rows_product",
    )(*pieces, w, *scale, *deps, *carry)


def outer_kernel(counts, extra, *refs):
    total = sum(counts)
    groups, start = [], 0
    for count in counts:
        groups.append(refs[start : start + count])
        start += count
    rights = refs[total : total + len(counts)]
    out_ref, rows, sems = refs[total + len(counts) + extra :]
    first = 0
    for m, group in enumerate(groups):
        load(group, rows.at[m], sems.at[pl.ds(first, len(group))])
        first += len(group)
    value = tn(rights[0][...], rows[0])
    for m in range(1, len(counts)):
        value = value + tn(rights[m][...], rows[m])
    out_ref[...] = value.astype(BF).T


def outer(lefts, rights, deps=(), first=0, width=None):
    length = rights[0].shape[0]
    width = width or rights[0].shape[1]
    depth = lefts[0][0].shape[1]
    tile = pick(width, 512, 640, 384, 256, start=first)
    counts = tuple(len(group) for group in lefts)
    flat = [piece for group in lefts for piece in group]
    return pl.pallas_call(
        functools.partial(outer_kernel, counts, len(deps)),
        grid=(width // tile,),
        in_specs=[HBM] * len(flat)
        + [pl.BlockSpec((length, tile), lambda j: (0, first // tile + j))] * len(rights)
        + [HBM] * len(deps),
        out_specs=pl.BlockSpec((depth, tile), lambda j: (0, j)),
        out_shape=jax.ShapeDtypeStruct((depth, width), BF),
        scratch_shapes=[
            pltpu.VMEM((len(lefts), length, depth), BF),
            pltpu.SemaphoreType.DMA((len(flat),)),
        ],
        compiler_params=pltpu.CompilerParams(vmem_limit_bytes=60 * MIB),
        cost_estimate=CHEAP,
        name="weight_gradient",
    )(*flat, *rights, *deps)


def partial_kernel(form, layouts, against, extra, *refs):
    number = len(layouts)
    rows = refs[2 * number : 2 * number + against]
    outs = refs[2 * number + against + extra :]
    value = None
    for a_ref, w_ref, (size, pitch, start) in zip(refs[:number], refs[number:], layouts):
        for i in range(a_ref.shape[1] // size):
            cols = slice(i * pitch + start, i * pitch + start + size)
            part = nt(a_ref[:, i * size : (i + 1) * size], w_ref[:, cols])
            value = part if value is None else value + part
    if against:
        total, at = 0.0, 0
        for piece in rows:
            size = piece.shape[0]
            total = total + jnp.sum(value[at : at + size] * piece[...].astype(F32), axis=0, keepdims=True)
            at += size
        outs[-1][...] = total
        outs = outs[:-1]
    value = value.astype(BF)
    if form is None:
        outs[0][...] = value
        return
    size = outs[0].shape[0]
    half = size // 2
    blocks = [value[i * size : (i + 1) * size] for i in range(4)]
    if form != "both":
        own, pair, late = outs
        first, second = (1, 2) if form == "x" else (2, 1)
        own[...] = blocks[0]
        pair[:size] = blocks[first]
        pair[size:] = blocks[3]
        late[...] = blocks[second]
        return
    own, send_x, send_y, late_x, late_y = outs
    own[...] = blocks[0]
    send_x[:half] = blocks[1][:half]
    send_x[half:] = blocks[3][:half]
    send_y[:half] = blocks[2][half:]
    send_y[half:] = blocks[3][half:]
    late_x[...] = blocks[1][half:]
    late_y[...] = blocks[2][:half]


def partial_rows(lefts, weights, widths, ats, layouts, form, deps=(), pieces=()):
    length = lefts[0].shape[0]
    depth = weights[0].shape[0]
    tile = pick(depth, 512, 256)
    size = length // 4
    heights = {
        None: [length],
        "both": [size, size, size, size // 2, size // 2],
        "x": [size, 2 * size, size],
        "y": [size, 2 * size, size],
    }[form]
    sums = [jax.ShapeDtypeStruct((1, depth), F32)] if pieces else []
    return pl.pallas_call(
        functools.partial(partial_kernel, form, layouts, len(pieces), len(deps)),
        grid=(depth // tile,),
        in_specs=[pl.BlockSpec(a.shape, lambda j: (0, 0)) for a in lefts]
        + [pl.BlockSpec((tile, width), lambda j, at=at: (j, at)) for width, at in zip(widths, ats)]
        + [pl.BlockSpec((p.shape[0], tile), lambda j: (0, j)) for p in pieces]
        + [HBM] * len(deps),
        out_specs=[pl.BlockSpec((height, tile), lambda j: (0, j)) for height in heights]
        + [pl.BlockSpec((1, tile), lambda j: (0, j))] * len(sums),
        out_shape=[jax.ShapeDtypeStruct((height, depth), BF) for height in heights] + sums,
        compiler_params=pltpu.CompilerParams(vmem_limit_bytes=60 * MIB),
        cost_estimate=CHEAP,
        name="partial_rows",
    )(*lefts, *weights, *pieces, *deps)


def ff_kernel(count, count_cot, extra, *refs):
    total = count + count_cot
    pieces, cots = refs[:count], refs[count:total]
    w_ref, d_ref = refs[total : total + 2]
    hid_ref, g_ref, rows, cot, sems = refs[total + 2 + extra :]
    load(pieces, rows, sems.at[pl.ds(0, count)])
    load(cots, cot, sems.at[pl.ds(count, count_cot)])
    tile = d_ref.shape[1]
    length = rows.shape[0]
    step = pick(length, 256)
    c = 0.7978845608028654
    for i in range(length // step):
        part = slice(i * step, (i + 1) * step)
        both = nn(rows[part], w_ref[...])
        grad = nn(cot[part], d_ref[...])
        gate, up = both[:, :tile], both[:, tile:]
        square = gate * gate
        th = jnp.tanh(c * gate * (1.0 + 0.044715 * square))
        half = 0.5 * (1.0 + th)
        value = gate * half
        slope = half + 0.5 * gate * (1.0 - th * th) * (c + 3 * 0.044715 * c * square)
        hid_ref[part] = (value * up).astype(BF)
        g_ref[part, :tile] = (grad * up * slope).astype(BF)
        g_ref[part, tile:] = (grad * value).astype(BF)


def ff_tile(width):
    return pick(width, 256)


def feed_forward(pieces, cots, w, first, number, into=(), deps=()):
    length, depth, width = sum(p.shape[0] for p in pieces), w.shape[0], w.shape[1] // 3
    tile = ff_tile(width)
    count = len(pieces) + len(cots)
    extra = len(deps) + len(into)
    return pl.pallas_call(
        functools.partial(ff_kernel, len(pieces), len(cots), extra),
        grid=(number,),
        in_specs=[HBM] * count
        + [
            pl.BlockSpec((depth, 2 * tile), lambda j: (0, j + first)),
            pl.BlockSpec((depth, tile), lambda j: (0, j + first + 2 * width // tile)),
        ]
        + [HBM] * extra,
        out_specs=[
            pl.BlockSpec((length, tile), lambda j: (0, j + first)),
            pl.BlockSpec((length, 2 * tile), lambda j: (0, j + first)),
        ],
        out_shape=[
            jax.ShapeDtypeStruct((length, width), BF),
            jax.ShapeDtypeStruct((length, 2 * width), BF),
        ],
        input_output_aliases={count + 2 + i: i for i in range(len(into))},
        scratch_shapes=[
            pltpu.VMEM((length, depth), BF),
            pltpu.VMEM((length, depth), BF),
            pltpu.SemaphoreType.DMA((count,)),
        ],
        compiler_params=pltpu.CompilerParams(vmem_limit_bytes=60 * MIB),
        cost_estimate=CHEAP,
        name="feed_forward",
    )(*pieces, *cots, w, w, *into, *deps)


def hop(part, bit, count, axis="tensor"):
    return lax.ppermute(part, axis, [(i, i ^ bit) for i in range(count)])


class Gather:
    def __init__(self, part, via, count, then=()):
        self.own = part
        if count != 4:
            self.first = self.sent = (lax.all_gather(part, "tensor", axis=0, tiled=True),)
            self.pieces = list(self.first)
            return
        from_x, from_y = hop(part, 1, count), hop(part, 2, count)
        self.first = (from_x, from_y)
        half = part.shape[0] // 2
        self.pieces = [part, from_x, from_y]
        if then:
            from_x, from_y = lax.optimization_barrier((from_x, from_y, *then))[:2]
        if via == "x":
            self.pieces.append(hop(from_y, 1, count))
        elif via == "y":
            self.pieces.append(hop(from_x, 2, count))
        else:
            self.sent = (from_y[:half], from_x[half:])
            self.pieces += [hop(self.sent[0], 1, count), hop(self.sent[1], 2, count)]


def add_kernel(number, carried, *refs):
    ins, outs = refs[: 2 * number], refs[len(refs) - number - carried :][:number]
    for i, out in enumerate(outs):
        out[...] = (ins[2 * i][...].astype(F32) + ins[2 * i + 1][...].astype(F32)).astype(BF)


def add_arrived(pairs, deps, carry):
    depth = pairs[0][0].shape[1]
    tile = pick(depth, 1024)
    specs, args, outs = [], [], []
    for late, arrived in pairs:
        height = late.shape[0]
        specs += [pl.BlockSpec((height, tile), lambda j: (0, j)), pl.BlockSpec((height, tile), lambda j: (1, j))]
        args += [late, arrived]
        outs.append(late)
    return pl.pallas_call(
        functools.partial(add_kernel, len(pairs), len(carry)),
        grid=(depth // tile,),
        in_specs=specs + [HBM] * (len(deps) + len(carry)),
        out_specs=[pl.BlockSpec((o.shape[0], tile), lambda j: (0, j)) for o in outs] + [HBM] * len(carry),
        out_shape=[jax.ShapeDtypeStruct(o.shape, o.dtype) for o in (*outs, *carry)],
        input_output_aliases={len(args) + len(deps) + i: len(outs) + i for i in range(len(carry))},
        compiler_params=pltpu.CompilerParams(vmem_limit_bytes=60 * MIB),
        cost_estimate=CHEAP,
        name="add_arrived",
    )(*args, *deps, *carry)


class Reduce:
    def __init__(self, parts, form, count, then=()):
        if then:
            parts = lax.optimization_barrier((*parts, *then))[: len(parts)]
        self.form, self.count, self.parts = form, count, parts
        if count != 4:
            self.total = lax.psum_scatter(parts[0], "tensor", scatter_dimension=0, tiled=True).astype(F32)
        elif form == "both":
            self.arrived = (hop(parts[1], 1, count), hop(parts[2], 2, count))
        else:
            self.arrived = (hop(parts[1], 1 if form == "x" else 2, count),)

    def first(self, deps=(), carry=()):
        if self.count != 4:
            return (self.total, *carry)
        if self.form == "both":
            x_first, y_first = self.arrived
            late = add_arrived([(self.parts[3], y_first), (self.parts[4], x_first)], deps, carry)
            self.second = (hop(late[0], 1, self.count), hop(late[1], 2, self.count))
        else:
            late = add_arrived([(self.parts[2], self.arrived[0])], deps, carry)
            self.second = (hop(late[0], 2 if self.form == "x" else 1, self.count),)
        return tuple(late)

    def settle(self, function, rows, kinds, deps=(), carry=()):
        if self.count != 4:
            return (*function(self.total, *rows), *carry)
        return settle_rows(
            self.form, self.parts[0], self.arrived, self.second, function, rows, kinds, deps, carry
        )


def settle_kernel(form, function, number, extra, kinds, *refs):
    own = refs[0][...].astype(F32)
    if form == "both":
        x_first, y_first, x_second, y_second = refs[1:5]
        refs = refs[5:]
        low = pl.program_id(0) == 0
        total = own + jnp.where(
            low,
            x_first[...].astype(F32) + y_second[...].astype(F32),
            y_first[...].astype(F32) + x_second[...].astype(F32),
        )
    else:
        total = own + refs[1][...].astype(F32) + refs[2][...].astype(F32)
        refs = refs[3:]
    values = function(total, *(ref[...] for ref in refs[:number]))
    for out, kind, value in zip(refs[number + extra :], kinds, values):
        if kind != "sum":
            out[...] = value
            continue

        @pl.when(pl.program_id(0) == 0)
        def _(out=out):
            out[...] = jnp.zeros_like(out)

        out[...] += value


def settle_rows(form, own, arrived, second, function, rows, kinds, deps, carry):
    size, depth = own.shape
    half = size // 2
    block = pl.BlockSpec((half, depth), lambda i: (i, 0))
    top = pl.BlockSpec((half, depth), lambda i: (0, 0))
    others = [top] * 4 if form == "both" else [block] * 2
    out_specs, out_shape = [], []
    for kind in kinds:
        out_specs.append(pl.BlockSpec((1, depth), lambda i: (0, 0)) if kind == "sum" else block)
        out_shape.append(
            jax.ShapeDtypeStruct((1, depth), F32) if kind == "sum" else jax.ShapeDtypeStruct((size, depth), kind)
        )
    return pl.pallas_call(
        functools.partial(settle_kernel, form, function, len(rows), len(deps) + len(carry), kinds),
        grid=(2,),
        in_specs=[block] + others + [block] * len(rows) + [HBM] * (len(deps) + len(carry)),
        out_specs=out_specs + [HBM] * len(carry),
        out_shape=out_shape + [jax.ShapeDtypeStruct(c.shape, c.dtype) for c in carry],
        input_output_aliases={
            1 + len(others) + len(rows) + len(deps) + i: len(kinds) + i for i in range(len(carry))
        },
        compiler_params=pltpu.CompilerParams(vmem_limit_bytes=60 * MIB),
        cost_estimate=CHEAP,
        name="settle_rows",
    )(own, *arrived, *second, *rows, *deps, *carry)


def bits(count):
    assert count & (count - 1) == 0
    return [1 << i for i in range(count.bit_length() - 1)]


def sum_over(value, axis, count):
    for bit in bits(count):
        value = value + hop(value, bit, count, axis)
    return value


def norm_scale(rows):
    return lax.rsqrt(jnp.mean(rows * rows, axis=-1, keepdims=True) + EPSILON)


def add_branch(total, rows):
    middle = rows.astype(F32) + total
    return middle, (middle * norm_scale(middle)).astype(BF)


def add_last(total, middle):
    return ((middle + total).astype(BF),)


def turn_back(total, middle, cotangent):
    scale = norm_scale(middle)
    inner = jnp.mean(total * middle, axis=-1, keepdims=True)
    grad = cotangent.astype(F32) + scale * total - middle * (scale * scale * scale * inner)
    return grad, grad.astype(BF), jnp.sum(total * middle * scale, axis=0, keepdims=True)


def finish_back(total, rows, grad_middle):
    rows = rows.astype(F32)
    scale = norm_scale(rows)
    inner = jnp.mean(total * rows, axis=-1, keepdims=True)
    grad = grad_middle + total - rows * (scale * scale * inner)
    return (grad.astype(BF),)


def unpack_kernel(groups, pitch, *refs):
    parts, gain_ref, outs = refs[: len(groups)], refs[len(groups)], refs[len(groups) + 1 :]
    at = 0
    for part, number in zip(parts, groups):
        size = part.shape[1] // (number * pitch)
        for i in range(number):
            for k, out in enumerate(outs):
                start = (i * pitch + k) * size
                out[:, at : at + size] = part[:, start : start + size].astype(F32) * gain_ref[...]
            at += size


def turn_kernel(number, *refs):
    for part, out in zip(refs[:number], refs[number:]):
        out[...] = part[...].astype(F32).T


def turned(parts):
    return pl.pallas_call(
        functools.partial(turn_kernel, len(parts)),
        out_shape=[jax.ShapeDtypeStruct(p.shape[::-1], F32) for p in parts],
        compiler_params=pltpu.CompilerParams(vmem_limit_bytes=60 * MIB),
        cost_estimate=CHEAP,
        name="turned",
    )(*parts)


def unpack(parts, groups, pitch, gain):
    rows_w = gain.shape[0]
    width = sum(p.shape[1] for p in parts) // pitch
    return pl.pallas_call(
        functools.partial(unpack_kernel, groups, pitch),
        out_shape=[jax.ShapeDtypeStruct((rows_w, width), F32)] * pitch,
        compiler_params=pltpu.CompilerParams(vmem_limit_bytes=60 * MIB),
        cost_estimate=CHEAP,
        name="unpack",
    )(*parts, gain)


def local(
    count_dp,
    count,
    tokens,
    cotangent,
    doc_lengths,
    rel_bucket,
    gain_attn,
    w_query,
    w_key,
    w_value,
    w_out,
    rel_table,
    gain_ff,
    w_gate,
    w_up,
    w_down,
):
    slots = tokens.shape[0]
    length = slots * count
    blocks = length // B
    rows_w, width = w_query.shape
    width_ff = w_gate.shape[1]
    pairs = width // 128
    heads = width // HD
    buckets_local = rel_table.shape[0]
    buckets = buckets_local * count_dp
    docs = doc_lengths.shape[1]
    tile = ff_tile(width_ff)
    me = lax.axis_index("dp").astype(jnp.int32)

    def spread(part):
        return lax.all_gather(part, "dp", axis=0, tiled=True)

    def after(value, *others):
        return lax.optimization_barrier((value, *others))[0]

    xs = [tokens[:, m] for m in range(MICRO)]
    gain_one = gain_attn.astype(F32)[:, None]
    gain_two = gain_ff.astype(F32)[:, None]
    cuts = 2
    each = pairs // cuts
    part_w = each * 384

    def grouped(weights, size):
        number = weights[0].shape[1] // size
        return jnp.stack([w.reshape(rows_w, number, size) for w in weights], axis=2).reshape(rows_w, -1)

    def scaled(w, gain):
        return (w.astype(F32) * gain).astype(BF)

    local_qkv = grouped([scaled(w, gain_one) for w in (w_query, w_key, w_value)], 128)
    halves = [local_qkv[:, cut * part_w : (cut + 1) * part_w] for cut in range(cuts)]
    halves[-1] = jnp.concatenate([halves[-1], w_out.T], axis=1)
    full_qkv = [spread(half) for half in halves]
    full_out, out_at = full_qkv[-1], part_w
    local_ff = grouped([scaled(after(w_gate, xs[0]), gain_two), scaled(w_up, gain_two)], tile)
    full_ff = spread(jnp.concatenate([local_ff, w_down.T], axis=1))

    table = rel_table.reshape(1, buckets_local * heads)
    for bit in bits(count_dp):
        table = jnp.concatenate([table, hop(table, bit, count_dp, "dp")], axis=0)
    table = jnp.take(table, jnp.arange(count_dp, dtype=jnp.int32) ^ me, axis=0).reshape(buckets, heads)
    reverse = jnp.concatenate([jnp.full((1,), -1, jnp.int32), rel_bucket[::-1]])
    onehot = reverse[None, :] == jnp.arange(buckets, dtype=jnp.int32)[:, None]
    offsets = tn(table, onehot.astype(BF)).reshape(heads, 2 * blocks, B)
    tiles = 2 * blocks - 1
    ahead = offsets[:, ::-1]
    bias = bias_strips(jnp.concatenate([ahead[:, :tiles], ahead[:, 1:]], axis=2))

    order = jnp.arange(blocks, dtype=jnp.int32)
    if count == 4:
        order = order ^ lax.axis_index("tensor").astype(jnp.int32)
    positions = (order[:, None] * B + jnp.arange(B, dtype=jnp.int32)[None]).reshape(-1)
    ends = jnp.cumsum(doc_lengths, axis=1)
    lane = jnp.arange(128, dtype=jnp.int32) % HD

    cs, masks = [], []
    for m in range(MICRO):
        cs.append(cotangent[:, m])
        number = jnp.sum((positions[:, None] >= ends[m][None, :]).astype(jnp.int32), axis=1)
        by_block = number.reshape(blocks, B)
        least, most = by_block.min(axis=1), by_block.max(axis=1)
        active = (least[:, None] <= most[None, :]) & (least[None, :] <= most[:, None])
        same = number[:, None] == lane[None, :]
        feat_q = same.astype(BF)
        feat_k = jnp.where(same | (lane >= docs)[None, :], 0.0, -BIG).astype(BF)
        masks.append((feat_q, feat_k, active.astype(jnp.int32).reshape(-1)))
    form = "both" if count == 4 else None
    ones = [Gather(xs[0], "both", count, (bias,))]
    ones.append(Gather(after(xs[1], *ones[0].pieces), "x", count))

    def project(m, cut, scale, deps):
        mode = "take" if scale else "make"
        return product(ones[m].pieces, full_qkv[cut], 0, part_w, mode, scale, deps)

    def forward(m, cut, qkv, into, deps):
        feat_q, feat_k, active = masks[m]
        return attend_forward(qkv, feat_q, feat_k, bias, active, order, cut * each, into, deps)

    def out_rows(mixed, deps):
        return partial_rows([mixed], [full_out], [full_out.shape[1]], [0], [(width, width, out_at)], form, deps)

    def ff_rows(left, inner, way, deps):
        size = 2 * width_ff if inner else width_ff
        return partial_rows([left], [full_ff], [size], [0 if inner else 2], [(size, size, 0)], way, deps)

    def qkv_rows(projects, m, deps):
        return partial_rows(
            projects, full_qkv, [part_w] * cuts, [0] * cuts, [(part_w, part_w, 0)] * cuts, form, deps, ones[m].pieces
        )

    def scatter(value):
        return lax.psum_scatter(value, "dp", scatter_dimension=0, tiled=True)

    qkv_0a, scale_0 = project(0, 0, (), ())
    cots = [Gather(after(cs[0], qkv_0a), "y", count)]
    into = forward(0, 0, qkv_0a, (), ())
    (qkv_0b,) = project(0, 1, (scale_0,), (into[0], *ones[1].first))
    cots.append(Gather(after(cs[1], qkv_0b), "x", count))
    mixed_0, lse_0 = forward(0, 1, qkv_0b, into, ones[1].first)
    parts = out_rows(mixed_0, cots[0].first)
    sum_0 = Reduce(parts, form, count)
    qkv_1a, scale_1 = project(1, 0, (), (parts[0],))
    into = forward(1, 0, qkv_1a, (), (*cots[0].pieces, *cots[1].first))
    late = sum_0.first((into[0],))
    (qkv_1b,) = project(1, 1, (scale_1,), (late[0],))
    middle_0, normed = sum_0.settle(add_branch, [xs[0]], (F32, BF), (qkv_1b, *cots[1].pieces))
    twos = [Gather(normed, "both", count)]
    mixed_1, lse_1 = forward(1, 1, qkv_1b, into, (normed,))
    parts = out_rows(mixed_1, twos[0].sent)
    sum_1 = Reduce(parts, form, count)

    steps = width_ff // tile
    early = (steps + 1) // 2
    into = feed_forward(twos[0].pieces, cots[0].pieces, full_ff, 0, early, (), (parts[0],))
    late = sum_1.first((into[0],))
    hidden_0, grad_ff_0 = feed_forward(
        twos[0].pieces, cots[0].pieces, full_ff, early, steps - early, into, (late[0],)
    )
    middle_1, normed = sum_1.settle(add_branch, [xs[1]], (F32, BF), (hidden_0,))
    twos.append(Gather(normed, "both", count))
    parts = ff_rows(grad_ff_0, True, form, (normed,))
    sum_0 = Reduce(parts, form, count, twos[1].pieces)
    hidden_1, grad_ff_1 = feed_forward(
        twos[1].pieces, cots[1].pieces, full_ff, 0, steps, (), (parts[0],)
    )
    late = sum_0.first((hidden_1,))
    parts = ff_rows(grad_ff_1, True, form, (late[0],))
    sum_1 = Reduce(parts, form, count)
    grad_middle_0, rounded, gain_two_0 = sum_0.settle(
        turn_back, [middle_0, cs[0]], (F32, BF, "sum"), (parts[0],)
    )
    mids = [Gather(rounded, "both", count)]
    weight = outer([c.pieces for c in cots], [hidden_0, hidden_1], (rounded,))
    late = sum_1.first((), (weight,))
    grad_down = scatter(late[-1])
    two_pieces, grad_ffs = [g.pieces for g in twos], [grad_ff_0, grad_ff_1]
    ff_half = early * 2 * tile
    weight = outer(two_pieces, grad_ffs, (late[0], *mids[0].sent), 0, ff_half)
    grad_middle_1, rounded, gain_two_1, weight = sum_1.settle(
        turn_back, [middle_1, cs[1]], (F32, BF, "sum"), tuple(mids[0].pieces), (weight,)
    )
    grad_ff_a = scatter(weight)
    mids.append(Gather(rounded, "both", count))

    def backward(m, qkv, lse, mixed, grad, scale, cut, into, deps):
        feat_q, feat_k, active = masks[m]
        return attend_backward(
            qkv, feat_q, feat_k, bias, lse, mixed, grad, scale, active, order, cut * each, into, deps
        )

    way = ("x", "y") if form else (None, None)
    (grad,) = product(mids[0].pieces, full_out, out_at, width, deps=(rounded,))
    grad_0a, fold = backward(0, qkv_0a, lse_0, mixed_0, grad, scale_0, 0, (), ())
    parts = ff_rows(hidden_0, False, way[0], (grad_0a,))
    down_0 = Reduce(parts, way[0], count)
    grad_0b, fold_0 = backward(0, qkv_0b, lse_0, mixed_0, grad, scale_0, 1, (fold,), (parts[0],))
    *parts, gain_one_0 = qkv_rows([grad_0a, grad_0b], 0, (*mids[1].sent, grad_down))
    sum_0 = Reduce(parts, form, count)
    weight = outer(two_pieces, grad_ffs, (parts[0],), ff_half, 2 * width_ff - ff_half)
    late = down_0.first((grad_ff_a, weight))
    (grad,) = product(mids[1].pieces, full_out, out_at, width, deps=(late[0],))
    late = sum_0.first((grad,), (weight,))
    grad_ff_b = scatter(late[-1])
    grad_1a, fold = backward(1, qkv_1a, lse_1, mixed_1, grad, scale_1, 0, (), (late[0],))
    (output_0,) = down_0.settle(add_last, [middle_0], (BF,), (grad_1a,))
    weight = outer([g.pieces for g in mids], [mixed_0, mixed_1], (output_0,))
    token_0, weight = sum_0.settle(finish_back, [xs[0], grad_middle_0], (BF,), (), (weight,))
    grad_out = scatter(weight)
    weight = outer([g.pieces for g in ones], [grad_0a, grad_1a], (token_0,))
    parts = ff_rows(hidden_1, False, way[1], (weight, grad_ff_b))
    down_1 = Reduce(parts, way[1], count)
    grad_1b, fold_1 = backward(1, qkv_1b, lse_1, mixed_1, grad, scale_1, 1, (fold,), (parts[0],))
    late = down_1.first((grad_1b,), (weight,))
    grad_qkv_a = scatter(late[-1])
    *parts, gain_one_1 = qkv_rows([grad_1a, grad_1b], 1, (late[0], grad_out))
    sum_1 = Reduce(parts, form, count)
    weight = outer([g.pieces for g in ones], [grad_0b, grad_1b], (parts[0],))
    late = sum_1.first((), (weight,))
    grad_qkv_b = scatter(late[-1])
    (output_1,) = down_1.settle(add_last, [middle_1], (BF,), (late[0],))
    grad_gate, grad_up = unpack(
        [grad_ff_a, grad_ff_b], (early, steps - early), 2, gain_two
    )
    grad_out, grad_down = turned([grad_out, grad_down])
    fold = (fold_0 + fold_1).reshape(heads, tiles, 2 * B)
    zero = jnp.zeros((heads, 1, B), F32)
    by_offset = (
        jnp.concatenate([fold[:, :, :B], zero], axis=1)
        + jnp.concatenate([zero, fold[:, :, B:]], axis=1)
    )[:, ::-1].reshape(heads, 2 * length)
    grad_table = lax.dot_general(
        onehot.astype(F32), by_offset, (((1,), (1,)), ((), ())), precision=lax.Precision.HIGHEST
    )
    small = jnp.concatenate(
        [
            (gain_one_0 + gain_one_1).reshape(count_dp, rows_w),
            (gain_two_0 + gain_two_1).reshape(count_dp, rows_w),
            grad_table.reshape(count_dp, buckets_local * heads),
        ],
        axis=1,
    )
    small = lax.dynamic_index_in_dim(sum_over(small, "dp", count_dp), me, 0, keepdims=False)
    both_gains = sum_over(small[: 2 * rows_w], "tensor", count)
    (token_1,) = sum_1.settle(
        finish_back,
        [xs[1], grad_middle_1],
        (BF,),
        (output_1, grad_qkv_a, grad_gate, grad_out, grad_down, both_gains),
    )
    return (
        jnp.stack([output_0, output_1], axis=1),
        jnp.stack([token_0, token_1], axis=1),
        both_gains[:rows_w] / gain_one[:, 0],
        *unpack([grad_qkv_a, grad_qkv_b], (each, each), 3, gain_one),
        grad_out,
        small[2 * rows_w :].reshape(buckets_local, heads),
        both_gains[rows_w:] / gain_two[:, 0],
        grad_gate,
        grad_up,
        grad_down,
    )


def solution(mesh):
    row, col = P("dp", "tensor"), P("tensor", "dp")
    acts = P("tensor", "dp", None)
    in_specs = (
        acts, acts, P("dp", None), P(), P("dp"), row, row, row, col, row, P("dp"), row, row, col
    )
    out_specs = (acts, acts, P("dp"), row, row, row, col, row, P("dp"), row, row, col)
    body = functools.partial(local, mesh.shape["dp"], mesh.shape["tensor"])
    return jax.shard_map(body, mesh=mesh, in_specs=in_specs, out_specs=out_specs, check_vma=False)
```

```python
import functools
import jax
import jax.numpy as jnp
from jax import lax
from jax.experimental import pallas as pl
from jax.experimental.pallas import tpu as pltpu
from jax.sharding import PartitionSpec as P

HD=64
B=256
BIG=1e30
F32=jnp.float32; BF=jnp.bfloat16

def nt(a,b): return lax.dot_general(a,b,(((1,),(1,)),((),())),preferred_element_type=F32)
def nn(a,b): return lax.dot_general(a,b,(((1,),(0,)),((),())),preferred_element_type=F32)


EPSILON = 1e-06
MICRO = 2
HBM = pl.BlockSpec(memory_space=pltpu.HBM)
MIB = 1 << 20


def cost(flops):
    return pl.CostEstimate(flops=int(2 * flops), bytes_accessed=1, transcendentals=0)


def tn(left, right):
    return lax.dot_general(left, right, (((0,), (0,)), ((), ())), preferred_element_type=F32)


def pick(size, *tiles, start=0):
    return next(tile for tile in (*tiles, 128, size) if size % tile == 0 and start % tile == 0)


def strips_kernel(w_ref, out_ref):
    def body(i, _):
        wide = jnp.broadcast_to(w_ref[0, pl.ds(i, 1), :], (B, 2 * B))
        rolled = pltpu.roll(wide, 0, 1, stride=1, stride_axis=0)
        out_ref[0, pl.ds(pl.multiple_of(i * B, B), B), :] = rolled[:, :B]
        return 0

    lax.fori_loop(0, w_ref.shape[1], body, 0)


def bias_strips(w):
    heads, tiles, _ = w.shape
    return pl.pallas_call(
        strips_kernel,
        grid=(heads,),
        in_specs=[pl.BlockSpec((1, tiles, 2 * B), lambda h: (h, 0, 0))],
        out_specs=pl.BlockSpec((1, tiles * B, B), lambda h: (h, 0, 0)),
        out_shape=jax.ShapeDtypeStruct((heads, tiles * B, B), F32),
        compiler_params=pltpu.CompilerParams(vmem_limit_bytes=60 * MIB),
        cost_estimate=cost(6e9),
        name="bias_strips",
    )(w)


def by_tile(act_ref, base, n, *functions):
    count = act_ref[base]
    for i in range(1, n):
        count = count + act_ref[base + i]
    most = count * 4 >= 3 * n

    @pl.when(most)
    def _():
        for function in functions:
            for i in range(n):
                function(i)

    @pl.when(jnp.logical_not(most))
    def _():
        for function in functions:

            def step(i, _, function=function):
                @pl.when(act_ref[base + i] != 0)
                def _():
                    function(i)

                return 0

            lax.fori_loop(0, n, step, 0)


def attend_forward_kernel(n, extra, *refs):
    act_ref, blk_ref, qkv_ref, fq_ref, fk_ref, bias_ref = refs[:6]
    o_ref, lse_ref, qx, kx, vx, s_scr, m_scr, o_scr = refs[6 + extra :]
    lane = lax.broadcasted_iota(jnp.int32, (1, 128), 1)
    q, k, v = qkv_ref[:, 0:128], qkv_ref[:, 128:256], qkv_ref[:, 256:384]
    vt = v.T
    for h in range(2):
        own = (lane < HD) if h == 0 else (lane >= HD)
        qx[h] = jnp.where(own, q, fq_ref[...]).T
        kx[h] = jnp.where(own, k, fk_ref[...])
        vx[h] = jnp.concatenate([vt[h * HD : (h + 1) * HD], jnp.ones((16, vt.shape[1]), BF)], axis=0)

    def row(qi, _):
        qs = pl.ds(pl.multiple_of(qi * B, B), B)
        m_scr[...] = jnp.full_like(m_scr, -3e38)
        o_scr[...] = jnp.zeros_like(o_scr)

        def score(kb):
            ks = pl.ds(pl.multiple_of(kb * B, B), B)
            bs = pl.ds(pl.multiple_of((blk_ref[kb] - blk_ref[qi] + n - 1) * B, B), B)
            for h in range(2):
                s = nn(kx[h, ks, :], qx[h, :, qs]) + bias_ref[h, bs, :]
                s_scr[h, ks, :] = s
                m_scr[h] = jnp.maximum(m_scr[h], jnp.max(s.reshape(B // 8, 8, B), axis=0))

        def share(kb):
            ks = pl.ds(pl.multiple_of(kb * B, B), B)
            for h in range(2):
                p = jnp.exp(s_scr[h, ks, :] - jnp.max(m_scr[h], axis=0, keepdims=True)).astype(BF)
                o_scr[h] += nn(vx[h, :, ks], p)

        by_tile(act_ref, qi * n, n, score, share)
        peaks = [jnp.max(m_scr[h], axis=0, keepdims=True) for h in range(2)]
        outs = []
        for h in range(2):
            total = o_scr[h, HD : HD + 1, :]
            outs.append(o_scr[h, 0:HD, :] / total)
            lse_ref[0, pl.ds(h, 1), qs] = peaks[h] + jnp.log(total)
        o_ref[qs, :] = jnp.concatenate(outs, axis=0).T.astype(BF)
        return 0

    lax.fori_loop(0, n, row, 0)


def attend_forward(qkv, feat_q, feat_k, bias, active, order, first, into=(), deps=()):
    length, width3 = qkv.shape
    n, number, pairs = length // B, width3 // 384, bias.shape[0] // 2
    rows = (2 * n - 1) * B
    extra = len(into) + len(deps)
    whole = pl.BlockSpec((length, 128), lambda p, *_: (0, 0))
    return pl.pallas_call(
        functools.partial(attend_forward_kernel, n, extra),
        grid_spec=pltpu.PrefetchScalarGridSpec(
            num_scalar_prefetch=2,
            grid=(number,),
            in_specs=[
                pl.BlockSpec((length, 384), lambda p, *_: (0, p)),
                whole,
                whole,
                pl.BlockSpec((2, rows, B), lambda p, *_: (p + first, 0, 0)),
            ]
            + [HBM] * extra,
            out_specs=[
                pl.BlockSpec((length, 128), lambda p, *_: (0, p + first)),
                pl.BlockSpec((1, 2, length), lambda p, *_: (p + first, 0, 0)),
            ],
            scratch_shapes=[
                pltpu.VMEM((2, 128, length), BF),
                pltpu.VMEM((2, length, 128), BF),
                pltpu.VMEM((2, HD + 16, length), BF),
                pltpu.VMEM((2, length, B), F32),
                pltpu.VMEM((2, 8, B), F32),
                pltpu.VMEM((2, HD + 16, B), F32),
            ],
        ),
        out_shape=[
            jax.ShapeDtypeStruct((length, pairs * 128), BF),
            jax.ShapeDtypeStruct((pairs, 2, length), F32),
        ],
        input_output_aliases={6 + i: i for i in range(len(into))},
        compiler_params=pltpu.CompilerParams(vmem_limit_bytes=60 * MIB),
        cost_estimate=cost(3.7e9 * number),
        name="attend_forward",
    )(active, order, qkv, feat_q, feat_k, bias, *into, *deps)


def attend_backward_kernel(n, extra, *refs):
    act_ref, blk_ref, qkv_ref, fq_ref, fk_ref, bias_ref, lse_ref, o_ref, do_ref, sc_ref = refs[:10]
    g_ref, fold_ref, qx, kx, v0, kt, delta, dk, dv, dqt, diag, p_scr, ds_scr, dot_ = refs[10 + extra :]
    lane = lax.broadcasted_iota(jnp.int32, (1, 128), 1)
    q, k, v = qkv_ref[:, 0:128], qkv_ref[:, 128:256], qkv_ref[:, 256:384]
    for h in range(2):
        own = (lane < HD) if h == 0 else (lane >= HD)
        qx[h] = jnp.where(own, q, fq_ref[...]).T
        kx[h] = jnp.where(own, k, fk_ref[...])
        v0[h] = jnp.where(own, v, jnp.zeros_like(v))
    kt[...] = k.T
    dot_[...] = do_ref[...].T
    prod = (o_ref[...].astype(F32) * do_ref[...].astype(F32)).T
    for h in range(2):
        delta[h : h + 1, :] = jnp.sum(prod[h * HD : (h + 1) * HD], axis=0, keepdims=True)
    diag[...] = jnp.zeros_like(diag)
    dqt[...] = jnp.zeros_like(dqt)

    def column(kb, _):
        ks = pl.ds(pl.multiple_of(kb * B, B), B)

        def tile(qi):
            qs = pl.ds(pl.multiple_of(qi * B, B), B)
            bs = pl.ds(pl.multiple_of((blk_ref[kb] - blk_ref[qi] + n - 1) * B, B), B)
            for h in range(2):
                s = nn(kx[h, ks, :], qx[h, :, qs]) + bias_ref[h, bs, :]
                dp = nn(v0[h, ks, :], dot_[:, qs])
                p = jnp.exp(s - lse_ref[0, pl.ds(h, 1), qs])
                ds = p * (dp - delta[pl.ds(h, 1), qs])
                p_scr[h, :, qs] = p.astype(BF)
                ds_scr[h, :, qs] = ds.astype(BF)
                diag[h, bs, :] += ds

        count = act_ref[kb * n]
        for i in range(1, n):
            count = count + act_ref[kb * n + i]

        @pl.when(count * 4 < 3 * n)
        def _():
            p_scr[...] = jnp.zeros_like(p_scr)
            ds_scr[...] = jnp.zeros_like(ds_scr)

        by_tile(act_ref, kb * n, n, tile)
        for h in range(2):
            dv[h, ks, :] = nn(p_scr[h], do_ref[...])
            dk[h, ks, :] = nn(ds_scr[h], qkv_ref[:, 0:128])
            dqt[h * HD : (h + 1) * HD, :] += nn(kt[h * HD : (h + 1) * HD, ks], ds_scr[h])
        return 0

    lax.fori_loop(0, n, column, 0)
    g_ref[:, 0:128] = (dqt[...].T * sc_ref[...]).astype(BF)
    left = lane < HD
    g_ref[:, 128:256] = (jnp.where(left, dk[0], dk[1]) * sc_ref[...]).astype(BF)
    g_ref[:, 256:384] = (jnp.where(left, dv[0], dv[1]) * sc_ref[...]).astype(BF)
    row = lax.broadcasted_iota(jnp.int32, (B, B), 0)
    below = row >= lax.broadcasted_iota(jnp.int32, (B, B), 1)
    half = B // 2
    flip = lax.broadcasted_iota(jnp.int32, (half, half), 0) + lax.broadcasted_iota(jnp.int32, (half, half), 1)
    flip = (flip == half - 1).astype(BF)
    for h in range(2):
        for j in range(2 * n):
            low = diag[h, (j - 1) * B : j * B, :] if j > 0 else 0.0
            high = diag[h, j * B : (j + 1) * B, :] if j < 2 * n - 1 else 0.0
            part = jnp.where(below, low, high)
            part = part[:half] + jnp.concatenate([part[half:, half:], part[half:, :half]], axis=1)
            part = pltpu.roll(nn(flip, part.astype(BF)), half + 1, 1, stride=1, stride_axis=0)
            fold_ref[0, h, j : j + 1, :] = jnp.sum(part, axis=0, keepdims=True)


def attend_backward(
    qkv, feat_q, feat_k, bias, lse, mixed, grad, scale, active, order, first, into=(), deps=()
):
    length, width3 = qkv.shape
    n, number, pairs = length // B, width3 // 384, bias.shape[0] // 2
    tiles = 2 * n - 1
    rows = tiles * B
    extra = len(into) + len(deps)
    whole = pl.BlockSpec((length, 128), lambda p, *_: (0, 0))
    one = pl.BlockSpec((length, 128), lambda p, *_: (0, p + first))
    three = pl.BlockSpec((length, 384), lambda p, *_: (0, p))
    return pl.pallas_call(
        functools.partial(attend_backward_kernel, n, extra),
        grid_spec=pltpu.PrefetchScalarGridSpec(
            num_scalar_prefetch=2,
            grid=(number,),
            in_specs=[
                three,
                whole,
                whole,
                pl.BlockSpec((2, rows, B), lambda p, *_: (p + first, 0, 0)),
                pl.BlockSpec((1, 2, length), lambda p, *_: (p + first, 0, 0)),
                one,
                one,
                whole,
            ]
            + [HBM] * extra,
            out_specs=[three, pl.BlockSpec((1, 2, 2 * n, B), lambda p, *_: (p + first, 0, 0, 0))],
            scratch_shapes=[
                pltpu.VMEM((2, 128, length), BF),
                pltpu.VMEM((2, length, 128), BF),
                pltpu.VMEM((2, length, 128), BF),
                pltpu.VMEM((128, length), BF),
                pltpu.VMEM((2, length), F32),
                pltpu.VMEM((2, length, 128), F32),
                pltpu.VMEM((2, length, 128), F32),
                pltpu.VMEM((2 * HD, length), F32),
                pltpu.VMEM((2, rows, B), F32),
                pltpu.VMEM((2, B, length), BF),
                pltpu.VMEM((2, B, length), BF),
                pltpu.VMEM((128, length), BF),
            ],
        ),
        out_shape=[
            jax.ShapeDtypeStruct((length, width3), BF),
            jax.ShapeDtypeStruct((pairs, 2, 2 * n, B), F32),
        ],
        input_output_aliases={10: 1} if into else {},
        compiler_params=pltpu.CompilerParams(vmem_limit_bytes=60 * MIB),
        cost_estimate=cost(6.5e9 * number),
        name="attend_backward",
    )(active, order, qkv, feat_q, feat_k, bias, lse, mixed, grad, scale, *into, *deps)


def load(pieces, rows, sems):
    copies, start = [], 0
    for i, piece in enumerate(pieces):
        size = piece.shape[0]
        copies.append(pltpu.make_async_copy(piece, rows.at[pl.ds(start, size)], sems.at[i]))
        start += size

    @pl.when(pl.program_id(0) == 0)
    def _():
        for copy in copies:
            copy.start()
        for copy in copies:
            copy.wait()


def product_kernel(mode, count, extra, carried, *refs):
    pieces, w_ref = refs[:count], refs[count]
    refs = refs[count + 1 :]
    if mode == "take":
        sc_ref, refs = refs[0], refs[1:]
    refs = refs[extra:]
    o_ref, refs = refs[0], refs[1:]
    if mode == "make":
        sc_ref, refs = refs[0], refs[1:]
    rows, sems = refs[carried:]
    load(pieces, rows, sems)
    if mode == "make":

        @pl.when(pl.program_id(0) == 0)
        def _():
            step = pick(rows.shape[0], 256)

            def body(i, _):
                part = pl.ds(pl.multiple_of(i * step, step), step)
                x = rows[part, :].astype(F32)
                scale = norm_scale(x)
                sc_ref[part, :] = jnp.broadcast_to(scale, (step, 128))
                return 0

            lax.fori_loop(0, rows.shape[0] // step, body, 0)

    value = nn(rows[...], w_ref[...])
    if mode != "plain":
        value = value * sc_ref[:, 0:1]
    o_ref[...] = value.astype(BF)


def product(pieces, w, start, width, mode="plain", scale=(), deps=(), carry=()):
    length, depth = sum(p.shape[0] for p in pieces), w.shape[0]
    tile = pick(width, 512, 256, start=start)
    by_row = pl.BlockSpec((length, 128), lambda j: (0, 0))
    make = mode == "make"
    return pl.pallas_call(
        functools.partial(product_kernel, mode, len(pieces), len(deps) + len(carry), len(carry)),
        grid=(width // tile,),
        in_specs=[HBM] * len(pieces)
        + [pl.BlockSpec((depth, tile), lambda j: (0, start // tile + j))]
        + [by_row] * len(scale)
        + [HBM] * (len(deps) + len(carry)),
        out_specs=[pl.BlockSpec((length, tile), lambda j: (0, j))] + [by_row] * make + [HBM] * len(carry),
        out_shape=[jax.ShapeDtypeStruct((length, width), BF)]
        + [jax.ShapeDtypeStruct((length, 128), F32)] * make
        + [jax.ShapeDtypeStruct(c.shape, c.dtype) for c in carry],
        input_output_aliases={
            len(pieces) + 1 + len(scale) + len(deps) + i: 1 + make + i for i in range(len(carry))
        },
        scratch_shapes=[pltpu.VMEM((length, depth), BF), pltpu.SemaphoreType.DMA((len(pieces),))],
        compiler_params=pltpu.CompilerParams(vmem_limit_bytes=60 * MIB),
        cost_estimate=cost(2 * length * depth * width + 2e9),
        name="rows_product",
    )(*pieces, w, *scale, *deps, *carry)


def outer_kernel(counts, extra, *refs):
    total = sum(counts)
    groups, start = [], 0
    for count in counts:
        groups.append(refs[start : start + count])
        start += count
    rights = refs[total : total + len(counts)]
    out_ref, rows, sems = refs[total + len(counts) + extra :]
    first = 0
    for m, group in enumerate(groups):
        load(group, rows.at[m], sems.at[pl.ds(first, len(group))])
        first += len(group)
    value = tn(rights[0][...], rows[0])
    for m in range(1, len(counts)):
        value = value + tn(rights[m][...], rows[m])
    out_ref[...] = value.astype(BF).T


def outer(lefts, rights, deps=(), first=0, width=None):
    length = rights[0].shape[0]
    width = width or rights[0].shape[1]
    depth = lefts[0][0].shape[1]
    tile = pick(width, 512, 640, 384, 256, start=first)
    counts = tuple(len(group) for group in lefts)
    flat = [piece for group in lefts for piece in group]
    return pl.pallas_call(
        functools.partial(outer_kernel, counts, len(deps)),
        grid=(width // tile,),
        in_specs=[HBM] * len(flat)
        + [pl.BlockSpec((length, tile), lambda j: (0, first // tile + j))] * len(rights)
        + [HBM] * len(deps),
        out_specs=pl.BlockSpec((depth, tile), lambda j: (0, j)),
        out_shape=jax.ShapeDtypeStruct((depth, width), BF),
        scratch_shapes=[
            pltpu.VMEM((len(lefts), length, depth), BF),
            pltpu.SemaphoreType.DMA((len(flat),)),
        ],
        compiler_params=pltpu.CompilerParams(vmem_limit_bytes=60 * MIB),
        cost_estimate=cost(2 * len(lefts) * length * depth * width),
        name="weight_gradient",
    )(*flat, *rights, *deps)


def partial_kernel(form, layouts, against, extra, carried, *refs):
    number = len(layouts)
    rows = refs[2 * number : 2 * number + against]
    outs = refs[2 * number + against + extra : len(refs) - carried]
    value = None
    for a_ref, w_ref, (size, pitch, start) in zip(refs[:number], refs[number:], layouts):
        for i in range(a_ref.shape[1] // size):
            cols = slice(i * pitch + start, i * pitch + start + size)
            part = nt(a_ref[:, i * size : (i + 1) * size], w_ref[:, cols])
            value = part if value is None else value + part
    if against:
        total, at = 0.0, 0
        for piece in rows:
            size = piece.shape[0]
            total = total + jnp.sum(value[at : at + size] * piece[...].astype(F32), axis=0, keepdims=True)
            at += size
        outs[-1][...] = total
        outs = outs[:-1]
    value = value.astype(BF)
    if form is None:
        outs[0][...] = value
        return
    size = outs[0].shape[0]
    half = size // 2
    blocks = [value[i * size : (i + 1) * size] for i in range(4)]
    if form != "both":
        own, pair, late = outs
        first, second = (1, 2) if form == "x" else (2, 1)
        own[...] = blocks[0]
        pair[:size] = blocks[first]
        pair[size:] = blocks[3]
        late[...] = blocks[second]
        return
    own, send_x, send_y, late_x, late_y = outs
    own[...] = blocks[0]
    send_x[:half] = blocks[1][:half]
    send_x[half:] = blocks[3][:half]
    send_y[:half] = blocks[2][half:]
    send_y[half:] = blocks[3][half:]
    late_x[...] = blocks[1][half:]
    late_y[...] = blocks[2][:half]


def partial_rows(lefts, weights, widths, ats, layouts, form, deps=(), pieces=(), carry=()):
    length = lefts[0].shape[0]
    depth = weights[0].shape[0]
    tile = pick(depth, 512, 256)
    size = length // 4
    heights = {
        None: [length],
        "both": [size, size, size, size // 2, size // 2],
        "x": [size, 2 * size, size],
        "y": [size, 2 * size, size],
    }[form]
    sums = [jax.ShapeDtypeStruct((1, depth), F32)] if pieces else []
    return pl.pallas_call(
        functools.partial(partial_kernel, form, layouts, len(pieces), len(deps) + len(carry), len(carry)),
        grid=(depth // tile,),
        in_specs=[pl.BlockSpec(a.shape, lambda j: (0, 0)) for a in lefts]
        + [pl.BlockSpec((tile, width), lambda j, at=at: (j, at)) for width, at in zip(widths, ats)]
        + [pl.BlockSpec((p.shape[0], tile), lambda j: (0, j)) for p in pieces]
        + [HBM] * (len(deps) + len(carry)),
        out_specs=[pl.BlockSpec((height, tile), lambda j: (0, j)) for height in heights]
        + [pl.BlockSpec((1, tile), lambda j: (0, j))] * len(sums)
        + [HBM] * len(carry),
        out_shape=[jax.ShapeDtypeStruct((height, depth), BF) for height in heights]
        + sums
        + [jax.ShapeDtypeStruct(c.shape, c.dtype) for c in carry],
        input_output_aliases={
            len(lefts) + len(weights) + len(pieces) + len(deps) + i: len(heights) + len(sums) + i
            for i in range(len(carry))
        },
        compiler_params=pltpu.CompilerParams(vmem_limit_bytes=60 * MIB),
        cost_estimate=cost(2 * length * depth * sum(a.shape[1] for a in lefts)),
        name="partial_rows",
    )(*lefts, *weights, *pieces, *deps, *carry)


def ff_kernel(count, count_cot, extra, *refs):
    total = count + count_cot
    pieces, cots = refs[:count], refs[count:total]
    w_ref, d_ref = refs[total : total + 2]
    hid_ref, g_ref, rows, cot, sems = refs[total + 2 + extra :]
    load(pieces, rows, sems.at[pl.ds(0, count)])
    load(cots, cot, sems.at[pl.ds(count, count_cot)])
    tile = d_ref.shape[1]
    length = rows.shape[0]
    step = pick(length, 256)
    c = 0.7978845608028654
    for i in range(length // step):
        part = slice(i * step, (i + 1) * step)
        both = nn(rows[part], w_ref[...])
        grad = nn(cot[part], d_ref[...])
        gate, up = both[:, :tile], both[:, tile:]
        square = gate * gate
        th = jnp.tanh(c * gate * (1.0 + 0.044715 * square))
        half = 0.5 * (1.0 + th)
        value = gate * half
        slope = half + 0.5 * gate * (1.0 - th * th) * (c + 3 * 0.044715 * c * square)
        hid_ref[part] = (value * up).astype(BF)
        g_ref[part, :tile] = (grad * up * slope).astype(BF)
        g_ref[part, tile:] = (grad * value).astype(BF)


def ff_tile(width):
    return pick(width, 256)


def feed_forward(pieces, cots, w, first, number, into=(), deps=()):
    length, depth, width = sum(p.shape[0] for p in pieces), w.shape[0], w.shape[1] // 3
    tile = ff_tile(width)
    count = len(pieces) + len(cots)
    extra = len(deps) + len(into)
    return pl.pallas_call(
        functools.partial(ff_kernel, len(pieces), len(cots), extra),
        grid=(number,),
        in_specs=[HBM] * count
        + [
            pl.BlockSpec((depth, 2 * tile), lambda j: (0, j + first)),
            pl.BlockSpec((depth, tile), lambda j: (0, j + first + 2 * width // tile)),
        ]
        + [HBM] * extra,
        out_specs=[
            pl.BlockSpec((length, tile), lambda j: (0, j + first)),
            pl.BlockSpec((length, 2 * tile), lambda j: (0, j + first)),
        ],
        out_shape=[
            jax.ShapeDtypeStruct((length, width), BF),
            jax.ShapeDtypeStruct((length, 2 * width), BF),
        ],
        input_output_aliases={count + 2 + i: i for i in range(len(into))},
        scratch_shapes=[
            pltpu.VMEM((length, depth), BF),
            pltpu.VMEM((length, depth), BF),
            pltpu.SemaphoreType.DMA((count,)),
        ],
        compiler_params=pltpu.CompilerParams(vmem_limit_bytes=60 * MIB),
        cost_estimate=cost(6 * length * depth * tile * number),
        name="feed_forward",
    )(*pieces, *cots, w, w, *into, *deps)


def hop(part, bit, count, axis="tensor"):
    return lax.ppermute(part, axis, [(i, i ^ bit) for i in range(count)])


class Gather:
    def __init__(self, part, via, count, then=()):
        self.own = part
        self.sent = ()
        if count != 4:
            self.first = self.sent = (lax.all_gather(part, "tensor", axis=0, tiled=True),)
            self.pieces = list(self.first)
            return
        from_x, from_y = hop(part, 1, count), hop(part, 2, count)
        self.first = (from_x, from_y)
        half = part.shape[0] // 2
        self.pieces = [part, from_x, from_y]
        if then:
            from_x, from_y = lax.optimization_barrier((from_x, from_y, *then))[:2]
        if via == "x":
            self.pieces.append(hop(from_y, 1, count))
        elif via == "y":
            self.pieces.append(hop(from_x, 2, count))
        else:
            self.sent = (from_y[:half], from_x[half:])
            self.pieces += [hop(self.sent[0], 1, count), hop(self.sent[1], 2, count)]


def add_kernel(number, carried, *refs):
    ins, outs = refs[: 2 * number], refs[len(refs) - number - carried :][:number]
    for i, out in enumerate(outs):
        out[...] = (ins[2 * i][...].astype(F32) + ins[2 * i + 1][...].astype(F32)).astype(BF)


def add_arrived(pairs, deps, carry):
    depth = pairs[0][0].shape[1]
    tile = pick(depth, 1024)
    specs, args, outs = [], [], []
    for late, arrived in pairs:
        height = late.shape[0]
        specs += [pl.BlockSpec((height, tile), lambda j: (0, j)), pl.BlockSpec((height, tile), lambda j: (1, j))]
        args += [late, arrived]
        outs.append(late)
    return pl.pallas_call(
        functools.partial(add_kernel, len(pairs), len(carry)),
        grid=(depth // tile,),
        in_specs=specs + [HBM] * (len(deps) + len(carry)),
        out_specs=[pl.BlockSpec((o.shape[0], tile), lambda j: (0, j)) for o in outs] + [HBM] * len(carry),
        out_shape=[jax.ShapeDtypeStruct(o.shape, o.dtype) for o in (*outs, *carry)],
        input_output_aliases={len(args) + len(deps) + i: len(outs) + i for i in range(len(carry))},
        compiler_params=pltpu.CompilerParams(vmem_limit_bytes=60 * MIB),
        cost_estimate=cost(1.4e9),
        name="add_arrived",
    )(*args, *deps, *carry)


class Reduce:
    def __init__(self, parts, form, count, then=()):
        if then:
            parts = lax.optimization_barrier((*parts, *then))[: len(parts)]
        self.form, self.count, self.parts = form, count, parts
        if count != 4:
            self.total = lax.psum_scatter(parts[0], "tensor", scatter_dimension=0, tiled=True).astype(F32)
            self.arrived = (self.total,)
        elif form == "both":
            self.arrived = (hop(parts[1], 1, count), hop(parts[2], 2, count))
        else:
            self.arrived = (hop(parts[1], 1 if form == "x" else 2, count),)

    def first(self, deps=(), carry=()):
        if self.count != 4:
            return (self.total, *carry)
        if self.form == "both":
            x_first, y_first = self.arrived
            late = add_arrived([(self.parts[3], y_first), (self.parts[4], x_first)], deps, carry)
            self.second = (hop(late[0], 1, self.count), hop(late[1], 2, self.count))
        else:
            late = add_arrived([(self.parts[2], self.arrived[0])], deps, carry)
            self.second = (hop(late[0], 2 if self.form == "x" else 1, self.count),)
        return tuple(late)

    def settle(self, function, rows, kinds, deps=(), carry=()):
        if self.count != 4:
            return (*function(self.total, *rows), *carry)
        return settle_rows(
            self.form, self.parts[0], self.arrived, self.second, function, rows, kinds, deps, carry
        )


def settle_kernel(form, function, number, extra, kinds, *refs):
    own = refs[0][...].astype(F32)
    if form == "both":
        x_first, y_first, x_second, y_second = refs[1:5]
        refs = refs[5:]
        low = pl.program_id(0) == 0
        total = own + jnp.where(
            low,
            x_first[...].astype(F32) + y_second[...].astype(F32),
            y_first[...].astype(F32) + x_second[...].astype(F32),
        )
    else:
        total = own + refs[1][...].astype(F32) + refs[2][...].astype(F32)
        refs = refs[3:]
    values = function(total, *(ref[...] for ref in refs[:number]))
    for out, kind, value in zip(refs[number + extra :], kinds, values):
        if kind != "sum":
            out[...] = value
            continue

        @pl.when(pl.program_id(0) == 0)
        def _(out=out):
            out[...] = jnp.zeros_like(out)

        out[...] += value


def settle_rows(form, own, arrived, second, function, rows, kinds, deps, carry):
    size, depth = own.shape
    half = size // 2
    block = pl.BlockSpec((half, depth), lambda i: (i, 0))
    top = pl.BlockSpec((half, depth), lambda i: (0, 0))
    others = [top] * 4 if form == "both" else [block] * 2
    out_specs, out_shape = [], []
    for kind in kinds:
        out_specs.append(pl.BlockSpec((1, depth), lambda i: (0, 0)) if kind == "sum" else block)
        out_shape.append(
            jax.ShapeDtypeStruct((1, depth), F32) if kind == "sum" else jax.ShapeDtypeStruct((size, depth), kind)
        )
    return pl.pallas_call(
        functools.partial(settle_kernel, form, function, len(rows), len(deps) + len(carry), kinds),
        grid=(2,),
        in_specs=[block] + others + [block] * len(rows) + [HBM] * (len(deps) + len(carry)),
        out_specs=out_specs + [HBM] * len(carry),
        out_shape=out_shape + [jax.ShapeDtypeStruct(c.shape, c.dtype) for c in carry],
        input_output_aliases={
            1 + len(others) + len(rows) + len(deps) + i: len(kinds) + i for i in range(len(carry))
        },
        compiler_params=pltpu.CompilerParams(vmem_limit_bytes=60 * MIB),
        cost_estimate=cost(3e9),
        name="settle_rows",
    )(own, *arrived, *second, *rows, *deps, *carry)


def bits(count):
    assert count & (count - 1) == 0
    return [1 << i for i in range(count.bit_length() - 1)]


def sum_over(value, axis, count):
    for bit in bits(count):
        value = value + hop(value, bit, count, axis)
    return value


def norm_scale(rows):
    return lax.rsqrt(jnp.mean(rows * rows, axis=-1, keepdims=True) + EPSILON)


def add_branch(total, rows):
    middle = rows.astype(F32) + total
    return middle, (middle * norm_scale(middle)).astype(BF)


def add_last(total, middle):
    return ((middle + total).astype(BF),)


def turn_back(total, middle, cotangent):
    scale = norm_scale(middle)
    inner = jnp.mean(total * middle, axis=-1, keepdims=True)
    grad = cotangent.astype(F32) + scale * total - middle * (scale * scale * scale * inner)
    return grad, grad.astype(BF), jnp.sum(total * middle * scale, axis=0, keepdims=True)


def finish_back(total, rows, grad_middle):
    rows = rows.astype(F32)
    scale = norm_scale(rows)
    inner = jnp.mean(total * rows, axis=-1, keepdims=True)
    grad = grad_middle + total - rows * (scale * scale * inner)
    return (grad.astype(BF),)


def pack_kernel(size, number, turned_count, cuts, extra, *refs):
    weights, gain_ref = refs[:number], refs[number]
    others = refs[number + 1 : number + 1 + turned_count]
    outs = refs[number + 1 + turned_count + extra :]
    gain = gain_ref[...]
    groups = weights[0].shape[1] // size
    at = 0
    for i in range(groups):
        out = outs[i * cuts // groups]
        if i * cuts % groups == 0:
            at = 0
        for weight in weights:
            out[:, at : at + size] = (weight[:, i * size : (i + 1) * size].astype(F32) * gain).astype(BF)
            at += size
    for other in others:
        outs[-1][:, at : at + other.shape[0]] = other[...].T
        at += other.shape[0]


def pack(weights, gain, others, size, cuts, deps=()):
    rows_w, width = weights[0].shape
    widths = [len(weights) * width // cuts] * cuts
    widths[-1] += sum(other.shape[0] for other in others)
    whole = pl.BlockSpec(memory_space=pltpu.VMEM)
    return pl.pallas_call(
        functools.partial(pack_kernel, size, len(weights), len(others), cuts, len(deps)),
        in_specs=[whole] * (len(weights) + 1 + len(others)) + [HBM] * len(deps),
        out_specs=[whole] * cuts,
        out_shape=[jax.ShapeDtypeStruct((rows_w, w), BF) for w in widths],
        compiler_params=pltpu.CompilerParams(vmem_limit_bytes=60 * MIB),
        cost_estimate=cost(2e9),
        name="pack",
    )(*weights, gain, *others, *deps)


def unpack_kernel(groups, pitch, *refs):
    parts, gain_ref, outs = refs[: len(groups)], refs[len(groups)], refs[len(groups) + 1 :]
    at = 0
    for part, number in zip(parts, groups):
        size = part.shape[1] // (number * pitch)
        for i in range(number):
            for k, out in enumerate(outs):
                start = (i * pitch + k) * size
                out[:, at : at + size] = part[:, start : start + size].astype(F32) * gain_ref[...]
            at += size


def turn_kernel(number, *refs):
    for part, out in zip(refs[:number], refs[number:]):
        out[...] = part[...].astype(F32).T


def turned(parts):
    return pl.pallas_call(
        functools.partial(turn_kernel, len(parts)),
        out_shape=[jax.ShapeDtypeStruct(p.shape[::-1], F32) for p in parts],
        compiler_params=pltpu.CompilerParams(vmem_limit_bytes=60 * MIB),
        cost_estimate=cost(2e9),
        name="turned",
    )(*parts)


def unpack(parts, groups, pitch, gain):
    rows_w = gain.shape[0]
    width = sum(p.shape[1] for p in parts) // pitch
    return pl.pallas_call(
        functools.partial(unpack_kernel, groups, pitch),
        out_shape=[jax.ShapeDtypeStruct((rows_w, width), F32)] * pitch,
        compiler_params=pltpu.CompilerParams(vmem_limit_bytes=60 * MIB),
        cost_estimate=cost(2e9),
        name="unpack",
    )(*parts, gain)


def local(
    count_dp,
    count,
    tokens,
    cotangent,
    doc_lengths,
    rel_bucket,
    gain_attn,
    w_query,
    w_key,
    w_value,
    w_out,
    rel_table,
    gain_ff,
    w_gate,
    w_up,
    w_down,
):
    slots = tokens.shape[0]
    length = slots * count
    blocks = length // B
    rows_w, width = w_query.shape
    width_ff = w_gate.shape[1]
    pairs = width // 128
    heads = width // HD
    buckets_local = rel_table.shape[0]
    buckets = buckets_local * count_dp
    docs = doc_lengths.shape[1]
    tile = ff_tile(width_ff)
    me = lax.axis_index("dp").astype(jnp.int32)

    def spread(part):
        return lax.all_gather(part, "dp", axis=0, tiled=True)

    def after(value, *others):
        return lax.optimization_barrier((value, *others))[0]

    xs = [tokens[:, m] for m in range(MICRO)]
    gain_one = gain_attn.astype(F32)[:, None]
    gain_two = gain_ff.astype(F32)[:, None]
    cuts = 2
    each = pairs // cuts
    part_w = each * 384

    halves = pack([w_query, w_key, w_value], gain_one, [w_out], 128, cuts)
    full_qkv = [spread(half) for half in halves]
    full_out, out_at = full_qkv[-1], part_w
    form = "both" if count == 4 else None
    way = ("x", "y") if form else (None, None)

    table = rel_table.reshape(1, buckets_local * heads)
    for bit in bits(count_dp):
        table = jnp.concatenate([table, hop(table, bit, count_dp, "dp")], axis=0)
    table = jnp.take(table, jnp.arange(count_dp, dtype=jnp.int32) ^ me, axis=0).reshape(buckets, heads)
    reverse = jnp.concatenate([jnp.full((1,), -1, jnp.int32), rel_bucket[::-1]])
    onehot = reverse[None, :] == jnp.arange(buckets, dtype=jnp.int32)[:, None]
    offsets = tn(table, onehot.astype(BF)).reshape(heads, 2 * blocks, B)
    tiles = 2 * blocks - 1
    ahead = offsets[:, ::-1]
    bias = bias_strips(jnp.concatenate([ahead[:, :tiles], ahead[:, 1:]], axis=2))

    order = jnp.arange(blocks, dtype=jnp.int32)
    if count == 4:
        order = order ^ lax.axis_index("tensor").astype(jnp.int32)
    positions = (order[:, None] * B + jnp.arange(B, dtype=jnp.int32)[None]).reshape(-1)
    ends = jnp.cumsum(doc_lengths, axis=1)
    lane = jnp.arange(128, dtype=jnp.int32) % HD

    masks = []
    for m in range(MICRO):
        number = jnp.sum((positions[:, None] >= ends[m][None, :]).astype(jnp.int32), axis=1)
        by_block = number.reshape(blocks, B)
        least, most = by_block.min(axis=1), by_block.max(axis=1)
        active = (least[:, None] <= most[None, :]) & (least[None, :] <= most[:, None])
        same = number[:, None] == lane[None, :]
        feat_q = same.astype(BF)
        feat_k = jnp.where(same | (lane >= docs)[None, :], 0.0, -BIG).astype(BF)
        masks.append((feat_q, feat_k, active.astype(jnp.int32).reshape(-1)))
    ones = [Gather(xs[0], "both", count, (bias,))]
    (packed,) = pack([w_gate, w_up], gain_two, [w_down], tile, 1, (bias, *ones[0].sent))
    full_ff = spread(packed)

    def project(m, cut, scale, deps):
        mode = "take" if scale else "make"
        return product(ones[m].pieces, full_qkv[cut], 0, part_w, mode, scale, deps)

    def forward(m, cut, qkv, into, deps):
        feat_q, feat_k, active = masks[m]
        return attend_forward(qkv, feat_q, feat_k, bias, active, order, cut * each, into, deps)

    def out_rows(mixed, deps):
        return partial_rows([mixed], [full_out], [full_out.shape[1]], [0], [(width, width, out_at)], form, deps)

    def ff_rows(left, inner, way, deps, carry=()):
        size = 2 * width_ff if inner else width_ff
        return partial_rows(
            [left], [full_ff], [size], [0 if inner else 2], [(size, size, 0)], way, deps, (), carry
        )

    def qkv_rows(projects, m, deps, carry=()):
        return partial_rows(
            projects, full_qkv, [part_w] * cuts, [0] * cuts, [(part_w, part_w, 0)] * cuts, form, deps, ones[m].pieces, carry
        )

    def scatter(value):
        return lax.psum_scatter(value, "dp", scatter_dimension=0, tiled=True)

    qkv_0a, scale_0 = project(0, 0, (), (packed,))
    ones.append(Gather(after(xs[1], *ones[0].pieces), "x", count, (qkv_0a,)))
    into = forward(0, 0, qkv_0a, (), ())
    cs = [after(cotangent, qkv_0a)[:, m] for m in range(MICRO)]
    (qkv_0b,) = project(0, 1, (scale_0,), (into[0], *ones[1].first))
    cots = [Gather(cs[0], "y", count, (qkv_0b,))]
    mixed_0, lse_0 = forward(0, 1, qkv_0b, into, ())
    parts = out_rows(mixed_0, (*ones[1].pieces, *cots[0].first))
    sum_0 = Reduce(parts, form, count)
    cots.append(Gather(after(cs[1], qkv_0b), "x", count, (parts[0],)))
    qkv_1a, scale_1 = project(1, 0, (), (parts[0],))
    into = forward(1, 0, qkv_1a, (), tuple(cots[0].pieces))
    late = sum_0.first((into[0], *cots[1].first))
    (qkv_1b,) = project(1, 1, (scale_1,), (late[0],))
    middle_0, normed = sum_0.settle(add_branch, [xs[0]], (F32, BF), (qkv_1b,))
    twos = [Gather(normed, "both", count)]
    mixed_1, lse_1 = forward(1, 1, qkv_1b, into, (normed, *cots[1].pieces))
    parts = out_rows(mixed_1, twos[0].sent)
    sum_1 = Reduce(parts, form, count)
    late = sum_1.first((parts[0], *twos[0].pieces))

    steps = width_ff // tile
    early = (steps + 1) // 2
    hidden_0, grad_ff_0 = feed_forward(twos[0].pieces, cots[0].pieces, full_ff, 0, steps, (), (late[0],))
    middle_1, normed = sum_1.settle(add_branch, [xs[1]], (F32, BF), (hidden_0,))
    twos.append(Gather(normed, "both", count))
    parts = ff_rows(grad_ff_0, True, form, (normed,))
    sum_0 = Reduce(parts, form, count, twos[1].pieces)
    down = ff_rows(hidden_0, False, way[0], (parts[0], *twos[1].sent))
    hidden_1, grad_ff_1 = feed_forward(
        twos[1].pieces, cots[1].pieces, full_ff, 0, steps, (), (down[0],)
    )
    late = sum_0.first((hidden_1,))
    weight = outer([c.pieces for c in cots], [hidden_0, hidden_1], (late[0],))
    grad_middle_0, rounded, gain_two_0, weight = sum_0.settle(
        turn_back, [middle_0, cs[0]], (F32, BF, "sum"), (), (weight,)
    )
    grad_down = scatter(weight)
    mids = [Gather(rounded, "both", count)]
    parts = ff_rows(grad_ff_1, True, form, (rounded,))
    sum_1 = Reduce(parts, form, count)
    two_pieces, grad_ffs = [g.pieces for g in twos], [grad_ff_0, grad_ff_1]
    ff_half = early * 2 * tile
    weight = outer(two_pieces, grad_ffs, (parts[0], *mids[0].sent), 0, ff_half)
    late = sum_1.first(tuple(mids[0].pieces), (weight,))
    grad_ff_a = scatter(late[-1])

    def backward(m, qkv, lse, mixed, grad, scale, cut, into, deps):
        feat_q, feat_k, active = masks[m]
        return attend_backward(
            qkv, feat_q, feat_k, bias, lse, mixed, grad, scale, active, order, cut * each, into, deps
        )

    (grad,) = product(mids[0].pieces, full_out, out_at, width, deps=(late[0],))
    weight = outer(two_pieces, grad_ffs, (grad,), ff_half, 2 * width_ff - ff_half)
    grad_middle_1, rounded, gain_two_1, weight = sum_1.settle(
        turn_back, [middle_1, cs[1]], (F32, BF, "sum"), (), (weight,)
    )
    grad_ff_b = scatter(weight)
    mids.append(Gather(rounded, "both", count))
    grad_0a, fold = backward(0, qkv_0a, lse_0, mixed_0, grad, scale_0, 0, (), (rounded,))
    down_0 = Reduce(down, way[0], count, mids[1].first)
    grad_0b, fold_0 = backward(0, qkv_0b, lse_0, mixed_0, grad, scale_0, 1, (fold,), mids[1].sent)
    *parts, gain_one_0 = qkv_rows([grad_0a, grad_0b], 0, (grad_down,))
    sum_0 = Reduce(parts, form, count)
    (grad,) = product(mids[1].pieces, full_out, out_at, width, deps=(parts[0],))
    late = down_0.first((grad,))
    weight = outer([g.pieces for g in mids], [mixed_0, mixed_1], (late[0], grad_ff_a))
    late = sum_0.first((), (weight,))
    grad_out = scatter(late[-1])
    grad_1a, fold = backward(1, qkv_1a, lse_1, mixed_1, grad, scale_1, 0, (), (late[0],))
    (output_0,) = down_0.settle(add_last, [middle_0], (BF,), (grad_1a,))
    weight = outer([g.pieces for g in ones], [grad_0a, grad_1a], (output_0,))
    token_0, weight = sum_0.settle(finish_back, [xs[0], grad_middle_0], (BF,), (), (weight,))
    grad_qkv_a = scatter(weight)
    parts = ff_rows(hidden_1, False, form, (token_0,))
    down_1 = Reduce(parts, form, count)
    grad_1b, fold_1 = backward(1, qkv_1b, lse_1, mixed_1, grad, scale_1, 1, (fold,), (parts[0], grad_ff_b))
    late = down_1.first((grad_1b,))
    weight = outer([g.pieces for g in ones], [grad_0b, grad_1b], (late[0], grad_out))
    *parts, gain_one_1, weight = qkv_rows([grad_1a, grad_1b], 1, down_1.arrived, (weight,))
    grad_qkv_b = scatter(weight)
    sum_1 = Reduce(parts, form, count)
    (output_1,) = down_1.settle(add_last, [middle_1], (BF,), (parts[0],))
    late = sum_1.first((output_1,))
    grad_gate, grad_up = unpack(
        [grad_ff_a, grad_ff_b], (early, steps - early), 2, gain_two
    )
    grad_out, grad_down = turned([grad_out, grad_down])

    fold = (fold_0 + fold_1).reshape(heads, 2 * blocks, B)[:, ::-1]
    before = jnp.concatenate([jnp.zeros((heads, 1, B), F32), fold[:, :-1]], axis=1)
    by_offset = jnp.where(jnp.arange(B) == 0, before, fold).reshape(heads, 2 * length)
    grad_table = lax.dot_general(
        onehot.astype(F32), by_offset, (((1,), (1,)), ((), ())), precision=lax.Precision.HIGHEST
    )
    small = jnp.concatenate(
        [
            (gain_one_0 + gain_one_1).reshape(count_dp, rows_w),
            (gain_two_0 + gain_two_1).reshape(count_dp, rows_w),
            grad_table.reshape(count_dp, buckets_local * heads),
        ],
        axis=1,
    )
    small = lax.dynamic_index_in_dim(sum_over(small, "dp", count_dp), me, 0, keepdims=False)
    both_gains = sum_over(small[: 2 * rows_w], "tensor", count)
    (token_1,) = sum_1.settle(
        finish_back,
        [xs[1], grad_middle_1],
        (BF,),
        (late[0], grad_qkv_a, grad_gate, grad_out, grad_down, both_gains),
    )
    return (
        jnp.stack([output_0, output_1], axis=1),
        jnp.stack([token_0, token_1], axis=1),
        both_gains[:rows_w] / gain_one[:, 0],
        *unpack([grad_qkv_a, grad_qkv_b], (each, each), 3, gain_one),
        grad_out,
        small[2 * rows_w :].reshape(buckets_local, heads),
        both_gains[rows_w:] / gain_two[:, 0],
        grad_gate,
        grad_up,
        grad_down,
    )


def solution(mesh):
    row, col = P("dp", "tensor"), P("tensor", "dp")
    acts = P("tensor", "dp", None)
    in_specs = (
        acts, acts, P("dp", None), P(), P("dp"), row, row, row, col, row, P("dp"), row, row, col
    )
    out_specs = (acts, acts, P("dp"), row, row, row, col, row, P("dp"), row, row, col)
    body = functools.partial(local, mesh.shape["dp"], mesh.shape["tensor"])
    return jax.shard_map(body, mesh=mesh, in_specs=in_specs, out_specs=out_specs, check_vma=False)
```

```python
import functools
import jax
import jax.numpy as jnp
from jax import lax
from jax.experimental import pallas as pl
from jax.experimental.pallas import tpu as pltpu
from jax.sharding import PartitionSpec as P

HD=64
B=256
BIG=1e30
F32=jnp.float32; BF=jnp.bfloat16

def nt(a,b): return lax.dot_general(a,b,(((1,),(1,)),((),())),preferred_element_type=F32)
def nn(a,b): return lax.dot_general(a,b,(((1,),(0,)),((),())),preferred_element_type=F32)


EPSILON = 1e-06
MICRO = 2
HBM = pl.BlockSpec(memory_space=pltpu.HBM)
MIB = 1 << 20


def cost(flops):
    return pl.CostEstimate(flops=int(2 * flops), bytes_accessed=1, transcendentals=0)


def tn(left, right):
    return lax.dot_general(left, right, (((0,), (0,)), ((), ())), preferred_element_type=F32)


def pick(size, *tiles, start=0):
    return next(tile for tile in (*tiles, 128, size) if size % tile == 0 and start % tile == 0)


def strips_kernel(w_ref, out_ref):
    def body(i, _):
        wide = jnp.broadcast_to(w_ref[0, pl.ds(i, 1), :], (B, 2 * B))
        rolled = pltpu.roll(wide, 0, 1, stride=1, stride_axis=0)
        out_ref[0, pl.ds(pl.multiple_of(i * B, B), B), :] = rolled[:, :B]
        return 0

    lax.fori_loop(0, w_ref.shape[1], body, 0)


def bias_strips(w):
    heads, tiles, _ = w.shape
    return pl.pallas_call(
        strips_kernel,
        grid=(heads,),
        in_specs=[pl.BlockSpec((1, tiles, 2 * B), lambda h: (h, 0, 0))],
        out_specs=pl.BlockSpec((1, tiles * B, B), lambda h: (h, 0, 0)),
        out_shape=jax.ShapeDtypeStruct((heads, tiles * B, B), F32),
        compiler_params=pltpu.CompilerParams(vmem_limit_bytes=60 * MIB),
        cost_estimate=cost(6e9),
        name="bias_strips",
    )(w)


def by_tile(act_ref, base, n, *functions):
    count = act_ref[base]
    for i in range(1, n):
        count = count + act_ref[base + i]
    most = count * 4 >= 3 * n

    @pl.when(most)
    def _():
        for function in functions:
            for i in range(n):
                function(i)

    @pl.when(jnp.logical_not(most))
    def _():
        for function in functions:

            def step(i, _, function=function):
                @pl.when(act_ref[base + i] != 0)
                def _():
                    function(i)

                return 0

            lax.fori_loop(0, n, step, 0)


def attend_forward_kernel(n, extra, *refs):
    act_ref, blk_ref, qkv_ref, fq_ref, fk_ref, bias_ref = refs[:6]
    o_ref, lse_ref, qx, kx, vx, s_scr, m_scr, o_scr = refs[6 + extra :]
    lane = lax.broadcasted_iota(jnp.int32, (1, 128), 1)
    q, k, v = qkv_ref[:, 0:128], qkv_ref[:, 128:256], qkv_ref[:, 256:384]
    vt = v.T
    for h in range(2):
        own = (lane < HD) if h == 0 else (lane >= HD)
        qx[h] = jnp.where(own, q, fq_ref[...]).T
        kx[h] = jnp.where(own, k, fk_ref[...])
        vx[h] = jnp.concatenate([vt[h * HD : (h + 1) * HD], jnp.ones((16, vt.shape[1]), BF)], axis=0)

    def row(qi, _):
        qs = pl.ds(pl.multiple_of(qi * B, B), B)
        m_scr[...] = jnp.full_like(m_scr, -3e38)
        o_scr[...] = jnp.zeros_like(o_scr)

        def score(kb):
            ks = pl.ds(pl.multiple_of(kb * B, B), B)
            bs = pl.ds(pl.multiple_of((blk_ref[kb] - blk_ref[qi] + n - 1) * B, B), B)
            for h in range(2):
                s = nn(kx[h, ks, :], qx[h, :, qs]) + bias_ref[h, bs, :]
                s_scr[h, ks, :] = s
                m_scr[h] = jnp.maximum(m_scr[h], jnp.max(s.reshape(B // 8, 8, B), axis=0))

        def share(kb):
            ks = pl.ds(pl.multiple_of(kb * B, B), B)
            for h in range(2):
                p = jnp.exp(s_scr[h, ks, :] - jnp.max(m_scr[h], axis=0, keepdims=True)).astype(BF)
                o_scr[h] += nn(vx[h, :, ks], p)

        by_tile(act_ref, qi * n, n, score, share)
        peaks = [jnp.max(m_scr[h], axis=0, keepdims=True) for h in range(2)]
        outs = []
        for h in range(2):
            total = o_scr[h, HD : HD + 1, :]
            outs.append(o_scr[h, 0:HD, :] / total)
            lse_ref[0, pl.ds(h, 1), qs] = peaks[h] + jnp.log(total)
        o_ref[qs, :] = jnp.concatenate(outs, axis=0).T.astype(BF)
        return 0

    lax.fori_loop(0, n, row, 0)


def attend_forward(qkv, feat_q, feat_k, bias, active, order, first, into=(), deps=()):
    length, width3 = qkv.shape
    n, number, pairs = length // B, width3 // 384, bias.shape[0] // 2
    rows = (2 * n - 1) * B
    extra = len(into) + len(deps)
    whole = pl.BlockSpec((length, 128), lambda p, *_: (0, 0))
    return pl.pallas_call(
        functools.partial(attend_forward_kernel, n, extra),
        grid_spec=pltpu.PrefetchScalarGridSpec(
            num_scalar_prefetch=2,
            grid=(number,),
            in_specs=[
                pl.BlockSpec((length, 384), lambda p, *_: (0, p)),
                whole,
                whole,
                pl.BlockSpec((2, rows, B), lambda p, *_: (p + first, 0, 0)),
            ]
            + [HBM] * extra,
            out_specs=[
                pl.BlockSpec((length, 128), lambda p, *_: (0, p + first)),
                pl.BlockSpec((1, 2, length), lambda p, *_: (p + first, 0, 0)),
            ],
            scratch_shapes=[
                pltpu.VMEM((2, 128, length), BF),
                pltpu.VMEM((2, length, 128), BF),
                pltpu.VMEM((2, HD + 16, length), BF),
                pltpu.VMEM((2, length, B), F32),
                pltpu.VMEM((2, 8, B), F32),
                pltpu.VMEM((2, HD + 16, B), F32),
            ],
        ),
        out_shape=[
            jax.ShapeDtypeStruct((length, pairs * 128), BF),
            jax.ShapeDtypeStruct((pairs, 2, length), F32),
        ],
        input_output_aliases={6 + i: i for i in range(len(into))},
        compiler_params=pltpu.CompilerParams(vmem_limit_bytes=60 * MIB),
        cost_estimate=cost(3.7e9 * number),
        name="attend_forward",
    )(active, order, qkv, feat_q, feat_k, bias, *into, *deps)


def attend_backward_kernel(n, extra, *refs):
    act_ref, blk_ref, qkv_ref, fq_ref, fk_ref, bias_ref, lse_ref, o_ref, do_ref, sc_ref = refs[:10]
    g_ref, fold_ref, qx, kx, v0, kt, delta, dk, dv, dqt, diag, p_scr, ds_scr, dot_ = refs[10 + extra :]
    lane = lax.broadcasted_iota(jnp.int32, (1, 128), 1)
    q, k, v = qkv_ref[:, 0:128], qkv_ref[:, 128:256], qkv_ref[:, 256:384]
    for h in range(2):
        own = (lane < HD) if h == 0 else (lane >= HD)
        qx[h] = jnp.where(own, q, fq_ref[...]).T
        kx[h] = jnp.where(own, k, fk_ref[...])
        v0[h] = jnp.where(own, v, jnp.zeros_like(v))
    kt[...] = k.T
    dot_[...] = do_ref[...].T
    prod = (o_ref[...].astype(F32) * do_ref[...].astype(F32)).T
    for h in range(2):
        delta[h : h + 1, :] = jnp.sum(prod[h * HD : (h + 1) * HD], axis=0, keepdims=True)
    diag[...] = jnp.zeros_like(diag)
    dqt[...] = jnp.zeros_like(dqt)

    def column(kb, _):
        ks = pl.ds(pl.multiple_of(kb * B, B), B)

        def tile(qi):
            qs = pl.ds(pl.multiple_of(qi * B, B), B)
            bs = pl.ds(pl.multiple_of((blk_ref[kb] - blk_ref[qi] + n - 1) * B, B), B)
            for h in range(2):
                s = nn(kx[h, ks, :], qx[h, :, qs]) + bias_ref[h, bs, :]
                dp = nn(v0[h, ks, :], dot_[:, qs])
                p = jnp.exp(s - lse_ref[0, pl.ds(h, 1), qs])
                ds = p * (dp - delta[pl.ds(h, 1), qs])
                p_scr[h, :, qs] = p.astype(BF)
                ds_scr[h, :, qs] = ds.astype(BF)
                diag[h, bs, :] += ds

        count = act_ref[kb * n]
        for i in range(1, n):
            count = count + act_ref[kb * n + i]

        @pl.when(count * 4 < 3 * n)
        def _():
            p_scr[...] = jnp.zeros_like(p_scr)
            ds_scr[...] = jnp.zeros_like(ds_scr)

        by_tile(act_ref, kb * n, n, tile)
        for h in range(2):
            dv[h, ks, :] = nn(p_scr[h], do_ref[...])
            dk[h, ks, :] = nn(ds_scr[h], qkv_ref[:, 0:128])
            dqt[h * HD : (h + 1) * HD, :] += nn(kt[h * HD : (h + 1) * HD, ks], ds_scr[h])
        return 0

    lax.fori_loop(0, n, column, 0)
    g_ref[:, 0:128] = (dqt[...].T * sc_ref[...]).astype(BF)
    left = lane < HD
    g_ref[:, 128:256] = (jnp.where(left, dk[0], dk[1]) * sc_ref[...]).astype(BF)
    g_ref[:, 256:384] = (jnp.where(left, dv[0], dv[1]) * sc_ref[...]).astype(BF)
    row = lax.broadcasted_iota(jnp.int32, (B, B), 0)
    below = row >= lax.broadcasted_iota(jnp.int32, (B, B), 1)
    half = B // 2
    flip = lax.broadcasted_iota(jnp.int32, (half, half), 0) + lax.broadcasted_iota(jnp.int32, (half, half), 1)
    flip = (flip == half - 1).astype(BF)
    for h in range(2):
        for j in range(2 * n):
            low = diag[h, (j - 1) * B : j * B, :] if j > 0 else 0.0
            high = diag[h, j * B : (j + 1) * B, :] if j < 2 * n - 1 else 0.0
            part = jnp.where(below, low, high)
            part = part[:half] + jnp.concatenate([part[half:, half:], part[half:, :half]], axis=1)
            part = pltpu.roll(nn(flip, part.astype(BF)), half + 1, 1, stride=1, stride_axis=0)
            fold_ref[0, h, j : j + 1, :] = jnp.sum(part, axis=0, keepdims=True)


def attend_backward(
    qkv, feat_q, feat_k, bias, lse, mixed, grad, scale, active, order, first, into=(), deps=()
):
    length, width3 = qkv.shape
    n, number, pairs = length // B, width3 // 384, bias.shape[0] // 2
    tiles = 2 * n - 1
    rows = tiles * B
    extra = len(into) + len(deps)
    whole = pl.BlockSpec((length, 128), lambda p, *_: (0, 0))
    one = pl.BlockSpec((length, 128), lambda p, *_: (0, p + first))
    three = pl.BlockSpec((length, 384), lambda p, *_: (0, p))
    return pl.pallas_call(
        functools.partial(attend_backward_kernel, n, extra),
        grid_spec=pltpu.PrefetchScalarGridSpec(
            num_scalar_prefetch=2,
            grid=(number,),
            in_specs=[
                three,
                whole,
                whole,
                pl.BlockSpec((2, rows, B), lambda p, *_: (p + first, 0, 0)),
                pl.BlockSpec((1, 2, length), lambda p, *_: (p + first, 0, 0)),
                one,
                one,
                whole,
            ]
            + [HBM] * extra,
            out_specs=[three, pl.BlockSpec((1, 2, 2 * n, B), lambda p, *_: (p + first, 0, 0, 0))],
            scratch_shapes=[
                pltpu.VMEM((2, 128, length), BF),
                pltpu.VMEM((2, length, 128), BF),
                pltpu.VMEM((2, length, 128), BF),
                pltpu.VMEM((128, length), BF),
                pltpu.VMEM((2, length), F32),
                pltpu.VMEM((2, length, 128), F32),
                pltpu.VMEM((2, length, 128), F32),
                pltpu.VMEM((2 * HD, length), F32),
                pltpu.VMEM((2, rows, B), F32),
                pltpu.VMEM((2, B, length), BF),
                pltpu.VMEM((2, B, length), BF),
                pltpu.VMEM((128, length), BF),
            ],
        ),
        out_shape=[
            jax.ShapeDtypeStruct((length, width3), BF),
            jax.ShapeDtypeStruct((pairs, 2, 2 * n, B), F32),
        ],
        input_output_aliases={10: 1} if into else {},
        compiler_params=pltpu.CompilerParams(vmem_limit_bytes=60 * MIB),
        cost_estimate=cost(6.5e9 * number),
        name="attend_backward",
    )(active, order, qkv, feat_q, feat_k, bias, lse, mixed, grad, scale, *into, *deps)


def load(pieces, rows, sems):
    copies, start = [], 0
    for i, piece in enumerate(pieces):
        size = piece.shape[0]
        copies.append((start, pltpu.make_async_copy(piece, rows.at[pl.ds(start, size)], sems.at[i])))
        start += size
    first = pl.program_id(0) == 0

    @pl.when(first)
    def _():
        for _, copy in copies:
            copy.start()

    def ready(end):
        due = [copy for at, copy in copies if at < end]
        del copies[: len(due)]
        if due:

            @pl.when(first)
            def _():
                for copy in due:
                    copy.wait()

    return ready


def product_kernel(mode, count, extra, carried, *refs):
    pieces, w_ref = refs[:count], refs[count]
    refs = refs[count + 1 :]
    if mode == "take":
        sc_ref, refs = refs[0], refs[1:]
    refs = refs[extra:]
    o_ref, refs = refs[0], refs[1:]
    if mode == "make":
        sc_ref, refs = refs[0], refs[1:]
    rows, sems = refs[carried:]
    load(pieces, rows, sems)(rows.shape[0])
    if mode == "make":

        @pl.when(pl.program_id(0) == 0)
        def _():
            step = pick(rows.shape[0], 256)

            def body(i, _):
                part = pl.ds(pl.multiple_of(i * step, step), step)
                x = rows[part, :].astype(F32)
                scale = norm_scale(x)
                sc_ref[part, :] = jnp.broadcast_to(scale, (step, 128))
                return 0

            lax.fori_loop(0, rows.shape[0] // step, body, 0)

    value = nn(rows[...], w_ref[...])
    if mode != "plain":
        value = value * sc_ref[:, 0:1]
    o_ref[...] = value.astype(BF)


def product(pieces, w, start, width, mode="plain", scale=(), deps=(), carry=()):
    length, depth = sum(p.shape[0] for p in pieces), w.shape[0]
    tile = pick(width, 512, 256, start=start)
    by_row = pl.BlockSpec((length, 128), lambda j: (0, 0))
    make = mode == "make"
    return pl.pallas_call(
        functools.partial(product_kernel, mode, len(pieces), len(deps) + len(carry), len(carry)),
        grid=(width // tile,),
        in_specs=[HBM] * len(pieces)
        + [pl.BlockSpec((depth, tile), lambda j: (0, start // tile + j))]
        + [by_row] * len(scale)
        + [HBM] * (len(deps) + len(carry)),
        out_specs=[pl.BlockSpec((length, tile), lambda j: (0, j))] + [by_row] * make + [HBM] * len(carry),
        out_shape=[jax.ShapeDtypeStruct((length, width), BF)]
        + [jax.ShapeDtypeStruct((length, 128), F32)] * make
        + [jax.ShapeDtypeStruct(c.shape, c.dtype) for c in carry],
        input_output_aliases={
            len(pieces) + 1 + len(scale) + len(deps) + i: 1 + make + i for i in range(len(carry))
        },
        scratch_shapes=[pltpu.VMEM((length, depth), BF), pltpu.SemaphoreType.DMA((len(pieces),))],
        compiler_params=pltpu.CompilerParams(vmem_limit_bytes=60 * MIB),
        cost_estimate=cost(2 * length * depth * width + 2e9),
        name="rows_product",
    )(*pieces, w, *scale, *deps, *carry)


def outer_kernel(counts, based, extra, *refs):
    total = sum(counts)
    groups, start = [], 0
    for count in counts:
        groups.append(refs[start : start + count])
        start += count
    rights = refs[total : total + len(counts)]
    out_ref, rows, sems = refs[total + len(counts) + based + extra :]
    first = 0
    loads = []
    for m, group in enumerate(groups):
        loads.append(load(group, rows.at[m], sems.at[pl.ds(first, len(group))]))
        first += len(group)
    value = 0.0
    for m, ready in enumerate(loads):
        ready(rows.shape[1])
        value = value + tn(rights[m][...], rows[m])
    value = value.astype(BF).T
    if based:
        value = (value.astype(F32) + refs[total + len(counts)][...].astype(F32)).astype(BF)
    out_ref[...] = value


def outer(lefts, rights, deps=(), first=0, width=None, base=()):
    length = rights[0].shape[0]
    width = width or rights[0].shape[1]
    depth = lefts[0][0].shape[1]
    tile = pick(width, 512, 640, 384, 256, start=first)
    counts = tuple(len(group) for group in lefts)
    flat = [piece for group in lefts for piece in group]
    return pl.pallas_call(
        functools.partial(outer_kernel, counts, len(base), len(deps)),
        grid=(width // tile,),
        in_specs=[HBM] * len(flat)
        + [pl.BlockSpec((length, tile), lambda j: (0, first // tile + j))] * len(rights)
        + [pl.BlockSpec((depth, tile), lambda j: (0, j))] * len(base)
        + [HBM] * len(deps),
        out_specs=pl.BlockSpec((depth, tile), lambda j: (0, j)),
        out_shape=jax.ShapeDtypeStruct((depth, width), BF),
        scratch_shapes=[
            pltpu.VMEM((len(lefts), length, depth), BF),
            pltpu.SemaphoreType.DMA((len(flat),)),
        ],
        compiler_params=pltpu.CompilerParams(vmem_limit_bytes=60 * MIB),
        cost_estimate=cost(2 * len(lefts) * length * depth * width),
        name="weight_gradient",
    )(*flat, *rights, *base, *deps)


def partial_kernel(form, layouts, against, extra, carried, *refs):
    number = len(layouts)
    rows = refs[2 * number : 2 * number + against]
    outs = refs[2 * number + against + extra : len(refs) - carried]
    value = None
    for a_ref, w_ref, (size, pitch, start) in zip(refs[:number], refs[number:], layouts):
        for i in range(a_ref.shape[1] // size):
            cols = slice(i * pitch + start, i * pitch + start + size)
            part = nt(a_ref[:, i * size : (i + 1) * size], w_ref[:, cols])
            value = part if value is None else value + part
    if against:
        total, at = 0.0, 0
        for piece in rows:
            size = piece.shape[0]
            total = total + jnp.sum(value[at : at + size] * piece[...].astype(F32), axis=0, keepdims=True)
            at += size
        outs[-1][...] = total
        outs = outs[:-1]
    value = value.astype(BF)
    if form is None:
        outs[0][...] = value
        return
    size = outs[0].shape[0]
    half = size // 2
    blocks = [value[i * size : (i + 1) * size] for i in range(4)]
    if form != "both":
        own, pair, late = outs
        first, second = (1, 2) if form == "x" else (2, 1)
        own[...] = blocks[0]
        pair[:size] = blocks[first]
        pair[size:] = blocks[3]
        late[...] = blocks[second]
        return
    own, send_x, send_y, late_x, late_y = outs
    own[...] = blocks[0]
    send_x[:half] = blocks[1][:half]
    send_x[half:] = blocks[3][:half]
    send_y[:half] = blocks[2][half:]
    send_y[half:] = blocks[3][half:]
    late_x[...] = blocks[1][half:]
    late_y[...] = blocks[2][:half]


def partial_rows(lefts, weights, widths, ats, layouts, form, deps=(), pieces=(), carry=()):
    length = lefts[0].shape[0]
    depth = weights[0].shape[0]
    tile = pick(depth, 512, 256)
    size = length // 4
    heights = {
        None: [length],
        "both": [size, size, size, size // 2, size // 2],
        "x": [size, 2 * size, size],
        "y": [size, 2 * size, size],
    }[form]
    sums = [jax.ShapeDtypeStruct((1, depth), F32)] if pieces else []
    return pl.pallas_call(
        functools.partial(partial_kernel, form, layouts, len(pieces), len(deps) + len(carry), len(carry)),
        grid=(depth // tile,),
        in_specs=[pl.BlockSpec(a.shape, lambda j: (0, 0)) for a in lefts]
        + [pl.BlockSpec((tile, width), lambda j, at=at: (j, at)) for width, at in zip(widths, ats)]
        + [pl.BlockSpec((p.shape[0], tile), lambda j: (0, j)) for p in pieces]
        + [HBM] * (len(deps) + len(carry)),
        out_specs=[pl.BlockSpec((height, tile), lambda j: (0, j)) for height in heights]
        + [pl.BlockSpec((1, tile), lambda j: (0, j))] * len(sums)
        + [HBM] * len(carry),
        out_shape=[jax.ShapeDtypeStruct((height, depth), BF) for height in heights]
        + sums
        + [jax.ShapeDtypeStruct(c.shape, c.dtype) for c in carry],
        input_output_aliases={
            len(lefts) + len(weights) + len(pieces) + len(deps) + i: len(heights) + len(sums) + i
            for i in range(len(carry))
        },
        compiler_params=pltpu.CompilerParams(vmem_limit_bytes=60 * MIB),
        cost_estimate=cost(2 * length * depth * sum(a.shape[1] for a in lefts)),
        name="partial_rows",
    )(*lefts, *weights, *pieces, *deps, *carry)


def ff_kernel(count, count_cot, extra, *refs):
    total = count + count_cot
    pieces, cots = refs[:count], refs[count:total]
    w_ref, d_ref = refs[total : total + 2]
    hid_ref, g_ref, rows, cot, sems = refs[total + 2 + extra :]
    ready = load(pieces, rows, sems.at[pl.ds(0, count)])
    load(cots, cot, sems.at[pl.ds(count, count_cot)])(cot.shape[0])
    ready(rows.shape[0])
    tile = d_ref.shape[1]
    length = rows.shape[0]
    step = pick(length, 256)
    c = 0.7978845608028654
    for i in range(length // step):
        part = slice(i * step, (i + 1) * step)
        both = nn(rows[part], w_ref[...])
        grad = nn(cot[part], d_ref[...])
        gate, up = both[:, :tile], both[:, tile:]
        square = gate * gate
        th = jnp.tanh(c * gate * (1.0 + 0.044715 * square))
        half = 0.5 * (1.0 + th)
        value = gate * half
        slope = half + 0.5 * gate * (1.0 - th * th) * (c + 3 * 0.044715 * c * square)
        hid_ref[part] = (value * up).astype(BF)
        g_ref[part, :tile] = (grad * up * slope).astype(BF)
        g_ref[part, tile:] = (grad * value).astype(BF)


def ff_tile(width):
    return pick(width, 256)


def feed_forward(pieces, cots, w, first, number, into=(), deps=()):
    length, depth, width = sum(p.shape[0] for p in pieces), w.shape[0], w.shape[1] // 3
    tile = ff_tile(width)
    count = len(pieces) + len(cots)
    extra = len(deps) + len(into)
    return pl.pallas_call(
        functools.partial(ff_kernel, len(pieces), len(cots), extra),
        grid=(number,),
        in_specs=[HBM] * count
        + [
            pl.BlockSpec((depth, 2 * tile), lambda j: (0, j + first)),
            pl.BlockSpec((depth, tile), lambda j: (0, j + first + 2 * width // tile)),
        ]
        + [HBM] * extra,
        out_specs=[
            pl.BlockSpec((length, tile), lambda j: (0, j + first)),
            pl.BlockSpec((length, 2 * tile), lambda j: (0, j + first)),
        ],
        out_shape=[
            jax.ShapeDtypeStruct((length, width), BF),
            jax.ShapeDtypeStruct((length, 2 * width), BF),
        ],
        input_output_aliases={count + 2 + i: i for i in range(len(into))},
        scratch_shapes=[
            pltpu.VMEM((length, depth), BF),
            pltpu.VMEM((length, depth), BF),
            pltpu.SemaphoreType.DMA((count,)),
        ],
        compiler_params=pltpu.CompilerParams(vmem_limit_bytes=60 * MIB),
        cost_estimate=cost(6 * length * depth * tile * number),
        name="feed_forward",
    )(*pieces, *cots, w, w, *into, *deps)


def hop(part, bit, count, axis="tensor"):
    return lax.ppermute(part, axis, [(i, i ^ bit) for i in range(count)])


class Gather:
    def __init__(self, part, via, count, then=()):
        self.own = part
        self.sent = ()
        if count != 4:
            self.first = self.sent = (lax.all_gather(part, "tensor", axis=0, tiled=True),)
            self.pieces = list(self.first)
            return
        from_x, from_y = hop(part, 1, count), hop(part, 2, count)
        self.first = (from_x, from_y)
        half = part.shape[0] // 2
        self.pieces = [part, from_x, from_y]
        if then:
            from_x, from_y = lax.optimization_barrier((from_x, from_y, *then))[:2]
        if via == "x":
            self.pieces.append(hop(from_y, 1, count))
        elif via == "y":
            self.pieces.append(hop(from_x, 2, count))
        else:
            self.sent = (from_y[:half], from_x[half:])
            self.pieces += [hop(self.sent[0], 1, count), hop(self.sent[1], 2, count)]


def add_kernel(number, carried, *refs):
    ins, outs = refs[: 2 * number], refs[len(refs) - number - carried :][:number]
    for i, out in enumerate(outs):
        out[...] = (ins[2 * i][...].astype(F32) + ins[2 * i + 1][...].astype(F32)).astype(BF)


def add_arrived(pairs, deps, carry):
    depth = pairs[0][0].shape[1]
    tile = pick(depth, 1024)
    specs, args, outs = [], [], []
    for late, arrived in pairs:
        height = late.shape[0]
        specs += [pl.BlockSpec((height, tile), lambda j: (0, j)), pl.BlockSpec((height, tile), lambda j: (1, j))]
        args += [late, arrived]
        outs.append(late)
    return pl.pallas_call(
        functools.partial(add_kernel, len(pairs), len(carry)),
        grid=(depth // tile,),
        in_specs=specs + [HBM] * (len(deps) + len(carry)),
        out_specs=[pl.BlockSpec((o.shape[0], tile), lambda j: (0, j)) for o in outs] + [HBM] * len(carry),
        out_shape=[jax.ShapeDtypeStruct(o.shape, o.dtype) for o in (*outs, *carry)],
        input_output_aliases={len(args) + len(deps) + i: len(outs) + i for i in range(len(carry))},
        compiler_params=pltpu.CompilerParams(vmem_limit_bytes=60 * MIB),
        cost_estimate=cost(1.4e9),
        name="add_arrived",
    )(*args, *deps, *carry)


class Reduce:
    def __init__(self, parts, form, count, then=()):
        if then:
            parts = lax.optimization_barrier((*parts, *then))[: len(parts)]
        self.form, self.count, self.parts = form, count, parts
        if count != 4:
            self.total = lax.psum_scatter(parts[0], "tensor", scatter_dimension=0, tiled=True).astype(F32)
            self.arrived = (self.total,)
        elif form == "both":
            self.arrived = (hop(parts[1], 1, count), hop(parts[2], 2, count))
        else:
            self.arrived = (hop(parts[1], 1 if form == "x" else 2, count),)

    def first(self, deps=(), carry=()):
        if self.count != 4:
            return (self.total, *carry)
        if self.form == "both":
            x_first, y_first = self.arrived
            late = add_arrived([(self.parts[3], y_first), (self.parts[4], x_first)], deps, carry)
            self.second = (hop(late[0], 1, self.count), hop(late[1], 2, self.count))
        else:
            late = add_arrived([(self.parts[2], self.arrived[0])], deps, carry)
            self.second = (hop(late[0], 2 if self.form == "x" else 1, self.count),)
        return tuple(late)

    def settle(self, function, rows, kinds, deps=(), carry=()):
        if self.count != 4:
            return (*function(self.total, *rows), *carry)
        return settle_rows(
            self.form, self.parts[0], self.arrived, self.second, function, rows, kinds, deps, carry
        )


def settle_kernel(form, function, number, extra, kinds, *refs):
    own = refs[0][...].astype(F32)
    if form == "both":
        x_first, y_first, x_second, y_second = refs[1:5]
        refs = refs[5:]
        low = pl.program_id(0) == 0
        total = own + jnp.where(
            low,
            x_first[...].astype(F32) + y_second[...].astype(F32),
            y_first[...].astype(F32) + x_second[...].astype(F32),
        )
    else:
        total = own + refs[1][...].astype(F32) + refs[2][...].astype(F32)
        refs = refs[3:]
    values = function(total, *(ref[...] for ref in refs[:number]))
    for out, kind, value in zip(refs[number + extra :], kinds, values):
        if kind != "sum":
            out[...] = value
            continue

        @pl.when(pl.program_id(0) == 0)
        def _(out=out):
            out[...] = jnp.zeros_like(out)

        out[...] += value


def settle_rows(form, own, arrived, second, function, rows, kinds, deps, carry):
    size, depth = own.shape
    half = size // 2
    block = pl.BlockSpec((half, depth), lambda i: (i, 0))
    top = pl.BlockSpec((half, depth), lambda i: (0, 0))
    others = [top] * 4 if form == "both" else [block] * 2
    out_specs, out_shape = [], []
    for kind in kinds:
        out_specs.append(pl.BlockSpec((1, depth), lambda i: (0, 0)) if kind == "sum" else block)
        out_shape.append(
            jax.ShapeDtypeStruct((1, depth), F32) if kind == "sum" else jax.ShapeDtypeStruct((size, depth), kind)
        )
    return pl.pallas_call(
        functools.partial(settle_kernel, form, function, len(rows), len(deps) + len(carry), kinds),
        grid=(2,),
        in_specs=[block] + others + [block] * len(rows) + [HBM] * (len(deps) + len(carry)),
        out_specs=out_specs + [HBM] * len(carry),
        out_shape=out_shape + [jax.ShapeDtypeStruct(c.shape, c.dtype) for c in carry],
        input_output_aliases={
            1 + len(others) + len(rows) + len(deps) + i: len(kinds) + i for i in range(len(carry))
        },
        compiler_params=pltpu.CompilerParams(vmem_limit_bytes=60 * MIB),
        cost_estimate=cost(3e9),
        name="settle_rows",
    )(own, *arrived, *second, *rows, *deps, *carry)


def bits(count):
    assert count & (count - 1) == 0
    return [1 << i for i in range(count.bit_length() - 1)]


def sum_over(value, axis, count):
    for bit in bits(count):
        value = value + hop(value, bit, count, axis)
    return value


def norm_scale(rows):
    return lax.rsqrt(jnp.mean(rows * rows, axis=-1, keepdims=True) + EPSILON)


def add_branch(total, rows):
    middle = rows.astype(F32) + total
    return middle, (middle * norm_scale(middle)).astype(BF)


def add_last(total, middle):
    return ((middle + total).astype(BF),)


def turn_back(total, middle, cotangent):
    scale = norm_scale(middle)
    inner = jnp.mean(total * middle, axis=-1, keepdims=True)
    grad = cotangent.astype(F32) + scale * total - middle * (scale * scale * scale * inner)
    return grad, grad.astype(BF), jnp.sum(total * middle * scale, axis=0, keepdims=True)


def finish_back(total, rows, grad_middle):
    rows = rows.astype(F32)
    scale = norm_scale(rows)
    inner = jnp.mean(total * rows, axis=-1, keepdims=True)
    grad = grad_middle + total - rows * (scale * scale * inner)
    return (grad.astype(BF),)


def pack_kernel(size, number, turned_count, cuts, extra, *refs):
    weights, gain_ref = refs[:number], refs[number]
    others = refs[number + 1 : number + 1 + turned_count]
    outs = refs[number + 1 + turned_count + extra :]
    gain = gain_ref[...]
    groups = weights[0].shape[1] // size
    at = 0
    for i in range(groups):
        out = outs[i * cuts // groups]
        if i * cuts % groups == 0:
            at = 0
        for weight in weights:
            out[:, at : at + size] = (weight[:, i * size : (i + 1) * size].astype(F32) * gain).astype(BF)
            at += size
    for other in others:
        outs[-1][:, at : at + other.shape[0]] = other[...].T
        at += other.shape[0]


def pack(weights, gain, others, size, cuts, deps=()):
    rows_w, width = weights[0].shape
    widths = [len(weights) * width // cuts] * cuts
    widths[-1] += sum(other.shape[0] for other in others)
    whole = pl.BlockSpec(memory_space=pltpu.VMEM)
    return pl.pallas_call(
        functools.partial(pack_kernel, size, len(weights), len(others), cuts, len(deps)),
        in_specs=[whole] * (len(weights) + 1 + len(others)) + [HBM] * len(deps),
        out_specs=[whole] * cuts,
        out_shape=[jax.ShapeDtypeStruct((rows_w, w), BF) for w in widths],
        compiler_params=pltpu.CompilerParams(vmem_limit_bytes=60 * MIB),
        cost_estimate=cost(2e9),
        name="pack",
    )(*weights, gain, *others, *deps)


def unpack_kernel(groups, pitch, *refs):
    parts, gain_ref, outs = refs[: len(groups)], refs[len(groups)], refs[len(groups) + 1 :]
    at = 0
    for part, number in zip(parts, groups):
        size = part.shape[1] // (number * pitch)
        for i in range(number):
            for k, out in enumerate(outs):
                start = (i * pitch + k) * size
                out[:, at : at + size] = part[:, start : start + size].astype(F32) * gain_ref[...]
            at += size


def turn_kernel(number, *refs):
    for part, out in zip(refs[:number], refs[number:]):
        out[...] = part[...].astype(F32).T


def turned(parts):
    return pl.pallas_call(
        functools.partial(turn_kernel, len(parts)),
        out_shape=[jax.ShapeDtypeStruct(p.shape[::-1], F32) for p in parts],
        compiler_params=pltpu.CompilerParams(vmem_limit_bytes=60 * MIB),
        cost_estimate=cost(2e9),
        name="turned",
    )(*parts)


def unpack(parts, groups, pitch, gain):
    rows_w = gain.shape[0]
    width = sum(p.shape[1] for p in parts) // pitch
    return pl.pallas_call(
        functools.partial(unpack_kernel, groups, pitch),
        out_shape=[jax.ShapeDtypeStruct((rows_w, width), F32)] * pitch,
        compiler_params=pltpu.CompilerParams(vmem_limit_bytes=60 * MIB),
        cost_estimate=cost(2e9),
        name="unpack",
    )(*parts, gain)


def local(
    count_dp,
    count,
    tokens,
    cotangent,
    doc_lengths,
    rel_bucket,
    gain_attn,
    w_query,
    w_key,
    w_value,
    w_out,
    rel_table,
    gain_ff,
    w_gate,
    w_up,
    w_down,
):
    slots = tokens.shape[0]
    length = slots * count
    blocks = length // B
    rows_w, width = w_query.shape
    width_ff = w_gate.shape[1]
    pairs = width // 128
    heads = width // HD
    buckets_local = rel_table.shape[0]
    buckets = buckets_local * count_dp
    docs = doc_lengths.shape[1]
    tile = ff_tile(width_ff)
    me = lax.axis_index("dp").astype(jnp.int32)

    def spread(part):
        return lax.all_gather(part, "dp", axis=0, tiled=True)

    def after(value, *others):
        return lax.optimization_barrier((value, *others))[0]

    xs = [tokens[:, m] for m in range(MICRO)]
    gain_one = gain_attn.astype(F32)[:, None]
    gain_two = gain_ff.astype(F32)[:, None]
    cuts = 2
    each = pairs // cuts
    part_w = each * 384

    halves = pack([w_query, w_key, w_value], gain_one, [w_out], 128, cuts)
    full_qkv = [spread(half) for half in halves]
    full_out, out_at = full_qkv[-1], part_w
    form = "both" if count == 4 else None
    way = ("x", "y") if form else (None, None)

    table = rel_table.reshape(1, buckets_local * heads)
    for bit in bits(count_dp):
        table = jnp.concatenate([table, hop(table, bit, count_dp, "dp")], axis=0)
    table = jnp.take(table, jnp.arange(count_dp, dtype=jnp.int32) ^ me, axis=0).reshape(buckets, heads)
    reverse = jnp.concatenate([jnp.full((1,), -1, jnp.int32), rel_bucket[::-1]])
    onehot = reverse[None, :] == jnp.arange(buckets, dtype=jnp.int32)[:, None]
    offsets = tn(table, onehot.astype(BF)).reshape(heads, 2 * blocks, B)
    tiles = 2 * blocks - 1
    ahead = offsets[:, ::-1]
    bias = bias_strips(jnp.concatenate([ahead[:, :tiles], ahead[:, 1:]], axis=2))

    order = jnp.arange(blocks, dtype=jnp.int32)
    if count == 4:
        order = order ^ lax.axis_index("tensor").astype(jnp.int32)
    positions = (order[:, None] * B + jnp.arange(B, dtype=jnp.int32)[None]).reshape(-1)
    ends = jnp.cumsum(doc_lengths, axis=1)
    lane = jnp.arange(128, dtype=jnp.int32) % HD

    masks = []
    for m in range(MICRO):
        number = jnp.sum((positions[:, None] >= ends[m][None, :]).astype(jnp.int32), axis=1)
        by_block = number.reshape(blocks, B)
        least, most = by_block.min(axis=1), by_block.max(axis=1)
        active = (least[:, None] <= most[None, :]) & (least[None, :] <= most[:, None])
        same = number[:, None] == lane[None, :]
        feat_q = same.astype(BF)
        feat_k = jnp.where(same | (lane >= docs)[None, :], 0.0, -BIG).astype(BF)
        masks.append((feat_q, feat_k, active.astype(jnp.int32).reshape(-1)))
    ones = [Gather(xs[0], "both", count, (bias,))]
    (packed,) = pack([w_gate, w_up], gain_two, [w_down], tile, 1, (bias, *ones[0].sent))
    full_ff = spread(packed)

    def project(m, cut, scale, deps):
        mode = "take" if scale else "make"
        return product(ones[m].pieces, full_qkv[cut], 0, part_w, mode, scale, deps)

    def forward(m, cut, qkv, into, deps):
        feat_q, feat_k, active = masks[m]
        return attend_forward(qkv, feat_q, feat_k, bias, active, order, cut * each, into, deps)

    def out_rows(mixed, deps):
        return partial_rows([mixed], [full_out], [full_out.shape[1]], [0], [(width, width, out_at)], form, deps)

    def ff_rows(left, inner, way, deps, carry=()):
        size = 2 * width_ff if inner else width_ff
        return partial_rows(
            [left], [full_ff], [size], [0 if inner else 2], [(size, size, 0)], way, deps, (), carry
        )

    def qkv_rows(projects, m, deps, carry=()):
        return partial_rows(
            projects, full_qkv, [part_w] * cuts, [0] * cuts, [(part_w, part_w, 0)] * cuts, form, deps, ones[m].pieces, carry
        )

    def scatter(value):
        return lax.psum_scatter(value, "dp", scatter_dimension=0, tiled=True)

    qkv_0a, scale_0 = project(0, 0, (), (packed,))
    ones.append(Gather(after(xs[1], *ones[0].pieces), "both", count, (qkv_0a,)))
    into = forward(0, 0, qkv_0a, (), ())
    cs = [after(cotangent, qkv_0a)[:, m] for m in range(MICRO)]
    (qkv_0b,) = project(0, 1, (scale_0,), (into[0], *ones[1].first))
    cots = [Gather(cs[0], "both", count, (qkv_0b,))]
    mixed_0, lse_0 = forward(0, 1, qkv_0b, into, ())
    parts = out_rows(mixed_0, (*ones[1].pieces, *cots[0].first))
    sum_0 = Reduce(parts, form, count)
    qkv_1a, scale_1 = project(1, 0, (), (parts[0],))
    into = forward(1, 0, qkv_1a, (), tuple(cots[0].pieces))
    late = sum_0.first((into[0],))
    (qkv_1b,) = project(1, 1, (scale_1,), (late[0],))
    middle_0, normed = sum_0.settle(add_branch, [xs[0]], (F32, BF), (qkv_1b,))
    mixed_1, lse_1 = forward(1, 1, qkv_1b, into, (normed,))
    twos = [Gather(normed, "both", count, (mixed_1,))]
    parts = out_rows(mixed_1, twos[0].sent)
    sum_1 = Reduce(parts, form, count, twos[0].pieces)

    steps = width_ff // tile
    ff_half = (steps + 1) // 2 * 2 * tile
    hidden_0, grad_ff_0 = feed_forward(twos[0].pieces, cots[0].pieces, full_ff, 0, steps, (), (parts[0],))
    late = sum_1.first((hidden_0,))
    cots.append(Gather(after(cs[1], *twos[0].pieces), "both", count, (hidden_0,)))
    parts = ff_rows(grad_ff_0, True, form, (late[0],))
    middle_1, normed = sum_1.settle(add_branch, [xs[1]], (F32, BF), (parts[0],))
    twos.append(Gather(normed, "both", count))
    sum_0 = Reduce(parts, form, count, (*twos[1].pieces, *cots[1].pieces))
    down_part = outer([cots[0].pieces], [hidden_0], (normed,))
    ff_part_a = outer([twos[0].pieces], [grad_ff_0], (down_part,), 0, ff_half)
    ff_part_b = outer(
        [twos[0].pieces], [grad_ff_0], (ff_part_a, *twos[1].sent), ff_half, 2 * width_ff - ff_half
    )
    hidden_1, grad_ff_1 = feed_forward(
        twos[1].pieces, cots[1].pieces, full_ff, 0, steps, (), (ff_part_b,)
    )
    late = sum_0.first((hidden_1,))
    weight = outer([cots[1].pieces], [hidden_1], (late[0],), base=(down_part,))
    grad_middle_0, rounded, gain_two_0, weight = sum_0.settle(
        turn_back, [middle_0, cs[0]], (F32, BF, "sum"), (), (weight,)
    )
    grad_down = scatter(weight)
    mids = [Gather(rounded, "both", count)]
    parts = ff_rows(grad_ff_1, True, form, (rounded,))
    sum_1 = Reduce(parts, form, count)
    weight = outer(
        [twos[1].pieces], [grad_ff_1], (parts[0], *mids[0].sent), 0, ff_half, base=(ff_part_a,)
    )
    down = ff_rows(hidden_0, False, way[0], (weight,))
    late = sum_1.first((down[0], *mids[0].pieces), (weight,))
    grad_ff_a = scatter(late[-1])

    def backward(m, qkv, lse, mixed, grad, scale, cut, into, deps):
        feat_q, feat_k, active = masks[m]
        return attend_backward(
            qkv, feat_q, feat_k, bias, lse, mixed, grad, scale, active, order, cut * each, into, deps
        )

    (grad,) = product(mids[0].pieces, full_out, out_at, width, deps=(late[0],))
    weight = outer(
        [twos[1].pieces], [grad_ff_1], (grad,), ff_half, 2 * width_ff - ff_half, base=(ff_part_b,)
    )
    grad_middle_1, rounded, gain_two_1, weight = sum_1.settle(
        turn_back, [middle_1, cs[1]], (F32, BF, "sum"), (), (weight,)
    )
    grad_ff_b = scatter(weight)
    mids.append(Gather(rounded, "both", count))
    grad_0a, fold = backward(0, qkv_0a, lse_0, mixed_0, grad, scale_0, 0, (), (rounded,))
    down_0 = Reduce(down, way[0], count, mids[1].first)
    grad_0b, fold_0 = backward(0, qkv_0b, lse_0, mixed_0, grad, scale_0, 1, (fold,), mids[1].sent)
    *parts, gain_one_0 = qkv_rows([grad_0a, grad_0b], 0, (grad_down,))
    sum_0 = Reduce(parts, form, count)
    (grad,) = product(mids[1].pieces, full_out, out_at, width, deps=(parts[0],))
    weight = outer([g.pieces for g in mids], [mixed_0, mixed_1], (grad, grad_ff_a))
    late = sum_0.first((), (weight,))
    grad_out = scatter(late[-1])
    late = down_0.first((late[0],))
    grad_1a, fold = backward(1, qkv_1a, lse_1, mixed_1, grad, scale_1, 0, (), (late[0],))
    (output_0,) = down_0.settle(add_last, [middle_0], (BF,), (grad_1a,))
    weight = outer([g.pieces for g in ones], [grad_0a, grad_1a], (output_0,))
    token_0, weight = sum_0.settle(finish_back, [xs[0], grad_middle_0], (BF,), (), (weight,))
    grad_qkv_a = scatter(weight)
    parts = ff_rows(hidden_1, False, form, (token_0,))
    down_1 = Reduce(parts, form, count)
    grad_1b, fold_1 = backward(1, qkv_1b, lse_1, mixed_1, grad, scale_1, 1, (fold,), (parts[0], grad_ff_b))
    late = down_1.first((grad_1b,))
    weight = outer([g.pieces for g in ones], [grad_0b, grad_1b], (late[0], grad_out))
    output_1, weight = down_1.settle(add_last, [middle_1], (BF,), (), (weight,))
    grad_qkv_b = scatter(weight)
    *parts, gain_one_1 = qkv_rows([grad_1a, grad_1b], 1, (output_1,))
    sum_1 = Reduce(parts, form, count)
    grad_gate, grad_up = unpack(
        [grad_ff_a, grad_ff_b], ((steps + 1) // 2, steps // 2), 2, gain_two
    )
    grad_out, grad_down = turned([grad_out, grad_down])

    fold = (fold_0 + fold_1).reshape(heads, 2 * blocks, B)[:, ::-1]
    before = jnp.concatenate([jnp.zeros((heads, 1, B), F32), fold[:, :-1]], axis=1)
    by_offset = jnp.where(jnp.arange(B) == 0, before, fold).reshape(heads, 2 * length)
    grad_table = lax.dot_general(
        onehot.astype(F32), by_offset, (((1,), (1,)), ((), ())), precision=lax.Precision.HIGHEST
    )
    small = jnp.concatenate(
        [
            (gain_one_0 + gain_one_1).reshape(count_dp, rows_w),
            (gain_two_0 + gain_two_1).reshape(count_dp, rows_w),
            grad_table.reshape(count_dp, buckets_local * heads),
        ],
        axis=1,
    )
    small = sum_over(small, "dp", count_dp)
    late = sum_1.first((small, grad_gate, grad_out, grad_down))
    grad_qkv = unpack([grad_qkv_a, grad_qkv_b], (each, each), 3, gain_one)
    small, output_0, output_1 = lax.optimization_barrier((small, output_0, output_1, grad_qkv[0]))[:3]
    small = lax.dynamic_index_in_dim(small, me, 0, keepdims=False)
    both_gains = sum_over(small[: 2 * rows_w], "tensor", count)
    (token_1,) = sum_1.settle(
        finish_back,
        [xs[1], grad_middle_1],
        (BF,),
        (late[0], grad_qkv[0]),
    )
    return (
        jnp.stack([output_0, output_1], axis=1),
        jnp.stack([token_0, token_1], axis=1),
        both_gains[:rows_w] / gain_one[:, 0],
        *grad_qkv,
        grad_out,
        small[2 * rows_w :].reshape(buckets_local, heads),
        both_gains[rows_w:] / gain_two[:, 0],
        grad_gate,
        grad_up,
        grad_down,
    )


def solution(mesh):
    row, col = P("dp", "tensor"), P("tensor", "dp")
    acts = P("tensor", "dp", None)
    in_specs = (
        acts, acts, P("dp", None), P(), P("dp"), row, row, row, col, row, P("dp"), row, row, col
    )
    out_specs = (acts, acts, P("dp"), row, row, row, col, row, P("dp"), row, row, col)
    body = functools.partial(local, mesh.shape["dp"], mesh.shape["tensor"])
    return jax.shard_map(body, mesh=mesh, in_specs=in_specs, out_specs=out_specs, check_vma=False)
```

```python
import functools
import jax
import jax.numpy as jnp
from jax import lax
from jax.experimental import pallas as pl
from jax.experimental.pallas import tpu as pltpu
from jax.sharding import PartitionSpec as P

HD=64
B=256
BIG=1e30
F32=jnp.float32; BF=jnp.bfloat16

def nt(a,b): return lax.dot_general(a,b,(((1,),(1,)),((),())),preferred_element_type=F32)
def nn(a,b): return lax.dot_general(a,b,(((1,),(0,)),((),())),preferred_element_type=F32)


EPSILON = 1e-06
MICRO = 2
HBM = pl.BlockSpec(memory_space=pltpu.HBM)
MIB = 1 << 20


def cost(flops):
    return pl.CostEstimate(flops=int(2 * flops), bytes_accessed=1, transcendentals=0)


def tn(left, right):
    return lax.dot_general(left, right, (((0,), (0,)), ((), ())), preferred_element_type=F32)


def pick(size, *tiles, start=0):
    return next(tile for tile in (*tiles, 128, size) if size % tile == 0 and start % tile == 0)


def strips_kernel(w_ref, out_ref):
    def body(i, _):
        wide = jnp.broadcast_to(w_ref[0, pl.ds(i, 1), :], (B, 2 * B))
        rolled = pltpu.roll(wide, 0, 1, stride=1, stride_axis=0)
        out_ref[0, pl.ds(pl.multiple_of(i * B, B), B), :] = rolled[:, :B]
        return 0

    lax.fori_loop(0, w_ref.shape[1], body, 0)


def bias_strips(w):
    heads, tiles, _ = w.shape
    return pl.pallas_call(
        strips_kernel,
        grid=(heads,),
        in_specs=[pl.BlockSpec((1, tiles, 2 * B), lambda h: (h, 0, 0))],
        out_specs=pl.BlockSpec((1, tiles * B, B), lambda h: (h, 0, 0)),
        out_shape=jax.ShapeDtypeStruct((heads, tiles * B, B), F32),
        compiler_params=pltpu.CompilerParams(vmem_limit_bytes=60 * MIB),
        cost_estimate=cost(6e9),
        name="bias_strips",
    )(w)


def by_tile(act_ref, base, n, *functions):
    count = act_ref[base]
    for i in range(1, n):
        count = count + act_ref[base + i]
    most = count * 4 >= 3 * n

    @pl.when(most)
    def _():
        for function in functions:
            for i in range(n):
                function(i)

    @pl.when(jnp.logical_not(most))
    def _():
        for function in functions:

            def step(i, _, function=function):
                @pl.when(act_ref[base + i] != 0)
                def _():
                    function(i)

                return 0

            lax.fori_loop(0, n, step, 0)


def attend_forward_kernel(n, extra, *refs):
    act_ref, blk_ref, qkv_ref, fq_ref, fk_ref, bias_ref = refs[:6]
    o_ref, lse_ref, qx, kx, vx, s_scr, m_scr, o_scr = refs[6 + extra :]
    lane = lax.broadcasted_iota(jnp.int32, (1, 128), 1)
    q, k, v = qkv_ref[:, 0:128], qkv_ref[:, 128:256], qkv_ref[:, 256:384]
    vt = v.T
    for h in range(2):
        own = (lane < HD) if h == 0 else (lane >= HD)
        qx[h] = jnp.where(own, q, fq_ref[...]).T
        kx[h] = jnp.where(own, k, fk_ref[...])
        vx[h] = jnp.concatenate([vt[h * HD : (h + 1) * HD], jnp.ones((16, vt.shape[1]), BF)], axis=0)

    def row(qi, _):
        qs = pl.ds(pl.multiple_of(qi * B, B), B)
        m_scr[...] = jnp.full_like(m_scr, -3e38)
        o_scr[...] = jnp.zeros_like(o_scr)

        def score(kb):
            ks = pl.ds(pl.multiple_of(kb * B, B), B)
            bs = pl.ds(pl.multiple_of((blk_ref[kb] - blk_ref[qi] + n - 1) * B, B), B)
            for h in range(2):
                s = nn(kx[h, ks, :], qx[h, :, qs]) + bias_ref[h, bs, :]
                s_scr[h, ks, :] = s
                m_scr[h] = jnp.maximum(m_scr[h], jnp.max(s.reshape(B // 8, 8, B), axis=0))

        def share(kb):
            ks = pl.ds(pl.multiple_of(kb * B, B), B)
            for h in range(2):
                p = jnp.exp(s_scr[h, ks, :] - jnp.max(m_scr[h], axis=0, keepdims=True)).astype(BF)
                o_scr[h] += nn(vx[h, :, ks], p)

        by_tile(act_ref, qi * n, n, score, share)
        peaks = [jnp.max(m_scr[h], axis=0, keepdims=True) for h in range(2)]
        outs = []
        for h in range(2):
            total = o_scr[h, HD : HD + 1, :]
            outs.append(o_scr[h, 0:HD, :] / total)
            lse_ref[0, pl.ds(h, 1), qs] = peaks[h] + jnp.log(total)
        o_ref[qs, :] = jnp.concatenate(outs, axis=0).T.astype(BF)
        return 0

    lax.fori_loop(0, n, row, 0)


def attend_forward(qkv, feat_q, feat_k, bias, active, order, first, into=(), deps=()):
    length, width3 = qkv.shape
    n, number, pairs = length // B, width3 // 384, bias.shape[0] // 2
    rows = (2 * n - 1) * B
    extra = len(into) + len(deps)
    whole = pl.BlockSpec((length, 128), lambda p, *_: (0, 0))
    return pl.pallas_call(
        functools.partial(attend_forward_kernel, n, extra),
        grid_spec=pltpu.PrefetchScalarGridSpec(
            num_scalar_prefetch=2,
            grid=(number,),
            in_specs=[
                pl.BlockSpec((length, 384), lambda p, *_: (0, p)),
                whole,
                whole,
                pl.BlockSpec((2, rows, B), lambda p, *_: (p + first, 0, 0)),
            ]
            + [HBM] * extra,
            out_specs=[
                pl.BlockSpec((length, 128), lambda p, *_: (0, p + first)),
                pl.BlockSpec((1, 2, length), lambda p, *_: (p + first, 0, 0)),
            ],
            scratch_shapes=[
                pltpu.VMEM((2, 128, length), BF),
                pltpu.VMEM((2, length, 128), BF),
                pltpu.VMEM((2, HD + 16, length), BF),
                pltpu.VMEM((2, length, B), F32),
                pltpu.VMEM((2, 8, B), F32),
                pltpu.VMEM((2, HD + 16, B), F32),
            ],
        ),
        out_shape=[
            jax.ShapeDtypeStruct((length, pairs * 128), BF),
            jax.ShapeDtypeStruct((pairs, 2, length), F32),
        ],
        input_output_aliases={6 + i: i for i in range(len(into))},
        compiler_params=pltpu.CompilerParams(vmem_limit_bytes=60 * MIB),
        cost_estimate=cost(3.7e9 * number),
        name="attend_forward",
    )(active, order, qkv, feat_q, feat_k, bias, *into, *deps)


def attend_backward_kernel(n, extra, *refs):
    act_ref, blk_ref, qkv_ref, fq_ref, fk_ref, bias_ref, lse_ref, o_ref, do_ref, sc_ref = refs[:10]
    g_ref, fold_ref, qx, kx, v0, kt, delta, dk, dv, dqt, diag, p_scr, ds_scr, dot_ = refs[10 + extra :]
    lane = lax.broadcasted_iota(jnp.int32, (1, 128), 1)
    q, k, v = qkv_ref[:, 0:128], qkv_ref[:, 128:256], qkv_ref[:, 256:384]
    for h in range(2):
        own = (lane < HD) if h == 0 else (lane >= HD)
        qx[h] = jnp.where(own, q, fq_ref[...]).T
        kx[h] = jnp.where(own, k, fk_ref[...])
        v0[h] = jnp.where(own, v, jnp.zeros_like(v))
    kt[...] = k.T
    dot_[...] = do_ref[...].T
    prod = (o_ref[...].astype(F32) * do_ref[...].astype(F32)).T
    for h in range(2):
        delta[h : h + 1, :] = jnp.sum(prod[h * HD : (h + 1) * HD], axis=0, keepdims=True)
    diag[...] = jnp.zeros_like(diag)
    dqt[...] = jnp.zeros_like(dqt)

    def column(kb, _):
        ks = pl.ds(pl.multiple_of(kb * B, B), B)

        def tile(qi):
            qs = pl.ds(pl.multiple_of(qi * B, B), B)
            bs = pl.ds(pl.multiple_of((blk_ref[kb] - blk_ref[qi] + n - 1) * B, B), B)
            for h in range(2):
                s = nn(kx[h, ks, :], qx[h, :, qs]) + bias_ref[h, bs, :]
                dp = nn(v0[h, ks, :], dot_[:, qs])
                p = jnp.exp(s - lse_ref[0, pl.ds(h, 1), qs])
                ds = p * (dp - delta[pl.ds(h, 1), qs])
                p_scr[h, :, qs] = p.astype(BF)
                ds_scr[h, :, qs] = ds.astype(BF)
                diag[h, bs, :] += ds

        count = act_ref[kb * n]
        for i in range(1, n):
            count = count + act_ref[kb * n + i]

        @pl.when(count * 4 < 3 * n)
        def _():
            p_scr[...] = jnp.zeros_like(p_scr)
            ds_scr[...] = jnp.zeros_like(ds_scr)

        by_tile(act_ref, kb * n, n, tile)
        for h in range(2):
            dv[h, ks, :] = nn(p_scr[h], do_ref[...])
            dk[h, ks, :] = nn(ds_scr[h], qkv_ref[:, 0:128])
            dqt[h * HD : (h + 1) * HD, :] += nn(kt[h * HD : (h + 1) * HD, ks], ds_scr[h])
        return 0

    lax.fori_loop(0, n, column, 0)
    g_ref[:, 0:128] = (dqt[...].T * sc_ref[...]).astype(BF)
    left = lane < HD
    g_ref[:, 128:256] = (jnp.where(left, dk[0], dk[1]) * sc_ref[...]).astype(BF)
    g_ref[:, 256:384] = (jnp.where(left, dv[0], dv[1]) * sc_ref[...]).astype(BF)
    row = lax.broadcasted_iota(jnp.int32, (B, B), 0)
    below = row >= lax.broadcasted_iota(jnp.int32, (B, B), 1)
    half = B // 2
    flip = lax.broadcasted_iota(jnp.int32, (half, half), 0) + lax.broadcasted_iota(jnp.int32, (half, half), 1)
    flip = (flip == half - 1).astype(BF)
    for h in range(2):
        for j in range(2 * n):
            low = diag[h, (j - 1) * B : j * B, :] if j > 0 else 0.0
            high = diag[h, j * B : (j + 1) * B, :] if j < 2 * n - 1 else 0.0
            part = jnp.where(below, low, high)
            part = part[:half] + jnp.concatenate([part[half:, half:], part[half:, :half]], axis=1)
            part = pltpu.roll(nn(flip, part.astype(BF)), half + 1, 1, stride=1, stride_axis=0)
            fold_ref[0, h, j : j + 1, :] = jnp.sum(part, axis=0, keepdims=True)


def attend_backward(
    qkv, feat_q, feat_k, bias, lse, mixed, grad, scale, active, order, first, into=(), deps=()
):
    length, width3 = qkv.shape
    n, number, pairs = length // B, width3 // 384, bias.shape[0] // 2
    tiles = 2 * n - 1
    rows = tiles * B
    extra = len(into) + len(deps)
    whole = pl.BlockSpec((length, 128), lambda p, *_: (0, 0))
    one = pl.BlockSpec((length, 128), lambda p, *_: (0, p + first))
    three = pl.BlockSpec((length, 384), lambda p, *_: (0, p))
    return pl.pallas_call(
        functools.partial(attend_backward_kernel, n, extra),
        grid_spec=pltpu.PrefetchScalarGridSpec(
            num_scalar_prefetch=2,
            grid=(number,),
            in_specs=[
                three,
                whole,
                whole,
                pl.BlockSpec((2, rows, B), lambda p, *_: (p + first, 0, 0)),
                pl.BlockSpec((1, 2, length), lambda p, *_: (p + first, 0, 0)),
                one,
                one,
                whole,
            ]
            + [HBM] * extra,
            out_specs=[three, pl.BlockSpec((1, 2, 2 * n, B), lambda p, *_: (p + first, 0, 0, 0))],
            scratch_shapes=[
                pltpu.VMEM((2, 128, length), BF),
                pltpu.VMEM((2, length, 128), BF),
                pltpu.VMEM((2, length, 128), BF),
                pltpu.VMEM((128, length), BF),
                pltpu.VMEM((2, length), F32),
                pltpu.VMEM((2, length, 128), F32),
                pltpu.VMEM((2, length, 128), F32),
                pltpu.VMEM((2 * HD, length), F32),
                pltpu.VMEM((2, rows, B), F32),
                pltpu.VMEM((2, B, length), BF),
                pltpu.VMEM((2, B, length), BF),
                pltpu.VMEM((128, length), BF),
            ],
        ),
        out_shape=[
            jax.ShapeDtypeStruct((length, width3), BF),
            jax.ShapeDtypeStruct((pairs, 2, 2 * n, B), F32),
        ],
        input_output_aliases={10: 1} if into else {},
        compiler_params=pltpu.CompilerParams(vmem_limit_bytes=60 * MIB),
        cost_estimate=cost(6.5e9 * number),
        name="attend_backward",
    )(active, order, qkv, feat_q, feat_k, bias, lse, mixed, grad, scale, *into, *deps)


def load(pieces, rows, sems):
    copies, start = [], 0
    for i, piece in enumerate(pieces):
        size = piece.shape[0]
        copies.append((start, pltpu.make_async_copy(piece, rows.at[pl.ds(start, size)], sems.at[i])))
        start += size
    first = pl.program_id(0) == 0

    @pl.when(first)
    def _():
        for _, copy in copies:
            copy.start()

    def ready(end):
        due = [copy for at, copy in copies if at < end]
        del copies[: len(due)]
        if due:

            @pl.when(first)
            def _():
                for copy in due:
                    copy.wait()

    return ready


def product_kernel(mode, count, extra, carried, *refs):
    pieces, w_ref = refs[:count], refs[count]
    refs = refs[count + 1 :]
    if mode == "take":
        sc_ref, refs = refs[0], refs[1:]
    refs = refs[extra:]
    o_ref, refs = refs[0], refs[1:]
    if mode == "make":
        sc_ref, refs = refs[0], refs[1:]
    rows, sems = refs[carried:]
    load(pieces, rows, sems)(rows.shape[0])
    if mode == "make":

        @pl.when(pl.program_id(0) == 0)
        def _():
            step = pick(rows.shape[0], 256)

            def body(i, _):
                part = pl.ds(pl.multiple_of(i * step, step), step)
                x = rows[part, :].astype(F32)
                scale = norm_scale(x)
                sc_ref[part, :] = jnp.broadcast_to(scale, (step, 128))
                return 0

            lax.fori_loop(0, rows.shape[0] // step, body, 0)

    value = nn(rows[...], w_ref[...])
    if mode != "plain":
        value = value * sc_ref[:, 0:1]
    o_ref[...] = value.astype(BF)


def product(pieces, w, start, width, mode="plain", scale=(), deps=(), carry=()):
    length, depth = sum(p.shape[0] for p in pieces), w.shape[0]
    tile = pick(width, 512, 256, start=start)
    by_row = pl.BlockSpec((length, 128), lambda j: (0, 0))
    make = mode == "make"
    return pl.pallas_call(
        functools.partial(product_kernel, mode, len(pieces), len(deps) + len(carry), len(carry)),
        grid=(width // tile,),
        in_specs=[HBM] * len(pieces)
        + [pl.BlockSpec((depth, tile), lambda j: (0, start // tile + j))]
        + [by_row] * len(scale)
        + [HBM] * (len(deps) + len(carry)),
        out_specs=[pl.BlockSpec((length, tile), lambda j: (0, j))] + [by_row] * make + [HBM] * len(carry),
        out_shape=[jax.ShapeDtypeStruct((length, width), BF)]
        + [jax.ShapeDtypeStruct((length, 128), F32)] * make
        + [jax.ShapeDtypeStruct(c.shape, c.dtype) for c in carry],
        input_output_aliases={
            len(pieces) + 1 + len(scale) + len(deps) + i: 1 + make + i for i in range(len(carry))
        },
        scratch_shapes=[pltpu.VMEM((length, depth), BF), pltpu.SemaphoreType.DMA((len(pieces),))],
        compiler_params=pltpu.CompilerParams(vmem_limit_bytes=60 * MIB),
        cost_estimate=cost(2 * length * depth * width + 2e9),
        name="rows_product",
    )(*pieces, w, *scale, *deps, *carry)


def outer_kernel(counts, based, extra, *refs):
    total = sum(counts)
    groups, start = [], 0
    for count in counts:
        groups.append(refs[start : start + count])
        start += count
    rights = refs[total : total + len(counts)]
    out_ref, rows, sems = refs[total + len(counts) + based + extra :]
    first = 0
    loads = []
    for m, group in enumerate(groups):
        loads.append(load(group, rows.at[m], sems.at[pl.ds(first, len(group))]))
        first += len(group)
    value = 0.0
    for m, ready in enumerate(loads):
        ready(rows.shape[1])
        value = value + tn(rights[m][...], rows[m])
    value = value.astype(BF).T
    if based:
        value = (value.astype(F32) + refs[total + len(counts)][...].astype(F32)).astype(BF)
    out_ref[...] = value


def outer(lefts, rights, deps=(), first=0, width=None, base=()):
    length = rights[0].shape[0]
    width = width or rights[0].shape[1]
    depth = lefts[0][0].shape[1]
    tile = pick(width, 512, 640, 384, 256, start=first)
    counts = tuple(len(group) for group in lefts)
    flat = [piece for group in lefts for piece in group]
    return pl.pallas_call(
        functools.partial(outer_kernel, counts, len(base), len(deps)),
        grid=(width // tile,),
        in_specs=[HBM] * len(flat)
        + [pl.BlockSpec((length, tile), lambda j: (0, first // tile + j))] * len(rights)
        + [pl.BlockSpec((depth, tile), lambda j: (0, j))] * len(base)
        + [HBM] * len(deps),
        out_specs=pl.BlockSpec((depth, tile), lambda j: (0, j)),
        out_shape=jax.ShapeDtypeStruct((depth, width), BF),
        scratch_shapes=[
            pltpu.VMEM((len(lefts), length, depth), BF),
            pltpu.SemaphoreType.DMA((len(flat),)),
        ],
        compiler_params=pltpu.CompilerParams(vmem_limit_bytes=60 * MIB),
        cost_estimate=cost(2 * len(lefts) * length * depth * width),
        name="weight_gradient",
    )(*flat, *rights, *base, *deps)


def partial_kernel(form, layouts, against, extra, carried, *refs):
    number = len(layouts)
    rows = refs[2 * number : 2 * number + against]
    outs = refs[2 * number + against + extra : len(refs) - carried]
    value = None
    for a_ref, w_ref, (size, pitch, start) in zip(refs[:number], refs[number:], layouts):
        for i in range(a_ref.shape[1] // size):
            cols = slice(i * pitch + start, i * pitch + start + size)
            part = nt(a_ref[:, i * size : (i + 1) * size], w_ref[:, cols])
            value = part if value is None else value + part
    if against:
        total, at = 0.0, 0
        for piece in rows:
            size = piece.shape[0]
            total = total + jnp.sum(value[at : at + size] * piece[...].astype(F32), axis=0, keepdims=True)
            at += size
        outs[-1][...] = total
        outs = outs[:-1]
    value = value.astype(BF)
    if form is None:
        outs[0][...] = value
        return
    size = outs[0].shape[0]
    half = size // 2
    blocks = [value[i * size : (i + 1) * size] for i in range(4)]
    if form != "both":
        own, pair, late = outs
        first, second = (1, 2) if form == "x" else (2, 1)
        own[...] = blocks[0]
        pair[:size] = blocks[first]
        pair[size:] = blocks[3]
        late[...] = blocks[second]
        return
    own, send_x, send_y, late_x, late_y = outs
    own[...] = blocks[0]
    send_x[:half] = blocks[1][:half]
    send_x[half:] = blocks[3][:half]
    send_y[:half] = blocks[2][half:]
    send_y[half:] = blocks[3][half:]
    late_x[...] = blocks[1][half:]
    late_y[...] = blocks[2][:half]


def partial_rows(lefts, weights, widths, ats, layouts, form, deps=(), pieces=(), carry=()):
    length = lefts[0].shape[0]
    depth = weights[0].shape[0]
    tile = pick(depth, 512, 256)
    size = length // 4
    heights = {
        None: [length],
        "both": [size, size, size, size // 2, size // 2],
        "x": [size, 2 * size, size],
        "y": [size, 2 * size, size],
    }[form]
    sums = [jax.ShapeDtypeStruct((1, depth), F32)] if pieces else []
    return pl.pallas_call(
        functools.partial(partial_kernel, form, layouts, len(pieces), len(deps) + len(carry), len(carry)),
        grid=(depth // tile,),
        in_specs=[pl.BlockSpec(a.shape, lambda j: (0, 0)) for a in lefts]
        + [pl.BlockSpec((tile, width), lambda j, at=at: (j, at)) for width, at in zip(widths, ats)]
        + [pl.BlockSpec((p.shape[0], tile), lambda j: (0, j)) for p in pieces]
        + [HBM] * (len(deps) + len(carry)),
        out_specs=[pl.BlockSpec((height, tile), lambda j: (0, j)) for height in heights]
        + [pl.BlockSpec((1, tile), lambda j: (0, j))] * len(sums)
        + [HBM] * len(carry),
        out_shape=[jax.ShapeDtypeStruct((height, depth), BF) for height in heights]
        + sums
        + [jax.ShapeDtypeStruct(c.shape, c.dtype) for c in carry],
        input_output_aliases={
            len(lefts) + len(weights) + len(pieces) + len(deps) + i: len(heights) + len(sums) + i
            for i in range(len(carry))
        },
        compiler_params=pltpu.CompilerParams(vmem_limit_bytes=60 * MIB),
        cost_estimate=cost(2 * length * depth * sum(a.shape[1] for a in lefts)),
        name="partial_rows",
    )(*lefts, *weights, *pieces, *deps, *carry)


def ff_kernel(count, count_cot, extra, *refs):
    total = count + count_cot
    pieces, cots = refs[:count], refs[count:total]
    w_ref, d_ref = refs[total : total + 2]
    hid_ref, g_ref, rows, cot, sems = refs[total + 2 + extra :]
    ready = load(pieces, rows, sems.at[pl.ds(0, count)])
    load(cots, cot, sems.at[pl.ds(count, count_cot)])(cot.shape[0])
    ready(rows.shape[0])
    tile = d_ref.shape[1]
    length = rows.shape[0]
    step = pick(length, 256)
    c = 0.7978845608028654
    for i in range(length // step):
        part = slice(i * step, (i + 1) * step)
        both = nn(rows[part], w_ref[...])
        grad = nn(cot[part], d_ref[...])
        gate, up = both[:, :tile], both[:, tile:]
        square = gate * gate
        th = jnp.tanh(c * gate * (1.0 + 0.044715 * square))
        half = 0.5 * (1.0 + th)
        value = gate * half
        slope = half + 0.5 * gate * (1.0 - th * th) * (c + 3 * 0.044715 * c * square)
        hid_ref[part] = (value * up).astype(BF)
        g_ref[part, :tile] = (grad * up * slope).astype(BF)
        g_ref[part, tile:] = (grad * value).astype(BF)


def ff_tile(width):
    return pick(width, 256)


def feed_forward(pieces, cots, w, first, number, into=(), deps=()):
    length, depth, width = sum(p.shape[0] for p in pieces), w.shape[0], w.shape[1] // 3
    tile = ff_tile(width)
    count = len(pieces) + len(cots)
    extra = len(deps) + len(into)
    return pl.pallas_call(
        functools.partial(ff_kernel, len(pieces), len(cots), extra),
        grid=(number,),
        in_specs=[HBM] * count
        + [
            pl.BlockSpec((depth, 2 * tile), lambda j: (0, j + first)),
            pl.BlockSpec((depth, tile), lambda j: (0, j + first + 2 * width // tile)),
        ]
        + [HBM] * extra,
        out_specs=[
            pl.BlockSpec((length, tile), lambda j: (0, j + first)),
            pl.BlockSpec((length, 2 * tile), lambda j: (0, j + first)),
        ],
        out_shape=[
            jax.ShapeDtypeStruct((length, width), BF),
            jax.ShapeDtypeStruct((length, 2 * width), BF),
        ],
        input_output_aliases={count + 2 + i: i for i in range(len(into))},
        scratch_shapes=[
            pltpu.VMEM((length, depth), BF),
            pltpu.VMEM((length, depth), BF),
            pltpu.SemaphoreType.DMA((count,)),
        ],
        compiler_params=pltpu.CompilerParams(vmem_limit_bytes=60 * MIB),
        cost_estimate=cost(6 * length * depth * tile * number),
        name="feed_forward",
    )(*pieces, *cots, w, w, *into, *deps)


def hop(part, bit, count, axis="tensor"):
    return lax.ppermute(part, axis, [(i, i ^ bit) for i in range(count)])


class Gather:
    def __init__(self, part, via, count, then=()):
        self.own = part
        self.sent = ()
        if count != 4:
            self.first = self.sent = (lax.all_gather(part, "tensor", axis=0, tiled=True),)
            self.pieces = list(self.first)
            return
        from_x, from_y = hop(part, 1, count), hop(part, 2, count)
        self.first = (from_x, from_y)
        half = part.shape[0] // 2
        self.pieces = [part, from_x, from_y]
        if then:
            from_x, from_y = lax.optimization_barrier((from_x, from_y, *then))[:2]
        if via == "x":
            self.pieces.append(hop(from_y, 1, count))
        elif via == "y":
            self.pieces.append(hop(from_x, 2, count))
        else:
            self.sent = (from_y[:half], from_x[half:])
            self.pieces += [hop(self.sent[0], 1, count), hop(self.sent[1], 2, count)]


def add_kernel(number, carried, *refs):
    ins, outs = refs[: 2 * number], refs[len(refs) - number - carried :][:number]
    for i, out in enumerate(outs):
        out[...] = (ins[2 * i][...].astype(F32) + ins[2 * i + 1][...].astype(F32)).astype(BF)


def add_arrived(pairs, deps, carry):
    depth = pairs[0][0].shape[1]
    tile = pick(depth, 1024)
    specs, args, outs = [], [], []
    for late, arrived in pairs:
        height = late.shape[0]
        specs += [pl.BlockSpec((height, tile), lambda j: (0, j)), pl.BlockSpec((height, tile), lambda j: (1, j))]
        args += [late, arrived]
        outs.append(late)
    return pl.pallas_call(
        functools.partial(add_kernel, len(pairs), len(carry)),
        grid=(depth // tile,),
        in_specs=specs + [HBM] * (len(deps) + len(carry)),
        out_specs=[pl.BlockSpec((o.shape[0], tile), lambda j: (0, j)) for o in outs] + [HBM] * len(carry),
        out_shape=[jax.ShapeDtypeStruct(o.shape, o.dtype) for o in (*outs, *carry)],
        input_output_aliases={len(args) + len(deps) + i: len(outs) + i for i in range(len(carry))},
        compiler_params=pltpu.CompilerParams(vmem_limit_bytes=60 * MIB),
        cost_estimate=cost(1.4e9),
        name="add_arrived",
    )(*args, *deps, *carry)


class Reduce:
    def __init__(self, parts, form, count, then=()):
        if then:
            parts = lax.optimization_barrier((*parts, *then))[: len(parts)]
        self.form, self.count, self.parts = form, count, parts
        if count != 4:
            self.total = lax.psum_scatter(parts[0], "tensor", scatter_dimension=0, tiled=True).astype(F32)
            self.arrived = (self.total,)
        elif form == "both":
            self.arrived = (hop(parts[1], 1, count), hop(parts[2], 2, count))
        else:
            self.arrived = (hop(parts[1], 1 if form == "x" else 2, count),)

    def first(self, deps=(), carry=()):
        if self.count != 4:
            return (self.total, *carry)
        if self.form == "both":
            x_first, y_first = self.arrived
            late = add_arrived([(self.parts[3], y_first), (self.parts[4], x_first)], deps, carry)
            self.second = (hop(late[0], 1, self.count), hop(late[1], 2, self.count))
        else:
            late = add_arrived([(self.parts[2], self.arrived[0])], deps, carry)
            self.second = (hop(late[0], 2 if self.form == "x" else 1, self.count),)
        return tuple(late)

    def settle(self, function, rows, kinds, deps=(), carry=()):
        if self.count != 4:
            return (*function(self.total, *rows), *carry)
        return settle_rows(
            self.form, self.parts[0], self.arrived, self.second, function, rows, kinds, deps, carry
        )


def settle_kernel(form, function, number, extra, kinds, *refs):
    own = refs[0][...].astype(F32)
    if form == "both":
        x_first, y_first, x_second, y_second = refs[1:5]
        refs = refs[5:]
        low = pl.program_id(0) == 0
        total = own + jnp.where(
            low,
            x_first[...].astype(F32) + y_second[...].astype(F32),
            y_first[...].astype(F32) + x_second[...].astype(F32),
        )
    else:
        total = own + refs[1][...].astype(F32) + refs[2][...].astype(F32)
        refs = refs[3:]
    values = function(total, *(ref[...] for ref in refs[:number]))
    for out, kind, value in zip(refs[number + extra :], kinds, values):
        if kind != "sum":
            out[...] = value
            continue

        @pl.when(pl.program_id(0) == 0)
        def _(out=out):
            out[...] = jnp.zeros_like(out)

        out[...] += value


def settle_rows(form, own, arrived, second, function, rows, kinds, deps, carry):
    size, depth = own.shape
    half = size // 2
    block = pl.BlockSpec((half, depth), lambda i: (i, 0))
    top = pl.BlockSpec((half, depth), lambda i: (0, 0))
    others = [top] * 4 if form == "both" else [block] * 2
    out_specs, out_shape = [], []
    for kind in kinds:
        out_specs.append(pl.BlockSpec((1, depth), lambda i: (0, 0)) if kind == "sum" else block)
        out_shape.append(
            jax.ShapeDtypeStruct((1, depth), F32) if kind == "sum" else jax.ShapeDtypeStruct((size, depth), kind)
        )
    return pl.pallas_call(
        functools.partial(settle_kernel, form, function, len(rows), len(deps) + len(carry), kinds),
        grid=(2,),
        in_specs=[block] + others + [block] * len(rows) + [HBM] * (len(deps) + len(carry)),
        out_specs=out_specs + [HBM] * len(carry),
        out_shape=out_shape + [jax.ShapeDtypeStruct(c.shape, c.dtype) for c in carry],
        input_output_aliases={
            1 + len(others) + len(rows) + len(deps) + i: len(kinds) + i for i in range(len(carry))
        },
        compiler_params=pltpu.CompilerParams(vmem_limit_bytes=60 * MIB),
        cost_estimate=cost(3e9),
        name="settle_rows",
    )(own, *arrived, *second, *rows, *deps, *carry)


def bits(count):
    assert count & (count - 1) == 0
    return [1 << i for i in range(count.bit_length() - 1)]


def sum_over(value, axis, count):
    for bit in bits(count):
        value = value + hop(value, bit, count, axis)
    return value


def norm_scale(rows):
    return lax.rsqrt(jnp.mean(rows * rows, axis=-1, keepdims=True) + EPSILON)


def add_branch(total, rows):
    middle = rows.astype(F32) + total
    return middle, (middle * norm_scale(middle)).astype(BF)


def add_last(total, middle):
    return ((middle + total).astype(BF),)


def turn_back(total, middle, cotangent):
    scale = norm_scale(middle)
    inner = jnp.mean(total * middle, axis=-1, keepdims=True)
    grad = cotangent.astype(F32) + scale * total - middle * (scale * scale * scale * inner)
    return grad, grad.astype(BF), jnp.sum(total * middle * scale, axis=0, keepdims=True)


def finish_back(total, rows, grad_middle):
    rows = rows.astype(F32)
    scale = norm_scale(rows)
    inner = jnp.mean(total * rows, axis=-1, keepdims=True)
    grad = grad_middle + total - rows * (scale * scale * inner)
    return (grad.astype(BF),)


def pack_kernel(size, number, turned_count, cuts, extra, *refs):
    weights, gain_ref = refs[:number], refs[number]
    others = refs[number + 1 : number + 1 + turned_count]
    outs = refs[number + 1 + turned_count + extra :]
    gain = gain_ref[...]
    groups = weights[0].shape[1] // size
    at = 0
    for i in range(groups):
        out = outs[i * cuts // groups]
        if i * cuts % groups == 0:
            at = 0
        for weight in weights:
            out[:, at : at + size] = (weight[:, i * size : (i + 1) * size].astype(F32) * gain).astype(BF)
            at += size
    for other in others:
        outs[-1][:, at : at + other.shape[0]] = other[...].T
        at += other.shape[0]


def pack(weights, gain, others, size, cuts, deps=()):
    rows_w, width = weights[0].shape
    widths = [len(weights) * width // cuts] * cuts
    widths[-1] += sum(other.shape[0] for other in others)
    whole = pl.BlockSpec(memory_space=pltpu.VMEM)
    return pl.pallas_call(
        functools.partial(pack_kernel, size, len(weights), len(others), cuts, len(deps)),
        in_specs=[whole] * (len(weights) + 1 + len(others)) + [HBM] * len(deps),
        out_specs=[whole] * cuts,
        out_shape=[jax.ShapeDtypeStruct((rows_w, w), BF) for w in widths],
        compiler_params=pltpu.CompilerParams(vmem_limit_bytes=60 * MIB),
        cost_estimate=cost(2e9),
        name="pack",
    )(*weights, gain, *others, *deps)


def unpack_kernel(groups, pitch, *refs):
    parts, gain_ref, outs = refs[: len(groups)], refs[len(groups)], refs[len(groups) + 1 :]
    at = 0
    for part, number in zip(parts, groups):
        size = part.shape[1] // (number * pitch)
        for i in range(number):
            for k, out in enumerate(outs):
                start = (i * pitch + k) * size
                out[:, at : at + size] = part[:, start : start + size].astype(F32) * gain_ref[...]
            at += size


def turn_kernel(number, *refs):
    for part, out in zip(refs[:number], refs[number:]):
        out[...] = part[...].astype(F32).T


def turned(parts):
    return pl.pallas_call(
        functools.partial(turn_kernel, len(parts)),
        out_shape=[jax.ShapeDtypeStruct(p.shape[::-1], F32) for p in parts],
        compiler_params=pltpu.CompilerParams(vmem_limit_bytes=60 * MIB),
        cost_estimate=cost(2e9),
        name="turned",
    )(*parts)


def unpack(parts, groups, pitch, gain):
    rows_w = gain.shape[0]
    width = sum(p.shape[1] for p in parts) // pitch
    return pl.pallas_call(
        functools.partial(unpack_kernel, groups, pitch),
        out_shape=[jax.ShapeDtypeStruct((rows_w, width), F32)] * pitch,
        compiler_params=pltpu.CompilerParams(vmem_limit_bytes=60 * MIB),
        cost_estimate=cost(2e9),
        name="unpack",
    )(*parts, gain)


def local(
    count_dp,
    count,
    tokens,
    cotangent,
    doc_lengths,
    rel_bucket,
    gain_attn,
    w_query,
    w_key,
    w_value,
    w_out,
    rel_table,
    gain_ff,
    w_gate,
    w_up,
    w_down,
):
    slots = tokens.shape[0]
    length = slots * count
    blocks = length // B
    rows_w, width = w_query.shape
    width_ff = w_gate.shape[1]
    pairs = width // 128
    heads = width // HD
    buckets_local = rel_table.shape[0]
    buckets = buckets_local * count_dp
    docs = doc_lengths.shape[1]
    tile = ff_tile(width_ff)
    me = lax.axis_index("dp").astype(jnp.int32)

    def spread(part):
        return lax.all_gather(part, "dp", axis=0, tiled=True)

    def after(value, *others):
        return lax.optimization_barrier((value, *others))[0]

    xs = [tokens[:, m] for m in range(MICRO)]
    gain_one = gain_attn.astype(F32)[:, None]
    gain_two = gain_ff.astype(F32)[:, None]
    cuts = 2
    each = pairs // cuts
    part_w = each * 384

    halves = pack([w_query, w_key, w_value], gain_one, [w_out], 128, cuts)
    full_qkv = [spread(half) for half in halves]
    full_out, out_at = full_qkv[-1], part_w
    form = "both" if count == 4 else None
    way = ("x", "y") if form else (None, None)

    table = rel_table.reshape(1, buckets_local * heads)
    for bit in bits(count_dp):
        table = jnp.concatenate([table, hop(table, bit, count_dp, "dp")], axis=0)
    table = jnp.take(table, jnp.arange(count_dp, dtype=jnp.int32) ^ me, axis=0).reshape(buckets, heads)
    reverse = jnp.concatenate([jnp.full((1,), -1, jnp.int32), rel_bucket[::-1]])
    onehot = reverse[None, :] == jnp.arange(buckets, dtype=jnp.int32)[:, None]
    offsets = tn(table, onehot.astype(BF)).reshape(heads, 2 * blocks, B)
    tiles = 2 * blocks - 1
    ahead = offsets[:, ::-1]
    bias = bias_strips(jnp.concatenate([ahead[:, :tiles], ahead[:, 1:]], axis=2))

    order = jnp.arange(blocks, dtype=jnp.int32)
    if count == 4:
        order = order ^ lax.axis_index("tensor").astype(jnp.int32)
    positions = (order[:, None] * B + jnp.arange(B, dtype=jnp.int32)[None]).reshape(-1)
    ends = jnp.cumsum(doc_lengths, axis=1)
    lane = jnp.arange(128, dtype=jnp.int32) % HD

    masks = []
    for m in range(MICRO):
        number = jnp.sum((positions[:, None] >= ends[m][None, :]).astype(jnp.int32), axis=1)
        by_block = number.reshape(blocks, B)
        least, most = by_block.min(axis=1), by_block.max(axis=1)
        active = (least[:, None] <= most[None, :]) & (least[None, :] <= most[:, None])
        same = number[:, None] == lane[None, :]
        feat_q = same.astype(BF)
        feat_k = jnp.where(same | (lane >= docs)[None, :], 0.0, -BIG).astype(BF)
        masks.append((feat_q, feat_k, active.astype(jnp.int32).reshape(-1)))
    ones = [Gather(xs[0], "both", count, (bias,))]
    (packed,) = pack([w_gate, w_up], gain_two, [w_down], tile, 1, (bias, *ones[0].sent))
    full_ff = spread(packed)

    def project(m, cut, scale, deps):
        mode = "take" if scale else "make"
        return product(ones[m].pieces, full_qkv[cut], 0, part_w, mode, scale, deps)

    def forward(m, cut, qkv, into, deps):
        feat_q, feat_k, active = masks[m]
        return attend_forward(qkv, feat_q, feat_k, bias, active, order, cut * each, into, deps)

    def out_rows(mixed, deps):
        return partial_rows([mixed], [full_out], [full_out.shape[1]], [0], [(width, width, out_at)], form, deps)

    def ff_rows(left, inner, way, deps, carry=()):
        size = 2 * width_ff if inner else width_ff
        return partial_rows(
            [left], [full_ff], [size], [0 if inner else 2], [(size, size, 0)], way, deps, (), carry
        )

    def qkv_rows(projects, m, deps, carry=()):
        return partial_rows(
            projects, full_qkv, [part_w] * cuts, [0] * cuts, [(part_w, part_w, 0)] * cuts, form, deps, ones[m].pieces, carry
        )

    def scatter(value):
        return lax.psum_scatter(value, "dp", scatter_dimension=0, tiled=True)

    qkv_0a, scale_0 = project(0, 0, (), (packed,))
    ones.append(Gather(after(xs[1], *ones[0].pieces), "both", count, (qkv_0a,)))
    into = forward(0, 0, qkv_0a, (), ())
    cs = [after(cotangent, qkv_0a)[:, m] for m in range(MICRO)]
    (qkv_0b,) = project(0, 1, (scale_0,), (into[0], *ones[1].first))
    cots = [Gather(cs[0], "both", count, (qkv_0b,))]
    mixed_0, lse_0 = forward(0, 1, qkv_0b, into, ())
    parts = out_rows(mixed_0, (*ones[1].pieces, *cots[0].first))
    sum_0 = Reduce(parts, form, count)
    qkv_1a, scale_1 = project(1, 0, (), (parts[0],))
    into = forward(1, 0, qkv_1a, (), tuple(cots[0].pieces))
    late = sum_0.first((into[0],))
    (qkv_1b,) = project(1, 1, (scale_1,), (late[0],))
    middle_0, normed = sum_0.settle(add_branch, [xs[0]], (F32, BF), (qkv_1b,))
    mixed_1, lse_1 = forward(1, 1, qkv_1b, into, (normed,))
    twos = [Gather(normed, "both", count, (mixed_1,))]
    parts = out_rows(mixed_1, twos[0].sent)
    sum_1 = Reduce(parts, form, count, twos[0].pieces)

    steps = width_ff // tile
    ff_half = (steps + 1) // 2 * 2 * tile
    hidden_0, grad_ff_0 = feed_forward(twos[0].pieces, cots[0].pieces, full_ff, 0, steps, (), (parts[0],))
    late = sum_1.first((hidden_0,))
    cots.append(Gather(after(cs[1], *twos[0].pieces), "both", count, (hidden_0,)))
    parts = ff_rows(grad_ff_0, True, form, (late[0],))
    middle_1, normed = sum_1.settle(add_branch, [xs[1]], (F32, BF), (parts[0],))
    twos.append(Gather(normed, "both", count))
    sum_0 = Reduce(parts, form, count, (*twos[1].pieces, *cots[1].pieces))
    down_part = outer([cots[0].pieces], [hidden_0], (normed,))
    ff_part_a = outer([twos[0].pieces], [grad_ff_0], (down_part,), 0, ff_half)
    ff_part_b = outer(
        [twos[0].pieces], [grad_ff_0], (ff_part_a, *twos[1].sent), ff_half, 2 * width_ff - ff_half
    )
    hidden_1, grad_ff_1 = feed_forward(
        twos[1].pieces, cots[1].pieces, full_ff, 0, steps, (), (ff_part_b,)
    )
    late = sum_0.first((hidden_1,))
    weight = outer([cots[1].pieces], [hidden_1], (late[0],), base=(down_part,))
    grad_middle_0, rounded, gain_two_0, weight = sum_0.settle(
        turn_back, [middle_0, cs[0]], (F32, BF, "sum"), (), (weight,)
    )
    grad_down = scatter(weight)
    mids = [Gather(rounded, "both", count)]
    parts = ff_rows(grad_ff_1, True, form, (rounded,))
    sum_1 = Reduce(parts, form, count)
    weight = outer(
        [twos[1].pieces], [grad_ff_1], (parts[0], *mids[0].sent), 0, ff_half, base=(ff_part_a,)
    )
    down = ff_rows(hidden_0, False, form, (weight,))
    late = sum_1.first((down[0], *mids[0].pieces), (weight,))
    grad_ff_a = scatter(late[-1])

    def backward(m, qkv, lse, mixed, grad, scale, cut, into, deps):
        feat_q, feat_k, active = masks[m]
        return attend_backward(
            qkv, feat_q, feat_k, bias, lse, mixed, grad, scale, active, order, cut * each, into, deps
        )

    (grad,) = product(mids[0].pieces, full_out, out_at, width, deps=(late[0],))
    weight = outer(
        [twos[1].pieces], [grad_ff_1], (grad,), ff_half, 2 * width_ff - ff_half, base=(ff_part_b,)
    )
    grad_middle_1, rounded, gain_two_1, weight = sum_1.settle(
        turn_back, [middle_1, cs[1]], (F32, BF, "sum"), (), (weight,)
    )
    grad_ff_b = scatter(weight)
    mids.append(Gather(rounded, "both", count))
    grad_0a, fold = backward(0, qkv_0a, lse_0, mixed_0, grad, scale_0, 0, (), (rounded,))
    down_0 = Reduce(down, form, count, mids[1].first)
    grad_0b, fold_0 = backward(0, qkv_0b, lse_0, mixed_0, grad, scale_0, 1, (fold,), mids[1].sent)
    *parts, gain_one_0 = qkv_rows([grad_0a, grad_0b], 0, (grad_down,))
    sum_0 = Reduce(parts, form, count)
    (grad,) = product(mids[1].pieces, full_out, out_at, width, deps=(parts[0],))
    weight = outer([g.pieces for g in mids], [mixed_0, mixed_1], (grad, grad_ff_a))
    late = sum_0.first((), (weight,))
    grad_out = scatter(late[-1])
    late = down_0.first((late[0],))
    grad_1a, fold = backward(1, qkv_1a, lse_1, mixed_1, grad, scale_1, 0, (), (late[0],))
    (output_0,) = down_0.settle(add_last, [middle_0], (BF,), (grad_1a,))
    weight = outer([g.pieces for g in ones], [grad_0a, grad_1a], (output_0,))
    token_0, weight = sum_0.settle(finish_back, [xs[0], grad_middle_0], (BF,), (), (weight,))
    grad_qkv_a = scatter(weight)
    parts = ff_rows(hidden_1, False, form, (token_0,))
    down_1 = Reduce(parts, form, count)
    grad_1b, fold_1 = backward(1, qkv_1b, lse_1, mixed_1, grad, scale_1, 1, (fold,), (parts[0], grad_ff_b))
    late = down_1.first((grad_1b,))
    weight = outer([g.pieces for g in ones], [grad_0b, grad_1b], (late[0], grad_out))
    output_1, weight = down_1.settle(add_last, [middle_1], (BF,), (), (weight,))
    grad_qkv_b = scatter(weight)
    *parts, gain_one_1 = qkv_rows([grad_1a, grad_1b], 1, (output_1,))
    sum_1 = Reduce(parts, form, count)
    grad_gate, grad_up = unpack(
        [grad_ff_a, grad_ff_b], ((steps + 1) // 2, steps // 2), 2, gain_two
    )
    grad_out, grad_down = turned([grad_out, grad_down])

    fold = (fold_0 + fold_1).reshape(heads, 2 * blocks, B)[:, ::-1]
    before = jnp.concatenate([jnp.zeros((heads, 1, B), F32), fold[:, :-1]], axis=1)
    by_offset = jnp.where(jnp.arange(B) == 0, before, fold).reshape(heads, 2 * length)
    grad_table = lax.dot_general(
        onehot.astype(F32), by_offset, (((1,), (1,)), ((), ())), precision=lax.Precision.HIGHEST
    )
    small = jnp.concatenate(
        [
            (gain_one_0 + gain_one_1).reshape(count_dp, rows_w),
            (gain_two_0 + gain_two_1).reshape(count_dp, rows_w),
            grad_table.reshape(count_dp, buckets_local * heads),
        ],
        axis=1,
    )
    small = sum_over(small, "dp", count_dp)
    late = sum_1.first((small, grad_gate, grad_out, grad_down))
    grad_qkv = unpack([grad_qkv_a, grad_qkv_b], (each, each), 3, gain_one)
    small, output_0, output_1 = lax.optimization_barrier((small, output_0, output_1, grad_qkv[0]))[:3]
    small = lax.dynamic_index_in_dim(small, me, 0, keepdims=False)
    both_gains = sum_over(small[: 2 * rows_w], "tensor", count)
    (token_1,) = sum_1.settle(
        finish_back,
        [xs[1], grad_middle_1],
        (BF,),
        (late[0], grad_qkv[0]),
    )
    return (
        jnp.stack([output_0, output_1], axis=1),
        jnp.stack([token_0, token_1], axis=1),
        both_gains[:rows_w] / gain_one[:, 0],
        *grad_qkv,
        grad_out,
        small[2 * rows_w :].reshape(buckets_local, heads),
        both_gains[rows_w:] / gain_two[:, 0],
        grad_gate,
        grad_up,
        grad_down,
    )


def solution(mesh):
    row, col = P("dp", "tensor"), P("tensor", "dp")
    acts = P("tensor", "dp", None)
    in_specs = (
        acts, acts, P("dp", None), P(), P("dp"), row, row, row, col, row, P("dp"), row, row, col
    )
    out_specs = (acts, acts, P("dp"), row, row, row, col, row, P("dp"), row, row, col)
    body = functools.partial(local, mesh.shape["dp"], mesh.shape["tensor"])
    return jax.shard_map(body, mesh=mesh, in_specs=in_specs, out_specs=out_specs, check_vma=False)
```
